32 devices in a mesh: seq: 4 (over z), dp: 8 (over y, x, core).
Axes of the slice: x: 2, y: 2, z: 4, core: 2. Of those that a mesh axis runs over, the one named last changes fastest.
Arguments:
- tokens: bfloat16 [8, 2048, 1024], P('dp', 'seq'), may hold values from -6 to 6
- lengths: int32 [8, 4], P('dp'), may hold values from 0 to 2048, as said below
- cotangent: bfloat16 [8, 2048, 1024], P('dp', 'seq'), may hold values from -6 to 6
- mixer_input: bfloat16 [1024, 3072], P('dp'), may hold values from -0.1875 to 0.1875
- mixer_output: bfloat16 [1024, 1024], P('dp'), may hold values from -1.5 to 1.5
- expand_weight: bfloat16 [1024, 4096], P('dp'), may hold values from -0.1875 to 0.1875
- reduce_weight: bfloat16 [4096, 1024], P('dp'), may hold values from -0.09375 to 0.09375
- first_gain: bfloat16 [1024], P('dp'), may hold values from 0.5 to 1.5
- first_shift: bfloat16 [1024], P('dp'), may hold values from -4 to 4
- second_gain: bfloat16 [1024], P('dp'), may hold values from 0.5 to 1.5
- second_shift: bfloat16 [1024], P('dp'), may hold values from -4 to 4
- output_bias: bfloat16 [1024], P('dp'), may hold values from -4 to 4
- expand_bias: bfloat16 [4096], P('dp'), may hold values from -4 to 4
- reduce_bias: bfloat16 [1024], P('dp'), may hold values from -4 to 4
Outputs:
- layer_output: bfloat16 [8, 2048, 1024], P('dp', 'seq')
- tokens_gradient: float32 [8, 2048, 1024], P('dp', 'seq')
- mixer_input_gradient: float32 [1024, 3072], P('dp')
- mixer_output_gradient: float32 [1024, 1024], P('dp')
- expand_weight_gradient: float32 [1024, 4096], P('dp')
- reduce_weight_gradient: float32 [4096, 1024], P('dp')
- first_gain_gradient: float32 [1024], P('dp')
- first_shift_gradient: float32 [1024], P('dp')
- second_gain_gradient: float32 [1024], P('dp')
- second_shift_gradient: float32 [1024], P('dp')
- output_bias_gradient: float32 [1024], P('dp')
- expand_bias_gradient: float32 [4096], P('dp')
- reduce_bias_gradient: float32 [1024], P('dp')
The draws below stay inside these ranges and needn't reach their ends.
Inputs may be any that keep to these rules, and one draw needn't show every extreme that they name: `lengths`: entries are 0 or 64 to 2048; a bucket's entries sum to at most 2048; in every bucket one sequence begins in the first quarter of the slots and ends in the last quarter; some bucket holds one sequence of 2048.
All inputs are finite; a program needn't handle non-finite values.
Results may differ from the reference program's by a relative error of at most 0.0096.
Values may be sent and summed in bfloat16 or wider, within the bound.
A program may use at most 256 MiB of HBM per device.

```python
import jax
import jax.numpy as jnp
from jax import lax

D = 1024
HEADS = 16
HEAD_DIM = 64
FF = 4096
SLOTS = 2048
MAXSEQ = 4
MIN_LEN = 64
BUCKETS = 8


def draw_lengths(key, part):
    key = jax.random.fold_in(key, 11)
    streams = jax.random.split(key, 7)
    count = BUCKETS
    coin = jax.random.randint(streams[0], (count,), 0, 2)
    first = coin * jax.random.randint(streams[1], (count,), MIN_LEN, SLOTS // 8 + 1)
    longest = jax.random.randint(streams[2], (count,), 3 * SLOTS // 4 + 1 - first, SLOTS + 1 - first)
    rest = SLOTS - first - longest
    third = jax.random.randint(streams[3], (count,), MIN_LEN, jnp.maximum(rest, MIN_LEN) + 1)
    third = jnp.where(rest >= MIN_LEN, third, 0)
    remain = rest - third
    fourth = jax.random.randint(streams[4], (count,), MIN_LEN, jnp.maximum(remain, MIN_LEN) + 1)
    other = jax.random.randint(streams[5], (count,), 0, 2)
    fourth = jnp.where((remain >= MIN_LEN) & (other == 1), fourth, 0)
    table = jnp.stack([first, longest, third, fourth], axis=1)
    chosen = jax.random.randint(streams[6], (), 0, count)
    full_row = jnp.zeros((MAXSEQ,), jnp.int32).at[0].set(SLOTS)
    table = jnp.where((jnp.arange(count) == chosen)[:, None], full_row[None, :], table)
    return table.astype(jnp.int32)


def levels(own_key, shape, cuts, least, top_value):
    def one(dim, parts):
        steps = jax.random.uniform(jax.random.fold_in(jax.random.fold_in(own_key, 6), dim), (parts,), jnp.float32, least / len(cuts), top_value / len(cuts))
        return jnp.repeat(jnp.exp(steps), shape[dim] // parts).reshape((-1,) + (1,) * (len(shape) - dim - 1))

    factor_of = one(*cuts[0])
    for cut in cuts[1:]:
        factor_of = factor_of * one(*cut)
    return factor_of


def centred(rng, dims, scale, reach, cuts=(), held_as=jnp.bfloat16):
    values = scale * jax.random.normal(rng, dims, jnp.float32)
    if cuts:
        values = values * levels(rng, dims, cuts, -0.22, 0.18)
    return jnp.clip(values, -reach, reach).astype(held_as)


def setup_inputs(seed: int = 0) -> dict:
    arg_keys = jax.random.split(jax.random.key(seed), 15)
    return {
        "tokens": centred(arg_keys[0], (BUCKETS, SLOTS, D), 1.0, 6.0, ((0, 8), (1, 4))),
        "lengths": draw_lengths(jax.random.fold_in(arg_keys[14], 71), 0),
        "cotangent": centred(arg_keys[2], (BUCKETS, SLOTS, D), 1.0, 6.0, ((0, 8), (1, 4))),
        "mixer_input": centred(arg_keys[3], (D, 3 * D), D ** -0.5, 0.1875, ((0, 8),)),
        "mixer_output": centred(arg_keys[4], (D, D), (max(D // 64, 4)) ** -0.5, 1.5, ((0, 8),)),
        "expand_weight": centred(arg_keys[5], (D, FF), D ** -0.5, 0.1875, ((0, 8),)),
        "reduce_weight": centred(arg_keys[6], (FF, D), FF ** -0.5, 0.09375, ((0, 8),)),
        "first_gain": jnp.clip(1.0 + 0.1 * jax.random.normal(arg_keys[7], (D,), jnp.float32), 0.5, 1.5).astype(jnp.bfloat16),
        "first_shift": centred(arg_keys[8], (D,), 0.3, 4.0, ((0, 8),)),
        "second_gain": jnp.clip(1.0 + 0.1 * jax.random.normal(arg_keys[9], (D,), jnp.float32), 0.5, 1.5).astype(jnp.bfloat16),
        "second_shift": centred(arg_keys[10], (D,), 0.3, 4.0, ((0, 8),)),
        "output_bias": centred(arg_keys[11], (D,), 0.3, 4.0, ((0, 8),)),
        "expand_bias": centred(arg_keys[12], (FF,), 0.3, 4.0, ((0, 8),)),
        "reduce_bias": centred(arg_keys[13], (D,), 0.3, 4.0, ((0, 8),)),
    }


@jax.custom_vjp
def low(v):
    return lax.optimization_barrier(v.astype(jnp.bfloat16)).astype(jnp.float32)

@jax.custom_vjp
def low_back(v):
    return v

def low_keep(v):
    return (low(v), None)

def low_pass(kept, grad):
    return (grad,)

def back_keep(v):
    return (v, None)

def back_low(kept, grad):
    return (low(grad),)
low.defvjp(low_keep, low_pass)
low_back.defvjp(back_keep, back_low)
norm_eps = 1e-05
masked_score = -1e+30
highest_mode = lax.Precision.HIGHEST

def layer_normalize(values, gain, shift):
    center = values - lax.optimization_barrier(jnp.mean(values, axis=-1, keepdims=True))
    spread = lax.optimization_barrier(jnp.mean(center * center, axis=-1, keepdims=True))
    return center * lax.rsqrt(spread + norm_eps) * gain + shift

def smooth_gate(values):
    return jax.nn.gelu(values, approximate=True)

def product(left, right):
    return jnp.dot(left, right, precision=highest_mode)

def visible_mask(lengths_row, query_place, key_place):
    ends = jnp.cumsum(lengths_row)
    query_doc = lax.optimization_barrier(jnp.sum((query_place[:, None] >= ends[None, :]).astype(jnp.int32), axis=1))
    key_doc = lax.optimization_barrier(jnp.sum((key_place[:, None] >= ends[None, :]).astype(jnp.int32), axis=1))
    key_live = key_place < ends[-1]
    same_doc = key_live[None, :] & (query_doc[:, None] == key_doc[None, :]) & (key_place[None, :] <= query_place[:, None])
    return same_doc | (key_place[None, :] == query_place[:, None])

def bucket_forward(inputs, lengths_row, weights):
    mixer_input, mixer_output, expand_weight, reduce_weight, first_gain, first_shift, second_gain, second_shift, output_bias, expand_bias, reduce_bias = weights
    place = jnp.arange(SLOTS, dtype=jnp.int32)
    allowed = visible_mask(lengths_row, place, place)
    normed_one = low(layer_normalize(inputs, first_gain, first_shift))
    mixed = low(low_back(product(normed_one, mixer_input)))
    queries = mixed[:, :D].reshape(SLOTS, HEADS, HEAD_DIM)
    keys_all = mixed[:, D:2 * D].reshape(SLOTS, HEADS, HEAD_DIM)
    values_all = mixed[:, 2 * D:].reshape(SLOTS, HEADS, HEAD_DIM)
    scores = low_back(jnp.einsum('qhd,khd->hqk', queries, keys_all, precision=highest_mode) * HEAD_DIM ** (-0.5))
    scores = jnp.where(allowed[None], scores, masked_score)
    highest = lax.optimization_barrier(jnp.max(scores, axis=-1, keepdims=True))
    powers = jnp.exp(scores - highest)
    shares = low(powers / lax.optimization_barrier(jnp.sum(powers, axis=-1, keepdims=True)))
    attended = jnp.einsum('hqk,khd->qhd', shares, values_all, precision=highest_mode).reshape(SLOTS, D)
    attention = low(low_back(attended))
    resid = inputs + low_back(product(attention, mixer_output)) + output_bias
    normed_two = low(layer_normalize(resid, second_gain, second_shift))
    expanded = low_back(product(normed_two, expand_weight)) + expand_bias
    active = low(smooth_gate(expanded))
    return resid + low_back(product(active, reduce_weight)) + reduce_bias

def reference(tokens, lengths, cotangent, mixer_input, mixer_output, expand_weight, reduce_weight, first_gain, first_shift, second_gain, second_shift, output_bias, expand_bias, reduce_bias):
    params = (mixer_input.astype(jnp.float32), mixer_output.astype(jnp.float32), expand_weight.astype(jnp.float32), reduce_weight.astype(jnp.float32), first_gain.astype(jnp.float32), first_shift.astype(jnp.float32), second_gain.astype(jnp.float32), second_shift.astype(jnp.float32), output_bias.astype(jnp.float32), expand_bias.astype(jnp.float32), reduce_bias.astype(jnp.float32))

    def forward(inputs, weights):

        def one_bucket(pair):
            return jax.checkpoint(bucket_forward)(pair[0], pair[1], weights)
        return lax.map(one_bucket, (inputs, lengths))
    result, backward = jax.vjp(forward, tokens.astype(jnp.float32), params)
    place = jnp.arange(SLOTS, dtype=jnp.int32)
    live = (place[None, :] < lax.optimization_barrier(jnp.sum(lengths, axis=1))[:, None]).astype(jnp.float32)
    tokens_grad, weight_grads = backward(cotangent.astype(jnp.float32) * live[:, :, None])
    return (result.astype(jnp.bfloat16), tokens_grad, weight_grads[0], weight_grads[1], weight_grads[2], weight_grads[3], weight_grads[4], weight_grads[5], weight_grads[6], weight_grads[7], weight_grads[8], weight_grads[9], weight_grads[10])
```

```python
import functools

import jax
import jax.numpy as jnp
from jax import lax
from jax.experimental import pallas as pl
from jax.experimental.pallas import tpu as pltpu
from jax.sharding import PartitionSpec as P

HEADS = 16
EPS = 1e-05
NEG = -1e30
F32 = jnp.float32
BF = jnp.bfloat16


def _dot(a, b, ca, cb):
    return lax.dot_general(a, b, (((ca,), (cb,)), ((), ())), preferred_element_type=F32)


def mm(a, b):
    return _dot(a, b, 1, 0)


def mm_left(a, b):
    return _dot(a, b, 0, 0)


def mm_right(a, b):
    return _dot(a, b, 1, 1)


def fwd_kernel(st_ref, q_ref, k_ref, v_ref, o_ref, lse_ref, qt_ref, vt_ref, *, bq, bk, scale):
    n = q_ref.shape[0]
    d = q_ref.shape[1] // 2
    qt_ref[...] = jnp.transpose(q_ref[...])
    vt_ref[...] = jnp.transpose(v_ref[...])
    for i in range(n // bq):
        cs = slice(i * bq, (i + 1) * bq)
        st = st_ref[:, cs]
        outs = []
        for h in range(2):
            row = lax.broadcasted_iota(jnp.int32, (2 * d, bq), 0)
            qm = jnp.where((row >= h * d) & (row < (h + 1) * d), qt_ref[:, cs], jnp.zeros((), BF))
            m = jnp.full((1, bq), NEG, F32)
            l = jnp.zeros((1, bq), F32)
            acc = jnp.zeros((d, bq), F32)
            for j in range(0, (i + 1) * bq, bk):
                s = _dot(k_ref[j : j + bk, :], qm, 1, 0) * scale
                key = lax.broadcasted_iota(jnp.int32, (bk, bq), 0) + j
                ok = key >= st
                if j + bk > i * bq:
                    ok = ok & (key <= lax.broadcasted_iota(jnp.int32, (bk, bq), 1) + i * bq)
                s = jnp.where(ok, s, NEG)
                mn = jnp.maximum(m, jnp.max(s, axis=0, keepdims=True))
                p = jnp.exp(s - mn)
                a = jnp.exp(m - mn)
                l = a * l + jnp.sum(p, axis=0, keepdims=True)
                acc = a * acc + _dot(vt_ref[h * d : (h + 1) * d, j : j + bk], p.astype(BF), 1, 0)
                m = mn
            outs.append(acc / l)
            lse_ref[0, h : h + 1, cs] = m + jnp.log(l)
        o_ref[cs, :] = jnp.transpose(jnp.concatenate(outs, axis=0)).astype(BF)


def flash_fwd(starts, qkv, heads, d, bq=512, bk=512):
    n, w, pairs = starts.shape[1], 2 * d, heads // 2
    blk = lambda c: pl.BlockSpec((n, w), lambda p: (0, c + p))
    return pl.pallas_call(
        functools.partial(fwd_kernel, bq=bq, bk=bk, scale=d**-0.5),
        grid=(pairs,),
        in_specs=[pl.BlockSpec((1, n), lambda p: (0, 0)), blk(0), blk(pairs), blk(2 * pairs)],
        out_specs=[blk(0), pl.BlockSpec((1, 2, n), lambda p: (p, 0, 0))],
        out_shape=[
            jax.ShapeDtypeStruct((n, pairs * w), BF),
            jax.ShapeDtypeStruct((pairs, 2, n), F32),
        ],
        scratch_shapes=[pltpu.VMEM((w, n), BF), pltpu.VMEM((w, n), BF)],
        compiler_params=pltpu.CompilerParams(vmem_limit_bytes=48 << 20),
        cost_estimate=pl.CostEstimate(
            flops=8 * n * n * d * heads, bytes_accessed=8 * n * w * pairs, transcendentals=n * n * heads
        ),
    )(starts, qkv, qkv, qkv)


def bwd_kernel(
    st_ref, q_ref, k_ref, v_ref, do_ref, o_ref, lse_ref, dq_ref, dk_ref, dv_ref,
    qm_ref, dom_ref, qt_ref, dot_ref, kt_ref, dqt_ref, delta_ref, *, bq, bk, scale
):
    n, w = q_ref.shape
    d = w // 2
    lane = lax.broadcasted_iota(jnp.int32, (n, w), 1)
    z = jnp.zeros((), BF)
    for h in range(2):
        sel = (lane >= h * d) & (lane < (h + 1) * d)
        qm = jnp.where(sel, q_ref[...], z)
        dom = jnp.where(sel, do_ref[...], z)
        qm_ref[h] = qm
        dom_ref[h] = dom
        qt_ref[h] = jnp.transpose(qm)
        dot_ref[h] = jnp.transpose(dom)
    kt_ref[...] = jnp.transpose(k_ref[...])
    prod = jnp.transpose(do_ref[...].astype(F32) * o_ref[...].astype(F32))
    for h in range(2):
        delta_ref[h : h + 1, :] = jnp.sum(prod[h * d : (h + 1) * d], axis=0, keepdims=True)
    dqt_ref[...] = jnp.zeros_like(dqt_ref)
    for j in range(0, n, bk):
        dk = jnp.zeros((bk, w), F32)
        dv = jnp.zeros((bk, w), F32)
        for i in range(j // bq, n // bq):
            cs = slice(i * bq, (i + 1) * bq)
            st = st_ref[:, cs]
            key = lax.broadcasted_iota(jnp.int32, (bk, bq), 0) + j
            ok = key >= st
            if j + bk > i * bq:
                ok = ok & (key <= lax.broadcasted_iota(jnp.int32, (bk, bq), 1) + i * bq)
            for h in range(2):
                s = _dot(k_ref[j : j + bk, :], qt_ref[h, :, cs], 1, 0) * scale
                s = jnp.where(ok, s, NEG)
                p = jnp.exp(s - lse_ref[0, h : h + 1, cs])
                dp = _dot(v_ref[j : j + bk, :], dot_ref[h, :, cs], 1, 0)
                ds = (p * (dp - delta_ref[h : h + 1, cs])).astype(BF)
                dv = dv + _dot(p.astype(BF), dom_ref[h, cs, :], 1, 0)
                dk = dk + _dot(ds, qm_ref[h, cs, :], 1, 0)
                dqt_ref[h * d : (h + 1) * d, cs] += _dot(kt_ref[h * d : (h + 1) * d, j : j + bk], ds, 1, 0)
        dk_ref[j : j + bk, :] = (dk * scale).astype(BF)
        dv_ref[j : j + bk, :] = dv.astype(BF)
    dq_ref[...] = (jnp.transpose(dqt_ref[...]) * scale).astype(BF)


def flash_bwd(starts, qkv, grad, out, lse, heads, d, bq=256, bk=512):
    n, w, pairs = starts.shape[1], 2 * d, heads // 2
    blk = lambda c: pl.BlockSpec((n, w), lambda p: (0, c + p))
    return pl.pallas_call(
        functools.partial(bwd_kernel, bq=bq, bk=bk, scale=d**-0.5),
        grid=(pairs,),
        in_specs=[
            pl.BlockSpec((1, n), lambda p: (0, 0)), blk(0), blk(pairs), blk(2 * pairs), blk(0), blk(0),
            pl.BlockSpec((1, 2, n), lambda p: (p, 0, 0)),
        ],
        out_specs=[blk(0)] * 3,
        out_shape=[jax.ShapeDtypeStruct((n, pairs * w), BF)] * 3,
        scratch_shapes=[
            pltpu.VMEM((2, n, w), BF), pltpu.VMEM((2, n, w), BF), pltpu.VMEM((2, w, n), BF),
            pltpu.VMEM((2, w, n), BF), pltpu.VMEM((w, n), BF), pltpu.VMEM((w, n), F32), pltpu.VMEM((2, n), F32),
        ],
        compiler_params=pltpu.CompilerParams(vmem_limit_bytes=56 << 20),
        cost_estimate=pl.CostEstimate(
            flops=20 * n * n * d * heads, bytes_accessed=16 * n * w * pairs, transcendentals=n * n * heads
        ),
    )(starts, qkv, qkv, qkv, grad, out, lse)


def layer_normalize(values, gain, shift):
    center = values - jnp.mean(values, axis=-1, keepdims=True)
    spread = jnp.mean(center * center, axis=-1, keepdims=True)
    return center * lax.rsqrt(spread + EPS) * gain + shift


def smooth_gate(values):
    return jax.nn.gelu(values, approximate=True)


def rows(array, start, size):
    return lax.dynamic_slice_in_dim(array, start, size, 0)


def cols(array, start, size):
    return lax.dynamic_slice_in_dim(array, start, size, 1)


def put(array, piece, row, col):
    return lax.dynamic_update_slice(array, piece, (row, col))


def bf_round(x):
    return lax.reduce_precision(x, 8, 7)


class Links:
    def __init__(self, ns, nd):
        self.ns, self.nd = ns, nd

    def go(self, array, target):
        pairs = []
        for s in range(self.ns):
            for d in range(self.nd):
                ts, td = target(s, d)
                pairs.append((s * self.nd + d, ts * self.nd + td))
        return lax.ppermute(array, ("seq", "dp"), pairs)

    def dp(self, array, k):
        return self.go(array, lambda s, d: (s, d ^ k))

    def core(self, array):
        return self.dp(array, 1)

    def near(self, array):
        return self.go(array, lambda s, d: (s ^ 1, d))

    def far(self, array):
        return self.go(array, lambda s, d: (s ^ 2, d))

    def both(self, array):
        return self.go(array, lambda s, d: (s ^ 1, d ^ 1))

    def swap(self, array):
        return self.go(array, lambda s, d: (2 * (d % 2) + s % 2, d - d % 2 + s // 2))


def on_device(
    tokens, lengths, cotangent, mixer_input, mixer_output, expand_weight, reduce_weight,
    first_gain, first_shift, second_gain, second_shift, output_bias, expand_bias, reduce_bias,
):
    ns, nd = lax.axis_size("seq"), lax.axis_size("dp")
    links = Links(ns, nd)
    seq, me = lax.axis_index("seq"), lax.axis_index("dp")
    half, near_bit, core = seq // 2, seq % 2, me % 2
    column = me // 2
    member = 2 * core + near_bit
    n_rows, width = tokens.shape[1:]
    slots = n_rows * ns
    head_dim = width // HEADS
    hidden = reduce_weight.shape[0] * nd
    group = width // 4
    my_heads = HEADS // 4

    x_low = links.swap(tokens[0])
    vectors = jnp.concatenate(
        [first_gain, first_shift, second_gain, second_shift, output_bias, reduce_bias, expand_bias]
    )
    small = width // nd
    vectors = lax.all_gather(vectors.reshape(-1, small), "dp", axis=0).astype(F32)
    gain_one, shift_one, gain_two, shift_two, output_add, reduce_add = (
        vectors[:, i].reshape(-1) for i in range(6)
    )
    expand_add = vectors[:, 6:].reshape(-1)

    def group_columns(array, which):
        return jnp.concatenate([cols(array, i * width + which * group, group) for i in range(3)], axis=1)

    for_even = group_columns(mixer_input, member)
    for_odd = group_columns(mixer_input, member ^ 2)
    small_rows = mixer_input.shape[0]
    input_full = jnp.zeros((width, 3 * group), BF)
    input_full = put(input_full, for_even, me * small_rows, 0)
    for k in range(1, nd):
        piece = links.dp(for_odd if k % 2 else for_even, k)
        input_full = put(input_full, piece, (me ^ k) * small_rows, 0)

    def gather(shard):
        high = shard.shape[0]
        full = jnp.zeros((high * nd, shard.shape[1]), BF)
        for k in range(0, nd, 2):
            piece = links.dp(shard, k) if k else shard
            full = put(full, piece, (me ^ k) * high, 0)
            full = put(full, links.core(piece), (me ^ k ^ 1) * high, 0)
        return full

    output_full = gather(mixer_output)
    expand_full = gather(expand_weight)
    reduce_full = gather(reduce_weight)
    grad_low = links.swap(cotangent[0])
    lengths_row = jnp.where(half == core, lengths[0], links.core(lengths)[0])

    entry = jnp.arange(lengths_row.shape[0])
    ends = jnp.sum(jnp.where(entry[None, :] <= entry[:, None], lengths_row[None, :], 0), axis=1)
    place = jnp.arange(slots, dtype=jnp.int32)
    passed = place[:, None] >= ends[None, :]
    starts = jnp.max(jnp.where(passed, ends[None, :], 0), axis=1)
    starts = jnp.where(place < ends[-1], starts, place).reshape(1, slots)
    live = (member * n_rows + jnp.arange(n_rows, dtype=jnp.int32) < ends[-1]).astype(F32)

    inputs = x_low.astype(F32)
    normed_one = layer_normalize(inputs, gain_one, shift_one).astype(BF)
    near_normed = links.near(normed_one)
    normed_all = jnp.zeros((slots, width), BF)
    normed_all = put(normed_all, normed_one, member * n_rows, 0)
    normed_all = put(normed_all, near_normed, (member ^ 1) * n_rows, 0)
    normed_all = put(normed_all, links.core(normed_one), (member ^ 2) * n_rows, 0)
    normed_all = put(normed_all, links.core(near_normed), (member ^ 3) * n_rows, 0)
    qkv = mm(normed_all, input_full).astype(BF)
    attended, logsum = flash_fwd(starts, qkv, my_heads, head_dim)

    moves = (lambda a: a, links.near, links.core, links.both)
    attention = jnp.zeros((n_rows, width), BF)
    for j in range(4):
        piece = moves[j](rows(attended, (member ^ j) * n_rows, n_rows))
        attention = put(attention, piece, 0, (member ^ j) * group)

    resid = inputs + mm(attention, output_full) + output_add
    normed_two = layer_normalize(resid, gain_two, shift_two).astype(BF)
    expanded = mm(normed_two, expand_full) + expand_add
    active = smooth_gate(expanded).astype(BF)
    result = (resid + mm(active, reduce_full) + reduce_add).astype(BF)
    layer_output = links.swap(result)

    def scatter(parts):
        chip = [parts(k).astype(F32) + links.core(parts(k ^ 1).astype(BF)).astype(F32) for k in range(0, nd, 2)]
        total = chip[0]
        for i in range(1, nd // 2):
            total = total + links.dp(chip[i].astype(BF), 2 * i).astype(F32)
        high = total.shape[0] // 2
        part = rows(total, near_bit * high, high)
        part = part + links.near(rows(total, (1 - near_bit) * high, high).astype(BF)).astype(F32)
        quarter = rows(part, half * (high // 2), high // 2)
        quarter = quarter + links.far(rows(part, (1 - half) * (high // 2), high // 2).astype(BF)).astype(F32)
        quarter = quarter.astype(BF)
        other = links.far(quarter)
        part = jnp.zeros((high, total.shape[1]), BF)
        part = put(part, quarter, half * (high // 2), 0)
        part = put(part, other, (1 - half) * (high // 2), 0)
        other = links.near(part)
        full = jnp.zeros(total.shape, F32)
        full = put(full, part.astype(F32), near_bit * high, 0)
        return put(full, other.astype(F32), (1 - near_bit) * high, 0)

    def scatter_rows(array):
        high = array.shape[0] // nd
        return scatter(lambda k: rows(array, (me ^ k) * high, high))

    grad_result = grad_low.astype(F32) * live[:, None]
    result_low = grad_result.astype(BF)
    reduce_sum = scatter_rows(mm_left(active, result_low).astype(BF))
    reduce_bias_sum = jnp.sum(grad_result, axis=0)
    grad_active = mm_right(result_low, reduce_full)
    _, gate_back = jax.vjp(smooth_gate, expanded)
    grad_expanded = gate_back(grad_active)[0]
    expand_bias_sum = jnp.sum(grad_expanded, axis=0)
    expanded_low = grad_expanded.astype(BF)
    expand_sum = scatter_rows(mm_left(normed_two, expanded_low).astype(BF))
    grad_normed_two = mm_right(expanded_low, expand_full)
    _, second_back = jax.vjp(layer_normalize, resid, gain_two, shift_two)
    resid_part, gain_two_sum, shift_two_sum = second_back(grad_normed_two)
    grad_resid = grad_result + resid_part
    output_bias_sum = jnp.sum(grad_resid, axis=0)
    resid_low = grad_resid.astype(BF)
    output_sum = scatter_rows(mm_left(attention, resid_low).astype(BF))
    grad_attention = mm_right(resid_low, output_full).astype(BF)

    grad_attended = jnp.zeros((slots, group), BF)
    for j in range(4):
        piece = moves[j](cols(grad_attention, (member ^ j) * group, group))
        grad_attended = put(grad_attended, piece, (member ^ j) * n_rows, 0)
    grad_mixed = jnp.concatenate(
        flash_bwd(starts, qkv, grad_attended, attended, logsum, my_heads, head_dim), axis=1
    )

    def normed_grad(j):
        return mm_right(rows(grad_mixed, (member ^ j) * n_rows, n_rows), input_full)

    near_term = normed_grad(1) + links.core(normed_grad(3).astype(BF)).astype(F32)
    near_term = links.near(near_term.astype(BF)).astype(F32)
    grad_normed_one = normed_grad(0) + links.core(normed_grad(2).astype(BF)).astype(F32) + near_term
    _, first_back = jax.vjp(layer_normalize, inputs, gain_one, shift_one)
    inputs_part, gain_one_sum, shift_one_sum = first_back(grad_normed_one)
    tokens_gradient = links.swap((grad_resid + inputs_part).astype(BF)).astype(F32)

    input_term = mm_left(normed_all, grad_mixed)
    pair_rows = 2 * small_rows
    total = rows(input_term, column * pair_rows, pair_rows)
    for i in range(1, nd // 2):
        piece = rows(input_term, (column ^ i) * pair_rows, pair_rows).astype(BF)
        total = total + links.dp(piece, 2 * i).astype(F32)
    total = bf_round(total)
    total = (total + links.far(total.astype(BF)).astype(F32)).astype(BF)
    near_total = links.near(total)
    held = [
        (member, rows(total, core * small_rows, small_rows)),
        (member ^ 1, rows(near_total, core * small_rows, small_rows)),
        (member ^ 2, links.core(rows(total, (1 - core) * small_rows, small_rows))),
        (member ^ 3, links.core(rows(near_total, (1 - core) * small_rows, small_rows))),
    ]
    input_sum = jnp.zeros((small_rows, 3 * width), F32)
    for which, piece in held:
        for i in range(3):
            part = piece[:, i * group : (i + 1) * group].astype(F32)
            input_sum = put(input_sum, part, 0, i * width + which * group)

    sums = jnp.stack([gain_one_sum, shift_one_sum, gain_two_sum, shift_two_sum, output_bias_sum, reduce_bias_sum])
    sums = jnp.concatenate([sums.reshape(-1), expand_bias_sum])
    sums = lax.psum(sums, ("seq", "dp"))
    wide = hidden // nd
    vector_sums = [lax.dynamic_slice(sums, (i * width + me * small,), (small,)) for i in range(6)]
    expand_bias_out = lax.dynamic_slice(sums, (6 * width + me * wide,), (wide,))

    return (
        layer_output[None],
        tokens_gradient[None],
        input_sum,
        output_sum,
        expand_sum,
        reduce_sum,
        vector_sums[0],
        vector_sums[1],
        vector_sums[2],
        vector_sums[3],
        vector_sums[4],
        expand_bias_out,
        vector_sums[5],
    )


def solution(mesh):
    row, vec = P("dp", None), P("dp")
    act = P("dp", "seq", None)
    return jax.shard_map(
        on_device,
        mesh=mesh,
        in_specs=(act, row, act, row, row, row, row, vec, vec, vec, vec, vec, vec, vec),
        out_specs=(act, act, row, row, row, row, vec, vec, vec, vec, vec, vec, vec),
        check_vma=False,
    )
```

```python
import functools

import jax
import jax.numpy as jnp
from jax import lax
from jax.experimental import pallas as pl
from jax.experimental.pallas import tpu as pltpu
from jax.sharding import PartitionSpec as P

HEADS = 16
EPS = 1e-05
NEG = -1e30
F32 = jnp.float32
BF = jnp.bfloat16


def _dot(a, b, ca, cb):
    return lax.dot_general(a, b, (((ca,), (cb,)), ((), ())), preferred_element_type=F32)


def mm(a, b):
    return _dot(a, b, 1, 0)


def mm_left(a, b):
    return _dot(a, b, 0, 0)


def mm_right(a, b):
    return _dot(a, b, 1, 1)


MESH = pl.DeviceIdType.MESH


def front_kernel(
    tok, cot, win, wo, we, wr, vec, st,
    x_ref, g_ref, n1, wf, wof, wef, wrf, vecs, qkv, att, lse, attn,
    qt, vt, win_s, win_r, vec_s, vec_r, tok_s, tok_r, tok_l, near_s, near_r, core_s, core_r, fwd_s, fwd_r,
    cot_s, cot_r, cot_l, own_l, w_s, w_r, move_s, move_r, move_l,
    *, ns, nd, heads, d, bq, bk, chunks,
):
    seq, me = lax.axis_index("seq"), lax.axis_index("dp")
    half, nearb, core = seq // 2, seq % 2, me % 2
    member = 2 * core + nearb
    n_rows, width = tok.shape
    group = width // 4
    small_rows = win.shape[0]
    stays = half == core
    swap_to = (2 * core + nearb, me - core + half)
    near_to = (seq + 1 - 2 * nearb, me)
    core_to = (seq, me + 1 - 2 * core)

    def offset(k):
        out = me
        bit = 1
        while bit <= k:
            if k & bit:
                out = out + bit - 2 * bit * ((me // bit) % 2)
            bit *= 2
        return out

    def rcopy(src, dst, ss, rs, dev):
        return pltpu.make_async_remote_copy(
            src_ref=src, dst_ref=dst, send_sem=ss, recv_sem=rs, device_id=dev, device_id_type=MESH
        )

    barrier = pltpu.get_barrier_semaphore()

    def hello(dev):
        pl.semaphore_signal(barrier, inc=1, device_id=dev, device_id_type=MESH)

    for k in range(1, nd):
        hello((seq, offset(k)))
    hello(near_to)
    hello((near_to[0], core_to[1]))

    @pl.when(jnp.logical_not(stays))
    def _():
        hello(swap_to)
        pl.semaphore_wait(barrier, nd + 2)

    @pl.when(stays)
    def _():
        pl.semaphore_wait(barrier, nd + 1)

    sends = []

    step = n_rows // chunks
    tok_remote, tok_local = [], []
    for c in range(chunks):
        cut = pl.ds(c * step, step)
        tok_remote.append(rcopy(tok.at[cut], x_ref.at[cut], tok_s.at[c], tok_r.at[c], swap_to))
        tok_local.append(pltpu.make_async_copy(tok.at[cut], x_ref.at[cut], tok_l.at[c]))

    @pl.when(jnp.logical_not(stays))
    def _():
        for c in tok_remote:
            c.start()

    @pl.when(stays)
    def _():
        for c in tok_local:
            c.start()

    vec_copies, win_copies, own_copies = [], [], []
    for k in range(1, nd):
        c = rcopy(vec, vecs.at[me], vec_s.at[k], vec_r.at[k], (seq, offset(k)))
        c.start()
        vec_copies.append(c)
    c = pltpu.make_async_copy(vec, vecs.at[me], own_l.at[0])
    c.start()
    vec_copies.append(c)
    my_rows = pl.ds(pl.multiple_of(me * small_rows, small_rows), small_rows)
    for k in range(nd):
        target = 2 * (core if k % 2 == 0 else 1 - core) + nearb
        for i in range(3):
            src = win.at[:, pl.ds(pl.multiple_of(i * width + target * group, 128), group)]
            dst = wf.at[my_rows, pl.ds(i * group, group)]
            if k == 0:
                c = pltpu.make_async_copy(src, dst, own_l.at[1 + i])
            else:
                c = rcopy(src, dst, win_s.at[k, i], win_r.at[k, i], (seq, offset(k)))
            c.start()
            win_copies.append(c)

    pairs = ((wo, wof), (we, wef), (wr, wrf))

    def at(a, k, part=None):
        high = pairs[a][0].shape[0]
        if part is None:
            return pairs[a][1].at[pl.ds(pl.multiple_of(offset(k) * high, high), high)]
        return pairs[a][1].at[pl.ds(pl.multiple_of(offset(k) * high + part * (high // 2), high // 2), high // 2)]

    held = {}

    def send(a, slot, src, dst, k):
        c = rcopy(src, dst, w_s.at[a, slot], w_r.at[a, slot], (seq, offset(k)))
        c.start()
        held[a, slot] = c

    def weights_start(a):
        if nd == 8:
            send(a, 0, pairs[a][0], at(a, 0), 2)
            send(a, 1, pairs[a][0], at(a, 0), 4)
        else:
            for k in range(2, nd, 2):
                send(a, k, pairs[a][0], at(a, 0), k)
        send(a, 2 if nd == 8 else 1, pairs[a][0], at(a, 0), 1)
        c = pltpu.make_async_copy(pairs[a][0], at(a, 0), own_l.at[4 + a])
        c.start()
        held[a, "own"] = c

    def weights_forward(a):
        if nd == 8:
            held[a, 0].wait_recv()
            send(a, 3, at(a, 2, 0), at(a, 2, 0), 4)
            send(a, 4, at(a, 2), at(a, 2), 1)
            held[a, 1].wait_recv()
            send(a, 5, at(a, 4, 1), at(a, 4, 1), 2)
            send(a, 6, at(a, 4), at(a, 4), 1)
        else:
            for k in range(2, nd, 2):
                held[a, k].wait_recv()
                send(a, k + 1, at(a, k), at(a, k), 1)

    def weights_last(a):
        if nd == 8:
            held[a, 3].wait_recv()
            send(a, 7, at(a, 6, 0), at(a, 6, 0), 1)
            held[a, 5].wait_recv()
            send(a, 8, at(a, 6, 1), at(a, 6, 1), 1)

    def weights_end(a):
        held[a, "own"].wait()
        for slot in (2, 4, 6, 7, 8) if nd == 8 else range(1, nd, 2):
            held[a, slot].wait_recv()
        for slot in range(9) if nd == 8 else range(1, nd):
            held[a, slot].wait_send()

    for c in vec_copies[:-1]:
        c.wait_recv()
        sends.append(c)
    vec_copies[-1].wait()

    def vector(i):
        return jnp.concatenate([vecs[k, i : i + 1, :] for k in range(nd)], axis=1).astype(F32)

    gain, shift = vector(0), vector(1)
    near_copies, core_copies = [], []
    for c in range(chunks):
        cut = pl.ds(c * step, step)

        @pl.when(jnp.logical_not(stays))
        def _(c=c):
            tok_remote[c].wait_recv()

        @pl.when(stays)
        def _(c=c):
            tok_local[c].wait()

        value = x_ref[cut, :].astype(F32)
        center = value - jnp.mean(value, axis=-1, keepdims=True)
        spread = jnp.mean(center * center, axis=-1, keepdims=True)
        place = pl.ds(pl.multiple_of(member * n_rows + c * step, step), step)
        n1[place, :] = (center * lax.rsqrt(spread + EPS) * gain + shift).astype(BF)
        r = rcopy(n1.at[place], n1.at[place], near_s.at[c], near_r.at[c], near_to)
        r.start()
        near_copies.append(r)
        r = rcopy(n1.at[place], n1.at[place], core_s.at[c], core_r.at[c], core_to)
        r.start()
        core_copies.append(r)

    for c in win_copies[:3]:
        c.wait()
    for c in win_copies[3:]:
        c.wait_recv()
        sends.append(c)
    for a in range(3):
        weights_start(a)

    def project(block, c=None):
        size = n_rows if c is None else step
        place = pl.ds(pl.multiple_of(block * n_rows + (0 if c is None else c * step), size), size)
        mixed = _dot(n1[place, :], wf[...], 1, 0).astype(BF)
        qkv[place, :] = mixed
        qt[:, place] = jnp.transpose(mixed[:, :group])
        vt[:, place] = jnp.transpose(mixed[:, 2 * group :])

    project(member)
    for c in core_copies:
        c.wait_recv()
        sends.append(c)
    twin = 2 * (1 - core) + nearb
    project(twin)
    fwd_copies = []
    beside = 2 * core + 1 - nearb
    across = 2 * (1 - core) + 1 - nearb
    for c in range(chunks):
        near_copies[c].wait_recv()
        sends.append(near_copies[c])
        place = pl.ds(pl.multiple_of(beside * n_rows + c * step, step), step)
        r = rcopy(n1.at[place], n1.at[place], fwd_s.at[c], fwd_r.at[c], core_to)
        r.start()
        fwd_copies.append(r)
    project(beside)
    for c in fwd_copies:
        c.wait_recv()
        sends.append(c)
    project(across)

    cot_remote = rcopy(cot, g_ref, cot_s, cot_r, swap_to)
    cot_local = pltpu.make_async_copy(cot, g_ref, cot_l)

    @pl.when(jnp.logical_not(stays))
    def _():
        cot_remote.start()

    @pl.when(stays)
    def _():
        cot_local.start()

    n = ns * n_rows
    scale = d**-0.5
    w = 2 * d
    moves = []
    for i in range(n // bq):
        cs = slice(i * bq, (i + 1) * bq)

        def pair(p, carry, i=i, cs=cs):
            lanes = pl.ds(pl.multiple_of(p * w, w), w)
            key_lanes = pl.ds(pl.multiple_of(group + p * w, w), w)
            outs = []
            for h in range(2):
                row = lax.broadcasted_iota(jnp.int32, (w, bq), 0)
                qm = jnp.where((row >= h * d) & (row < (h + 1) * d), qt[lanes, cs], jnp.zeros((), BF))
                m = jnp.full((1, bq), NEG, F32)
                l = jnp.zeros((1, bq), F32)
                acc = jnp.zeros((d, bq), F32)
                for j in range(0, (i + 1) * bq, bk):
                    s = _dot(qkv[j : j + bk, key_lanes], qm, 1, 0) * scale
                    key = lax.broadcasted_iota(jnp.int32, (bk, bq), 0) + j
                    ok = key >= st[:, cs]
                    if j + bk > i * bq:
                        ok = ok & (key <= lax.broadcasted_iota(jnp.int32, (bk, bq), 1) + i * bq)
                    s = jnp.where(ok, s, NEG)
                    mn = jnp.maximum(m, jnp.max(s, axis=0, keepdims=True))
                    e = jnp.exp(s - mn)
                    a = jnp.exp(m - mn)
                    l = a * l + jnp.sum(e, axis=0, keepdims=True)
                    rows_h = pl.ds(pl.multiple_of(p * w + h * d, d), d)
                    acc = a * acc + _dot(vt[rows_h, j : j + bk], e.astype(BF), 1, 0)
                    m = mn
                outs.append(acc / l)
                lse[p, h : h + 1, cs] = m + jnp.log(l)
            att[cs, lanes] = jnp.transpose(jnp.concatenate(outs, axis=0)).astype(BF)
            return carry

        lax.fori_loop(0, heads // 2, pair, 0)
        mine = attn.at[:, pl.ds(pl.multiple_of(member * group, group), group)]
        dev = (seq - nearb + i % 2, me - core + i // 2)
        r = rcopy(att.at[cs], mine, move_s.at[i], move_r.at[member], dev)
        keep = pltpu.make_async_copy(att.at[cs], mine, move_l)
        moves.append((r, keep))

        @pl.when(member != i)
        def _(r=r):
            r.start()

        @pl.when(member == i)
        def _(keep=keep):
            keep.start()

        if i < 3:
            weights_forward(i)
    for a in range(3):
        weights_last(a)
    for a in range(3):
        weights_end(a)
    for i, (r, keep) in enumerate(moves):
        source = attn.at[:, pl.ds(i * group, group)]
        arrival = pltpu.make_async_copy(source, source, move_r.at[i])

        @pl.when(member != i)
        def _(r=r, arrival=arrival):
            r.wait_send()
            arrival.wait()

        @pl.when(member == i)
        def _(keep=keep):
            keep.wait()

    @pl.when(jnp.logical_not(stays))
    def _():
        cot_remote.wait()
        for c in tok_remote:
            c.wait_send()

    @pl.when(stays)
    def _():
        cot_local.wait()

    for c in sends:
        c.wait_send()


def front(tok, cot, win, wo, we, wr, vec, starts, ns, nd, heads, d):
    n_rows, width = tok.shape
    n, group, chunks = n_rows * ns, width // 4, 4
    slots = 9 if nd == 8 else nd
    any_, vmem = pl.BlockSpec(memory_space=pl.ANY), pl.BlockSpec(memory_space=pltpu.VMEM)
    full = lambda a: jax.ShapeDtypeStruct((a.shape[0] * nd, a.shape[1]), BF)
    dma = lambda *shape: pltpu.SemaphoreType.DMA(shape)
    sds = jax.ShapeDtypeStruct
    return pl.pallas_call(
        functools.partial(front_kernel, ns=ns, nd=nd, heads=heads, d=d, bq=n_rows, bk=n_rows, chunks=chunks),
        in_specs=[any_] * 7 + [vmem],
        out_specs=[vmem, any_, vmem, vmem, any_, any_, any_, vmem, vmem, vmem, vmem, vmem],
        out_shape=[
            sds(tok.shape, BF), sds(tok.shape, BF), sds((n, width), BF), sds((width, 3 * group), BF),
            full(wo), full(we), full(wr), sds((nd, *vec.shape), BF), sds((n, 3 * group), BF),
            sds((n, group), BF), sds((heads // 2, 2, n), F32), sds(tok.shape, BF),
        ],
        scratch_shapes=[
            pltpu.VMEM((group, n), BF), pltpu.VMEM((group, n), BF),
            dma(nd, 3), dma(nd, 3), dma(nd), dma(nd), dma(chunks), dma(chunks), dma(chunks),
            dma(chunks), dma(chunks), dma(chunks), dma(chunks), dma(chunks), dma(chunks),
            pltpu.SemaphoreType.DMA, pltpu.SemaphoreType.DMA, pltpu.SemaphoreType.DMA,
            dma(7), dma(3, slots), dma(3, slots), dma(4), dma(4), pltpu.SemaphoreType.DMA,
        ],
        compiler_params=pltpu.CompilerParams(
            collective_id=0, has_side_effects=True, vmem_limit_bytes=52 << 20
        ),
        cost_estimate=pl.CostEstimate(
            flops=8 * n * n * d * heads, bytes_accessed=60_000_000, transcendentals=n * n * heads
        ),
    )(tok, cot, win, wo, we, wr, vec, starts)


def bwd_kernel(
    st_ref, q_ref, k_ref, v_ref, do_ref, o_ref, lse_ref, dq_ref, dk_ref, dv_ref,
    qm_ref, dom_ref, qt_ref, dot_ref, kt_ref, dqt_ref, delta_ref, *, bq, bk, scale
):
    n, w = q_ref.shape
    d = w // 2
    lane = lax.broadcasted_iota(jnp.int32, (n, w), 1)
    z = jnp.zeros((), BF)
    for h in range(2):
        sel = (lane >= h * d) & (lane < (h + 1) * d)
        qm = jnp.where(sel, q_ref[...], z)
        dom = jnp.where(sel, do_ref[...], z)
        qm_ref[h] = qm
        dom_ref[h] = dom
        qt_ref[h] = jnp.transpose(qm)
        dot_ref[h] = jnp.transpose(dom)
    kt_ref[...] = jnp.transpose(k_ref[...])
    prod = jnp.transpose(do_ref[...].astype(F32) * o_ref[...].astype(F32))
    for h in range(2):
        delta_ref[h : h + 1, :] = jnp.sum(prod[h * d : (h + 1) * d], axis=0, keepdims=True)
    dqt_ref[...] = jnp.zeros_like(dqt_ref)
    for j in range(0, n, bk):
        dk = jnp.zeros((bk, w), F32)
        dv = jnp.zeros((bk, w), F32)
        for i in range(j // bq, n // bq):
            cs = slice(i * bq, (i + 1) * bq)
            st = st_ref[:, cs]
            key = lax.broadcasted_iota(jnp.int32, (bk, bq), 0) + j
            ok = key >= st
            if j + bk > i * bq:
                ok = ok & (key <= lax.broadcasted_iota(jnp.int32, (bk, bq), 1) + i * bq)
            for h in range(2):
                s = _dot(k_ref[j : j + bk, :], qt_ref[h, :, cs], 1, 0) * scale
                s = jnp.where(ok, s, NEG)
                p = jnp.exp(s - lse_ref[0, h : h + 1, cs])
                dp = _dot(v_ref[j : j + bk, :], dot_ref[h, :, cs], 1, 0)
                ds = (p * (dp - delta_ref[h : h + 1, cs])).astype(BF)
                dv = dv + _dot(p.astype(BF), dom_ref[h, cs, :], 1, 0)
                dk = dk + _dot(ds, qm_ref[h, cs, :], 1, 0)
                dqt_ref[h * d : (h + 1) * d, cs] += _dot(kt_ref[h * d : (h + 1) * d, j : j + bk], ds, 1, 0)
        dk_ref[j : j + bk, :] = (dk * scale).astype(BF)
        dv_ref[j : j + bk, :] = dv.astype(BF)
    dq_ref[...] = (jnp.transpose(dqt_ref[...]) * scale).astype(BF)


def flash_bwd(starts, qkv, grad, out, lse, heads, d, bq=256, bk=512):
    n, w, pairs = starts.shape[1], 2 * d, heads // 2
    blk = lambda c: pl.BlockSpec((n, w), lambda p: (0, c + p))
    return pl.pallas_call(
        functools.partial(bwd_kernel, bq=bq, bk=bk, scale=d**-0.5),
        grid=(pairs,),
        in_specs=[
            pl.BlockSpec((1, n), lambda p: (0, 0)), blk(0), blk(pairs), blk(2 * pairs), blk(0), blk(0),
            pl.BlockSpec((1, 2, n), lambda p: (p, 0, 0)),
        ],
        out_specs=[blk(0)] * 3,
        out_shape=[jax.ShapeDtypeStruct((n, pairs * w), BF)] * 3,
        scratch_shapes=[
            pltpu.VMEM((2, n, w), BF), pltpu.VMEM((2, n, w), BF), pltpu.VMEM((2, w, n), BF),
            pltpu.VMEM((2, w, n), BF), pltpu.VMEM((w, n), BF), pltpu.VMEM((w, n), F32), pltpu.VMEM((2, n), F32),
        ],
        compiler_params=pltpu.CompilerParams(vmem_limit_bytes=56 << 20),
        cost_estimate=pl.CostEstimate(
            flops=20 * n * n * d * heads, bytes_accessed=16 * n * w * pairs, transcendentals=n * n * heads
        ),
    )(starts, qkv, qkv, qkv, grad, out, lse)


def layer_normalize(values, gain, shift):
    center = values - jnp.mean(values, axis=-1, keepdims=True)
    spread = jnp.mean(center * center, axis=-1, keepdims=True)
    return center * lax.rsqrt(spread + EPS) * gain + shift


def smooth_gate(values):
    return jax.nn.gelu(values, approximate=True)


def rows(array, start, size):
    return lax.dynamic_slice_in_dim(array, start, size, 0)


def cols(array, start, size):
    return lax.dynamic_slice_in_dim(array, start, size, 1)


def put(array, piece, row, col):
    return lax.dynamic_update_slice(array, piece, (row, col))


def bf_round(x):
    return lax.reduce_precision(x, 8, 7)


class Links:
    def __init__(self, ns, nd):
        self.ns, self.nd = ns, nd

    def go(self, array, target):
        pairs = []
        for s in range(self.ns):
            for d in range(self.nd):
                ts, td = target(s, d)
                pairs.append((s * self.nd + d, ts * self.nd + td))
        return lax.ppermute(array, ("seq", "dp"), pairs)

    def dp(self, array, k):
        return self.go(array, lambda s, d: (s, d ^ k))

    def core(self, array):
        return self.dp(array, 1)

    def near(self, array):
        return self.go(array, lambda s, d: (s ^ 1, d))

    def far(self, array):
        return self.go(array, lambda s, d: (s ^ 2, d))

    def both(self, array):
        return self.go(array, lambda s, d: (s ^ 1, d ^ 1))

    def swap(self, array):
        return self.go(array, lambda s, d: (2 * (d % 2) + s % 2, d - d % 2 + s // 2))


def on_device(
    tokens, lengths, cotangent, mixer_input, mixer_output, expand_weight, reduce_weight,
    first_gain, first_shift, second_gain, second_shift, output_bias, expand_bias, reduce_bias,
):
    ns, nd = lax.axis_size("seq"), lax.axis_size("dp")
    links = Links(ns, nd)
    seq, me = lax.axis_index("seq"), lax.axis_index("dp")
    half, near_bit, core = seq // 2, seq % 2, me % 2
    column = me // 2
    member = 2 * core + near_bit
    n_rows, width = tokens.shape[1:]
    slots = n_rows * ns
    head_dim = width // HEADS
    hidden = reduce_weight.shape[0] * nd
    group = width // 4
    my_heads = HEADS // 4

    lengths_row = jnp.where(half == core, lengths[0], links.core(lengths)[0])
    entry = jnp.arange(lengths_row.shape[0])
    ends = jnp.sum(jnp.where(entry[None, :] <= entry[:, None], lengths_row[None, :], 0), axis=1)
    place = jnp.arange(slots, dtype=jnp.int32)
    passed = place[:, None] >= ends[None, :]
    starts = jnp.max(jnp.where(passed, ends[None, :], 0), axis=1)
    starts = jnp.where(place < ends[-1], starts, place).reshape(1, slots)
    live = (member * n_rows + jnp.arange(n_rows, dtype=jnp.int32) < ends[-1]).astype(F32)

    small, small_rows = width // nd, mixer_input.shape[0]
    vectors = jnp.concatenate(
        [first_gain, first_shift, second_gain, second_shift, output_bias, reduce_bias, expand_bias]
    ).reshape(-1, small)
    vectors = jnp.concatenate([vectors, jnp.zeros((-vectors.shape[0] % 16, small), BF)])
    (
        x_low, grad_low, normed_all, input_full, output_full, expand_full, reduce_full, vectors,
        qkv, attended, logsum, attention,
    ) = front(
        tokens[0], cotangent[0], mixer_input, mixer_output, expand_weight, reduce_weight, vectors,
        starts, ns, nd, my_heads, head_dim,
    )
    vectors = vectors.astype(F32)
    gain_one, shift_one, gain_two, shift_two, output_add, reduce_add = (
        vectors[:, i].reshape(-1) for i in range(6)
    )
    expand_add = vectors[:, 6 : 6 + hidden // nd // small].reshape(-1)
    inputs = x_low.astype(F32)
    moves = (lambda a: a, links.near, links.core, links.both)

    resid = inputs + mm(attention, output_full) + output_add
    normed_two = layer_normalize(resid, gain_two, shift_two).astype(BF)
    expanded = mm(normed_two, expand_full) + expand_add
    active = smooth_gate(expanded).astype(BF)
    result = (resid + mm(active, reduce_full) + reduce_add).astype(BF)
    layer_output = links.swap(result)

    def scatter(parts):
        chip = [parts(k).astype(F32) + links.core(parts(k ^ 1).astype(BF)).astype(F32) for k in range(0, nd, 2)]
        total = chip[0]
        for i in range(1, nd // 2):
            total = total + links.dp(chip[i].astype(BF), 2 * i).astype(F32)
        high = total.shape[0] // 2
        part = rows(total, near_bit * high, high)
        part = part + links.near(rows(total, (1 - near_bit) * high, high).astype(BF)).astype(F32)
        quarter = rows(part, half * (high // 2), high // 2)
        quarter = quarter + links.far(rows(part, (1 - half) * (high // 2), high // 2).astype(BF)).astype(F32)
        quarter = quarter.astype(BF)
        other = links.far(quarter)
        part = jnp.zeros((high, total.shape[1]), BF)
        part = put(part, quarter, half * (high // 2), 0)
        part = put(part, other, (1 - half) * (high // 2), 0)
        other = links.near(part)
        full = jnp.zeros(total.shape, F32)
        full = put(full, part.astype(F32), near_bit * high, 0)
        return put(full, other.astype(F32), (1 - near_bit) * high, 0)

    def scatter_rows(array):
        high = array.shape[0] // nd
        return scatter(lambda k: rows(array, (me ^ k) * high, high))

    grad_result = grad_low.astype(F32) * live[:, None]
    result_low = grad_result.astype(BF)
    reduce_sum = scatter_rows(mm_left(active, result_low).astype(BF))
    reduce_bias_sum = jnp.sum(grad_result, axis=0)
    grad_active = mm_right(result_low, reduce_full)
    _, gate_back = jax.vjp(smooth_gate, expanded)
    grad_expanded = gate_back(grad_active)[0]
    expand_bias_sum = jnp.sum(grad_expanded, axis=0)
    expanded_low = grad_expanded.astype(BF)
    expand_sum = scatter_rows(mm_left(normed_two, expanded_low).astype(BF))
    grad_normed_two = mm_right(expanded_low, expand_full)
    _, second_back = jax.vjp(layer_normalize, resid, gain_two, shift_two)
    resid_part, gain_two_sum, shift_two_sum = second_back(grad_normed_two)
    grad_resid = grad_result + resid_part
    output_bias_sum = jnp.sum(grad_resid, axis=0)
    resid_low = grad_resid.astype(BF)
    output_sum = scatter_rows(mm_left(attention, resid_low).astype(BF))
    grad_attention = mm_right(resid_low, output_full).astype(BF)

    grad_attended = jnp.zeros((slots, group), BF)
    for j in range(4):
        piece = moves[j](cols(grad_attention, (member ^ j) * group, group))
        grad_attended = put(grad_attended, piece, (member ^ j) * n_rows, 0)
    grad_mixed = jnp.concatenate(
        flash_bwd(starts, qkv, grad_attended, attended, logsum, my_heads, head_dim), axis=1
    )

    def normed_grad(j):
        return mm_right(rows(grad_mixed, (member ^ j) * n_rows, n_rows), input_full)

    near_term = normed_grad(1) + links.core(normed_grad(3).astype(BF)).astype(F32)
    near_term = links.near(near_term.astype(BF)).astype(F32)
    grad_normed_one = normed_grad(0) + links.core(normed_grad(2).astype(BF)).astype(F32) + near_term
    _, first_back = jax.vjp(layer_normalize, inputs, gain_one, shift_one)
    inputs_part, gain_one_sum, shift_one_sum = first_back(grad_normed_one)
    tokens_gradient = links.swap((grad_resid + inputs_part).astype(BF)).astype(F32)

    input_term = mm_left(normed_all, grad_mixed)
    pair_rows = 2 * small_rows
    total = rows(input_term, column * pair_rows, pair_rows)
    for i in range(1, nd // 2):
        piece = rows(input_term, (column ^ i) * pair_rows, pair_rows).astype(BF)
        total = total + links.dp(piece, 2 * i).astype(F32)
    total = bf_round(total)
    total = (total + links.far(total.astype(BF)).astype(F32)).astype(BF)
    near_total = links.near(total)
    held = [
        (member, rows(total, core * small_rows, small_rows)),
        (member ^ 1, rows(near_total, core * small_rows, small_rows)),
        (member ^ 2, links.core(rows(total, (1 - core) * small_rows, small_rows))),
        (member ^ 3, links.core(rows(near_total, (1 - core) * small_rows, small_rows))),
    ]
    input_sum = jnp.zeros((small_rows, 3 * width), F32)
    for which, piece in held:
        for i in range(3):
            part = piece[:, i * group : (i + 1) * group].astype(F32)
            input_sum = put(input_sum, part, 0, i * width + which * group)

    sums = jnp.stack([gain_one_sum, shift_one_sum, gain_two_sum, shift_two_sum, output_bias_sum, reduce_bias_sum])
    sums = jnp.concatenate([sums.reshape(-1), expand_bias_sum])
    sums = lax.psum(sums, ("seq", "dp"))
    wide = hidden // nd
    vector_sums = [lax.dynamic_slice(sums, (i * width + me * small,), (small,)) for i in range(6)]
    expand_bias_out = lax.dynamic_slice(sums, (6 * width + me * wide,), (wide,))

    return (
        layer_output[None],
        tokens_gradient[None],
        input_sum,
        output_sum,
        expand_sum,
        reduce_sum,
        vector_sums[0],
        vector_sums[1],
        vector_sums[2],
        vector_sums[3],
        vector_sums[4],
        expand_bias_out,
        vector_sums[5],
    )


def solution(mesh):
    row, vec = P("dp", None), P("dp")
    act = P("dp", "seq", None)
    return jax.shard_map(
        on_device,
        mesh=mesh,
        in_specs=(act, row, act, row, row, row, row, vec, vec, vec, vec, vec, vec, vec),
        out_specs=(act, act, row, row, row, row, vec, vec, vec, vec, vec, vec, vec),
        check_vma=False,
    )
```

```python
import functools

import jax
import jax.numpy as jnp
from jax import lax
from jax.experimental import pallas as pl
from jax.experimental.pallas import tpu as pltpu
from jax.sharding import PartitionSpec as P

HEADS = 16
EPS = 1e-05
NEG = -1e30
F32 = jnp.float32
BF = jnp.bfloat16


def _dot(a, b, ca, cb):
    return lax.dot_general(a, b, (((ca,), (cb,)), ((), ())), preferred_element_type=F32)


def mm(a, b):
    return _dot(a, b, 1, 0)


def mm_left(a, b):
    return _dot(a, b, 0, 0)


def mm_right(a, b):
    return _dot(a, b, 1, 1)


MESH = pl.DeviceIdType.MESH


def front_kernel(
    tok, cot, win, wo, we, wr, vec, st,
    x_ref, g_ref, gp_ref, n1t, wf, wof, wef, wrf, vecs, qkv, att, lse, attn,
    n1, qt, vt, win_s, win_r, vec_s, vec_r, tok_s, tok_r, tok_l, near_s, near_r, core_s, core_r, fwd_s, fwd_r,
    cot_s, cot_r, cot_l, gp_s, gp_r, own_l, w_s, w_r, move_s, move_r, move_l,
    *, ns, nd, heads, d, bq, bk, chunks,
):
    seq, me = lax.axis_index("seq"), lax.axis_index("dp")
    half, nearb, core = seq // 2, seq % 2, me % 2
    member = 2 * core + nearb
    n_rows, width = tok.shape
    group = width // 4
    small_rows = win.shape[0]
    stays = half == core
    swap_to = (2 * core + nearb, me - core + half)
    near_to = (seq + 1 - 2 * nearb, me)
    core_to = (seq, me + 1 - 2 * core)

    def offset(k):
        out = me
        bit = 1
        while bit <= k:
            if k & bit:
                out = out + bit - 2 * bit * ((me // bit) % 2)
            bit *= 2
        return out

    def rcopy(src, dst, ss, rs, dev):
        return pltpu.make_async_remote_copy(
            src_ref=src, dst_ref=dst, send_sem=ss, recv_sem=rs, device_id=dev, device_id_type=MESH
        )

    barrier = pltpu.get_barrier_semaphore()

    def hello(dev):
        pl.semaphore_signal(barrier, inc=1, device_id=dev, device_id_type=MESH)

    for k in range(1, nd):
        hello((seq, offset(k)))
    hello(near_to)
    hello((near_to[0], core_to[1]))

    @pl.when(jnp.logical_not(stays))
    def _():
        hello(swap_to)
        pl.semaphore_wait(barrier, nd + 2)

    @pl.when(stays)
    def _():
        pl.semaphore_wait(barrier, nd + 1)

    sends = []

    step = n_rows // chunks
    tok_remote, tok_local = [], []
    for c in range(chunks):
        cut = pl.ds(c * step, step)
        tok_remote.append(rcopy(tok.at[cut], x_ref.at[cut], tok_s.at[c], tok_r.at[c], swap_to))
        tok_local.append(pltpu.make_async_copy(tok.at[cut], x_ref.at[cut], tok_l.at[c]))

    @pl.when(jnp.logical_not(stays))
    def _():
        for c in tok_remote:
            c.start()

    @pl.when(stays)
    def _():
        for c in tok_local:
            c.start()

    vec_copies, win_copies, own_copies = [], [], []
    for k in range(1, nd):
        c = rcopy(vec, vecs.at[me], vec_s.at[k], vec_r.at[k], (seq, offset(k)))
        c.start()
        vec_copies.append(c)
    c = pltpu.make_async_copy(vec, vecs.at[me], own_l.at[0])
    c.start()
    vec_copies.append(c)
    my_rows = pl.ds(pl.multiple_of(me * small_rows, small_rows), small_rows)
    for k in range(nd):
        target = 2 * (core if k % 2 == 0 else 1 - core) + nearb
        for i in range(3):
            src = win.at[:, pl.ds(pl.multiple_of(i * width + target * group, 128), group)]
            dst = wf.at[my_rows, pl.ds(i * group, group)]
            if k == 0:
                c = pltpu.make_async_copy(src, dst, own_l.at[1 + i])
            else:
                c = rcopy(src, dst, win_s.at[k, i], win_r.at[k, i], (seq, offset(k)))
            c.start()
            win_copies.append(c)

    pairs = ((wo, wof), (we, wef), (wr, wrf))

    def source(a, k):
        return we.at[core if k % 2 == 0 else 1 - core] if a == 1 else pairs[a][0]

    def at(a, k, part=None):
        high = pairs[a][0].shape[-2]
        row = (offset(k) // 2 if a == 2 else offset(k)) * high
        if part is None:
            return pairs[a][1].at[pl.ds(pl.multiple_of(row, high), high)]
        return pairs[a][1].at[pl.ds(pl.multiple_of(row + part * (high // 2), high // 2), high // 2)]

    held = {}

    def send(a, slot, src, dst, k):
        c = rcopy(src, dst, w_s.at[a, slot], w_r.at[a, slot], (seq, offset(k)))
        c.start()
        held[a, slot] = c

    direct = (2, 3, 4, 5) if nd == 8 else range(2, nd)

    def weights_start(a):
        for k in direct:
            if k % 2 == 0 or a == 1:
                send(a, k, source(a, k), at(a, 0), k)
        if a < 2:
            send(a, 1, source(a, 1), at(a, 0), 1)
        c = pltpu.make_async_copy(source(a, 0), at(a, 0), own_l.at[4 + a])
        c.start()
        held[a, "own"] = c

    def weights_forward(a):
        for k in direct:
            if k % 2 == 0 or a == 1:
                held[a, k].wait_recv()
                if nd == 8:
                    send(a, 8 + k, at(a, k, k // 4), at(a, k, k // 4), 6 - k // 2 * 2)
                if a == 0:
                    send(a, k + 1 if nd > 8 else 14 + k // 2, at(a, k), at(a, k), 1)

    def weights_last(a):
        if nd == 8 and a == 0:
            for part, k in ((0, 2), (1, 4)):
                held[a, 8 + k].wait_recv()
                send(a, 3 + 2 * part, at(a, 6, part), at(a, 6, part), 1)

    def weights_end(a):
        held[a, "own"].wait()
        waited = set(direct) if a else {k for k in direct if k % 2 == 0}
        if nd == 8 and a == 0:
            waited |= {10, 12}
        for (b, slot), c in held.items():
            if b == a and slot != "own":
                if slot not in waited:
                    c.wait_recv()
                c.wait_send()

    for c in vec_copies[:-1]:
        c.wait_recv()
        sends.append(c)
    vec_copies[-1].wait()

    def vector(i):
        return jnp.concatenate([vecs[k, i : i + 1, :] for k in range(nd)], axis=1).astype(F32)

    gain, shift = vector(0), vector(1)
    near_copies, core_copies = [], []
    for c in range(chunks):
        cut = pl.ds(c * step, step)

        @pl.when(jnp.logical_not(stays))
        def _(c=c):
            tok_remote[c].wait_recv()

        @pl.when(stays)
        def _(c=c):
            tok_local[c].wait()

        value = x_ref[cut, :].astype(F32)
        center = value - jnp.mean(value, axis=-1, keepdims=True)
        spread = jnp.mean(center * center, axis=-1, keepdims=True)
        place = pl.ds(pl.multiple_of(member * n_rows + c * step, step), step)
        n1[place, :] = (center * lax.rsqrt(spread + EPS) * gain + shift).astype(BF)
        r = rcopy(n1.at[place], n1.at[place], near_s.at[c], near_r.at[c], near_to)
        r.start()
        near_copies.append(r)
        r = rcopy(n1.at[place], n1.at[place], core_s.at[c], core_r.at[c], core_to)
        r.start()
        core_copies.append(r)

    for c in win_copies[:3]:
        c.wait()
    for c in win_copies[3:]:
        c.wait_recv()
        sends.append(c)
    for a in range(3):
        weights_start(a)

    def project(block, c=None):
        size = n_rows if c is None else step
        place = pl.ds(pl.multiple_of(block * n_rows + (0 if c is None else c * step), size), size)
        mixed = _dot(n1[place, :], wf[...], 1, 0).astype(BF)
        qkv[place, :] = mixed
        n1t[:, place] = jnp.transpose(n1[place, :])
        qt[:, place] = jnp.transpose(mixed[:, :group])
        vt[:, place] = jnp.transpose(mixed[:, 2 * group :])

    project(member)
    for c in core_copies:
        c.wait_recv()
        sends.append(c)
    twin = 2 * (1 - core) + nearb
    project(twin)
    fwd_copies = []
    beside = 2 * core + 1 - nearb
    across = 2 * (1 - core) + 1 - nearb
    for c in range(chunks):
        near_copies[c].wait_recv()
        sends.append(near_copies[c])
        place = pl.ds(pl.multiple_of(beside * n_rows + c * step, step), step)
        r = rcopy(n1.at[place], n1.at[place], fwd_s.at[c], fwd_r.at[c], core_to)
        r.start()
        fwd_copies.append(r)
    project(beside)
    for c in fwd_copies:
        c.wait_recv()
        sends.append(c)
    project(across)

    cot_remote = rcopy(cot, g_ref, cot_s, cot_r, swap_to)
    cot_local = pltpu.make_async_copy(cot, g_ref, cot_l)

    @pl.when(jnp.logical_not(stays))
    def _():
        cot_remote.start()

    @pl.when(stays)
    def _():
        cot_local.start()

    n = ns * n_rows
    scale = d**-0.5
    w = 2 * d
    moves = []
    for i in range(n // bq):
        cs = slice(i * bq, (i + 1) * bq)

        def pair(p, carry, i=i, cs=cs):
            lanes = pl.ds(pl.multiple_of(p * w, w), w)
            key_lanes = pl.ds(pl.multiple_of(group + p * w, w), w)
            outs = []
            for h in range(2):
                row = lax.broadcasted_iota(jnp.int32, (w, bq), 0)
                qm = jnp.where((row >= h * d) & (row < (h + 1) * d), qt[lanes, cs], jnp.zeros((), BF))
                m = jnp.full((1, bq), NEG, F32)
                l = jnp.zeros((1, bq), F32)
                acc = jnp.zeros((d, bq), F32)
                for j in range(0, (i + 1) * bq, bk):
                    s = _dot(qkv[j : j + bk, key_lanes], qm, 1, 0) * scale
                    key = lax.broadcasted_iota(jnp.int32, (bk, bq), 0) + j
                    ok = key >= st[:, cs]
                    if j + bk > i * bq:
                        ok = ok & (key <= lax.broadcasted_iota(jnp.int32, (bk, bq), 1) + i * bq)
                    s = jnp.where(ok, s, NEG)
                    mn = jnp.maximum(m, jnp.max(s, axis=0, keepdims=True))
                    e = jnp.exp(s - mn)
                    a = jnp.exp(m - mn)
                    l = a * l + jnp.sum(e, axis=0, keepdims=True)
                    rows_h = pl.ds(pl.multiple_of(p * w + h * d, d), d)
                    acc = a * acc + _dot(vt[rows_h, j : j + bk], e.astype(BF), 1, 0)
                    m = mn
                outs.append(acc / l)
                lse[p, h : h + 1, cs] = m + jnp.log(l)
            att[cs, lanes] = jnp.transpose(jnp.concatenate(outs, axis=0)).astype(BF)
            return carry

        lax.fori_loop(0, heads // 2, pair, 0)
        mine = attn.at[:, pl.ds(pl.multiple_of(member * group, group), group)]
        dev = (seq - nearb + i % 2, me - core + i // 2)
        r = rcopy(att.at[cs], mine, move_s.at[i], move_r.at[member], dev)
        keep = pltpu.make_async_copy(att.at[cs], mine, move_l)
        moves.append((r, keep))

        @pl.when(member != i)
        def _(r=r):
            r.start()

        @pl.when(member == i)
        def _(keep=keep):
            keep.start()

        if i < 3:
            weights_forward(i)
    weights_last(0)

    @pl.when(jnp.logical_not(stays))
    def _():
        cot_remote.wait_recv()

    @pl.when(stays)
    def _():
        cot_local.wait()

    twin_cot = rcopy(g_ref, gp_ref, gp_s, gp_r, core_to)
    twin_cot.start()
    for a in range(3):
        weights_end(a)
    for i, (r, keep) in enumerate(moves):
        source = attn.at[:, pl.ds(i * group, group)]
        arrival = pltpu.make_async_copy(source, source, move_r.at[i])

        @pl.when(member != i)
        def _(r=r, arrival=arrival):
            r.wait_send()
            arrival.wait()

        @pl.when(member == i)
        def _(keep=keep):
            keep.wait()

    @pl.when(jnp.logical_not(stays))
    def _():
        cot_remote.wait_send()
        for c in tok_remote:
            c.wait_send()

    twin_cot.wait()
    for c in sends:
        c.wait_send()


def front(tok, cot, win, wo, we, wr, vec, starts, ns, nd, heads, d):
    n_rows, width = tok.shape
    n, group, chunks = n_rows * ns, width // 4, 4
    slots = 17 if nd == 8 else nd
    compact = lambda a: jax.ShapeDtypeStruct((a.shape[0] * (nd // 2), a.shape[1]), BF)
    any_, vmem = pl.BlockSpec(memory_space=pl.ANY), pl.BlockSpec(memory_space=pltpu.VMEM)
    full = lambda a: jax.ShapeDtypeStruct((a.shape[0] * nd, a.shape[1]), BF)
    dma = lambda *shape: pltpu.SemaphoreType.DMA(shape)
    sds = jax.ShapeDtypeStruct
    return pl.pallas_call(
        functools.partial(front_kernel, ns=ns, nd=nd, heads=heads, d=d, bq=n_rows, bk=n_rows, chunks=chunks),
        in_specs=[any_] * 7 + [vmem],
        out_specs=[vmem, any_, any_, vmem, vmem, any_, any_, any_, vmem, vmem, vmem, vmem, vmem],
        out_shape=[
            sds(tok.shape, BF), sds(tok.shape, BF), sds(tok.shape, BF), sds((width, n), BF), sds((width, 3 * group), BF),
            full(wo), sds((width, we.shape[2]), BF), compact(wr), sds((nd, *vec.shape), BF), sds((n, 3 * group), BF),
            sds((n, group), BF), sds((heads // 2, 2, n), F32), sds(tok.shape, BF),
        ],
        scratch_shapes=[
            pltpu.VMEM((n, width), BF), pltpu.VMEM((group, n), BF), pltpu.VMEM((group, n), BF),
            dma(nd, 3), dma(nd, 3), dma(nd), dma(nd), dma(chunks), dma(chunks), dma(chunks),
            dma(chunks), dma(chunks), dma(chunks), dma(chunks), dma(chunks), dma(chunks),
            pltpu.SemaphoreType.DMA, pltpu.SemaphoreType.DMA, pltpu.SemaphoreType.DMA,
            pltpu.SemaphoreType.DMA, pltpu.SemaphoreType.DMA, dma(7), dma(3, slots), dma(3, slots), dma(4), dma(4), pltpu.SemaphoreType.DMA,
        ],
        compiler_params=pltpu.CompilerParams(
            collective_id=0, has_side_effects=True, vmem_limit_bytes=52 << 20
        ),
        cost_estimate=pl.CostEstimate(
            flops=8 * n * n * d * heads, bytes_accessed=60_000_000, transcendentals=n * n * heads
        ),
    )(tok, cot, win, wo, we, wr, vec, starts)


def back_kernel(
    ga, qkv, att, lse, st, n1t, wf, x, gres, gain, v_in, res, dwr, dwe, dwo,
    out, tg, insum, osum, esum, rsum, vout,
    go, qt, dot, kt, dqt, delta, gm, zin, far_in, tot, tot2, near_in, core_in, cst, crc, nst, nrc, tgs,
    vmine, vrc, vz, own, fwd, r1, r2, ns_st, ns_rc, keep, fs_st, fs_rc, fb, eb,
    move_s, move_r, move_l, a_s, a_r, a_l, d_s, d_r, out_s, out_r, out_l, tg_s, tg_r, tg_l, v_s, v_r, vz_s, vz_r,
    *, ns, nd, heads, d, bq, bk, chunks,
):
    seq, me = lax.axis_index("seq"), lax.axis_index("dp")
    half, nearb, core = seq // 2, seq % 2, me % 2
    member = 2 * core + nearb
    beside, twin, across = 2 * core + 1 - nearb, 2 * (1 - core) + nearb, 2 * (1 - core) + 1 - nearb
    n_rows, width = x.shape
    n, group, ncol = ns * n_rows, width // 4, nd // 2
    stays = half == core
    swap_to = (2 * core + nearb, me - core + half)
    near_to = (seq + 1 - 2 * nearb, me)
    far_to = (seq + 2 - 4 * half, me)
    third_to = (seq + 1 - 2 * nearb + 2 - 4 * half, me)
    core_to = (seq, me + 1 - 2 * core)

    def offset(k):
        result = me
        bit = 1
        while bit <= k:
            if k & bit:
                result = result + bit - 2 * bit * ((me // bit) % 2)
            bit *= 2
        return result

    def rcopy(src, dst, ss, rs, dev):
        return pltpu.make_async_remote_copy(
            src_ref=src, dst_ref=dst, send_sem=ss, recv_sem=rs, device_id=dev, device_id_type=MESH
        )

    def row_loop(total, size, body):
        def one(t, carry):
            body(pl.multiple_of(t * size, size))
            return carry

        lax.fori_loop(0, total // size, one, 0)

    barrier = pltpu.get_barrier_semaphore()

    def hello(dev):
        pl.semaphore_signal(barrier, inc=1, device_id=dev, device_id_type=MESH)

    for k in range(1, nd):
        hello((seq, offset(k)))
    for dev in (near_to, far_to, third_to, (near_to[0], core_to[1])):
        hello(dev)

    @pl.when(jnp.logical_not(stays))
    def _():
        hello(swap_to)
        pl.semaphore_wait(barrier, nd + 4)

    @pl.when(stays)
    def _():
        pl.semaphore_wait(barrier, nd + 3)

    sends = []
    held = {}

    moves = []
    for i in range(4):
        src = ga.at[:, pl.ds(i * group, group)]
        mine = go.at[pl.ds(pl.multiple_of(member * n_rows, n_rows), n_rows)]
        dev = (seq - nearb + i % 2, me - core + i // 2)
        r = rcopy(src, mine, move_s.at[i], move_r.at[member], dev)
        stay = pltpu.make_async_copy(src, mine, move_l)
        moves.append((r, stay))

        @pl.when(member != i)
        def _(r=r):
            r.start()

        @pl.when(member == i)
        def _(stay=stay):
            stay.start()

    terms = (dwr, dwe, dwo, zin)
    high = [t.shape[0] // ncol for t in terms]
    wide = [t.shape[1] for t in terms]

    def block(a, kc, part=None):
        row = (offset(2 * kc) // 2) * high[a]
        if part is None:
            return terms[a].at[pl.ds(pl.multiple_of(row, high[a]), high[a])]
        low = high[a] // 2
        return terms[a].at[pl.ds(pl.multiple_of(row + part * low, low), low)]

    def send(a, slot, src, dst, dev):
        c = rcopy(src, dst, a_s.at[a, slot], a_r.at[a, slot], dev)
        c.start()
        held[a, slot] = c
        sends.append(c)

    def lanes(first, size):
        return pl.ds(pl.multiple_of(first, 128), size)

    def s0(a):
        local = [pltpu.make_async_copy(block(a, 0), own[a], a_l.at[a, 0])]
        if nd == 8:
            x_to, y_to = (seq, offset(2)), (seq, offset(4))
            send(a, 0, block(a, 1, 0), r1[a].at[0], x_to)
            send(a, 2, block(a, 2, 1), r1[a].at[2], y_to)
            send(a, 1, block(a, 3, 0), r1[a].at[1], x_to)
            send(a, 3, block(a, 3, 1), r1[a].at[3], y_to)
            local.append(pltpu.make_async_copy(block(a, 2, 0), fwd[a].at[0], a_l.at[a, 1]))
            local.append(pltpu.make_async_copy(block(a, 1, 1), fwd[a].at[1], a_l.at[a, 2]))
        else:
            for kc in range(1, ncol):
                send(a, kc, block(a, kc), r1[a].at[kc - 1], (seq, offset(2 * kc)))
        for c in local:
            c.start()
        held[a, "local"] = local

    def s1(a):
        for c in held[a, "local"]:
            c.wait()
        if nd == 8:
            for part, k in ((0, 4), (1, 2)):
                held[a, 1 + 2 * part].wait_recv()

                def add(t, part=part):
                    cut = pl.ds(t, 16)
                    fwd[a][part, cut, :] = (
                        fwd[a][part, cut, :].astype(F32) + r1[a][1 + 2 * part, cut, :].astype(F32)
                    ).astype(BF)

                row_loop(high[a] // 2, 16, add)
                send(a, 4 + part, fwd[a].at[part], r2[a].at[part], (seq, offset(k)))

    def s2(a):
        c, low = wide[a], high[a] // 2
        if nd == 8:
            for slot in (0, 2, 4, 5):
                held[a, slot].wait_recv()
        else:
            for kc in range(1, ncol):
                held[a, kc].wait_recv()

        def total(part, t, cs):
            if nd == 8:
                return (
                    own[a][pl.ds(part * low + t, 16), cs].astype(F32)
                    + r1[a][2 * part, pl.ds(t, 16), cs].astype(F32)
                    + r2[a][part, pl.ds(t, 16), cs].astype(F32)
                )
            value = own[a][pl.ds(part * low + t, 16), cs].astype(F32)
            for kc in range(1, ncol):
                value = value + r1[a][kc - 1, pl.ds(part * low + t, 16), cs].astype(F32)
            return value

        for part in range(2):

            def add(t, part=part):
                cut = pl.ds(part * low + t, 16)
                if a == 3:
                    tot[cut, :] = total(part, t, slice(None)).astype(BF)
                else:
                    keep[a][cut, :] = total(part, t, lanes(nearb * (c // 2), c // 2))
                    ns_st[a][cut, :] = total(part, t, lanes((1 - nearb) * (c // 2), c // 2)).astype(BF)

            row_loop(low, 16, add)
        if a == 3:
            send(a, 6, tot, far_in, far_to)
        else:
            send(a, 6, ns_st[a], ns_rc[a], near_to)

    def s3(a):
        c = wide[a]
        held[a, 6].wait_recv()
        if a == 3:

            def add(t):
                cut = pl.ds(t, 16)
                tot2[cut, :] = (tot[cut, :].astype(F32) + far_in[cut, :].astype(F32)).astype(BF)

            row_loop(high[a], 16, add)
            send(a, 7, tot2, near_in, near_to)
            return

        def add(t):
            cut, cs = pl.ds(t, 16), lanes((1 - half) * (c // 4), c // 4)
            fs_st[a][cut, :] = (keep[a][cut, cs] + ns_rc[a][cut, cs].astype(F32)).astype(BF)

        row_loop(high[a], 16, add)
        send(a, 7, fs_st[a], fs_rc[a], far_to)

    def s4(a):
        c = wide[a]
        held[a, 7].wait_recv()
        low = high[a] // 2
        theirs = pl.ds(pl.multiple_of((1 - core) * low, low), low)
        if a == 3:
            send(a, 8, tot2.at[theirs], core_in.at[0], core_to)
            send(a, 9, near_in.at[theirs], core_in.at[1], core_to)
            return
        place = lanes(nearb * (c // 2) + half * (c // 4), c // 4)

        def add(t):
            cut, cs = pl.ds(t, 16), lanes(half * (c // 4), c // 4)
            value = keep[a][cut, cs] + ns_rc[a][cut, cs].astype(F32) + fs_rc[a][cut, :].astype(F32)
            fb[a][cut, place] = value.astype(BF)

        row_loop(high[a], 16, add)
        send(a, 8, fb[a].at[:, place], fb[a].at[:, place], far_to)

    def s5(a):
        c = wide[a]
        held[a, 8].wait_recv()
        low = high[a] // 2
        ours = pl.ds(pl.multiple_of(core * low, low), low)
        if a == 3:
            held[a, 9].wait_recv()
            for which, value in (
                (member, tot2[ours, :]), (beside, near_in[ours, :]), (twin, core_in[0]), (across, core_in[1])
            ):
                for i in range(3):
                    insum[:, lanes(i * width + which * group, group)] = value[:, i * group : (i + 1) * group]
            return
        place = lanes(nearb * (c // 2), c // 2)
        send(a, 9, fb[a].at[:, place], fb[a].at[:, place], near_to)

    def s6(a):
        held[a, 9].wait_recv()
        low = high[a] // 2
        theirs = pl.ds(pl.multiple_of((1 - core) * low, low), low)
        if a == 0:
            c = pltpu.make_async_copy(fb[a], rsum, a_l.at[a, 3])
            c.start()
            held[a, "last"] = c
        else:
            send(a, 10, fb[a].at[theirs], eb[a], core_to)

    def s7(a):
        if a == 0:
            held[a, "last"].wait()
            return
        held[a, 10].wait_recv()
        low = high[a] // 2
        ours = pl.ds(pl.multiple_of(core * low, low), low)
        if a == 2:
            size = wide[a]
            osum[:, lanes(core * size, size)] = fb[a][ours, :]
            osum[:, lanes((1 - core) * size, size)] = eb[a][...]
        else:
            size = wide[a] // ncol
            for i in range(ncol):
                cs = slice(i * size, (i + 1) * size)
                a0, a1 = fb[a][ours, cs], eb[a][:, cs]
                esum[:, 2 * i * size : (2 * i + 1) * size] = jnp.where(core == 0, a0, a1)
                esum[:, (2 * i + 1) * size : (2 * i + 2) * size] = jnp.where(core == 0, a1, a0)

    for a in range(3):
        s0(a)
    out_remote = rcopy(res, out, out_s, out_r, swap_to)
    out_local = pltpu.make_async_copy(res, out, out_l)

    @pl.when(jnp.logical_not(stays))
    def _():
        out_remote.start()

    @pl.when(stays)
    def _():
        out_local.start()

    w, scale = 2 * d, d**-0.5
    for i in range(4):
        cut = slice(i * n_rows, (i + 1) * n_rows)
        qt[:, cut] = jnp.transpose(qkv[cut, :group])
        kt[:, cut] = jnp.transpose(qkv[cut, group : 2 * group])
    dqt[...] = jnp.zeros_like(dqt)
    for i in range(4):
        cut = slice(i * n_rows, (i + 1) * n_rows)
        landing = go.at[pl.ds(i * n_rows, n_rows)]
        arrival = pltpu.make_async_copy(landing, landing, move_r.at[i])
        r, stay = moves[i]

        @pl.when(member != i)
        def _(r=r, arrival=arrival):
            arrival.wait()
            r.wait_send()

        @pl.when(member == i)
        def _(stay=stay):
            stay.wait()

    for i in range(4):
        cut = slice(i * n_rows, (i + 1) * n_rows)
        dot[:, cut] = jnp.transpose(go[cut, :])
        prod = jnp.transpose(go[cut, :].astype(F32) * att[cut, :].astype(F32))
        for h in range(heads):
            delta[h // 2, h % 2 : h % 2 + 1, cut] = jnp.sum(prod[h * d : (h + 1) * d], axis=0, keepdims=True)

    zero = jnp.zeros((), BF)
    for j in range(0, n, bk):

        def pair(p, carry, j=j):
            at = lambda first: pl.ds(pl.multiple_of(first + p * w, w), w)
            kb, vb = qkv[j : j + bk, at(group)], qkv[j : j + bk, at(2 * group)]
            dk = jnp.zeros((bk, w), F32)
            dv = jnp.zeros((bk, w), F32)
            row = lax.broadcasted_iota(jnp.int32, (w, bq), 0)
            lane = lax.broadcasted_iota(jnp.int32, (bq, w), 1)
            for i in range(j // bq, n // bq):
                cs = slice(i * bq, (i + 1) * bq)
                key = lax.broadcasted_iota(jnp.int32, (bk, bq), 0) + j
                ok = key >= st[:, cs]
                if j + bk > i * bq:
                    ok = ok & (key <= lax.broadcasted_iota(jnp.int32, (bk, bq), 1) + i * bq)
                for h in range(2):
                    rows_h = (row >= h * d) & (row < (h + 1) * d)
                    lanes_h = (lane >= h * d) & (lane < (h + 1) * d)
                    s = _dot(kb, jnp.where(rows_h, qt[at(0), cs], zero), 1, 0) * scale
                    s = jnp.where(ok, s, NEG)
                    e = jnp.exp(s - lse[p, h : h + 1, cs])
                    dp = _dot(vb, jnp.where(rows_h, dot[at(0), cs], zero), 1, 0)
                    ds = (e * (dp - delta[p, h : h + 1, cs])).astype(BF)
                    dv = dv + _dot(e.astype(BF), jnp.where(lanes_h, go[cs, at(0)], zero), 1, 0)
                    dk = dk + _dot(ds, jnp.where(lanes_h, qkv[cs, at(0)], zero), 1, 0)
                    head = pl.ds(pl.multiple_of(p * w + h * d, d), d)
                    dqt[head, cs] += _dot(kt[head, j : j + bk], ds, 1, 0)
            gm[j : j + bk, at(group)] = (dk * scale).astype(BF)
            gm[j : j + bk, at(2 * group)] = dv.astype(BF)
            return carry

        lax.fori_loop(0, heads // 2, pair, 0)
        if j == 0:
            s1(0)
        elif j == bk:
            s2(0)
        elif j == 2 * bk:
            s3(0)
    for i in range(4):
        cut = slice(i * n_rows, (i + 1) * n_rows)
        gm[cut, :group] = (jnp.transpose(dqt[:, cut]) * scale).astype(BF)

    step = n_rows // chunks

    def term(b, c):
        cut = pl.ds(pl.multiple_of(b * n_rows + c * step, step), step)
        return _dot(gm[cut, :], wf[...], 1, 1)

    quad = {}

    def quad_send(slot, src, dst, dev):
        c = rcopy(src, dst, d_s.at[slot], d_r.at[slot], dev)
        c.start()
        quad[slot] = c
        sends.append(c)

    for which, b in ((1, across), (0, twin)):
        for c in range(chunks):
            cut = pl.ds(c * step, step)
            cst[which, cut, :] = term(b, c).astype(BF)
            quad_send(which * chunks + c, cst.at[which, cut], crc.at[which, cut], core_to)
    for c in range(chunks):
        cut = pl.ds(c * step, step)
        value = term(beside, c)
        quad[chunks + c].wait_recv()
        nst[cut, :] = (value + crc[1, cut, :].astype(F32)).astype(BF)
        quad_send(2 * chunks + c, nst.at[cut], nrc.at[cut], near_to)

    s1(1)
    s1(2)
    s4(0)
    for i in range(4):
        cut = slice(i * group, (i + 1) * group)
        zin[cut, :] = _dot(n1t[cut, :], gm[...], 1, 0).astype(BF)
    s0(3)
    s5(0)

    tg_remote, tg_local = [], []
    gain_sum = jnp.zeros((1, width), F32)
    shift_sum = jnp.zeros((1, width), F32)
    for c in range(chunks):
        cut = pl.ds(c * step, step)
        value = term(member, c)
        quad[c].wait_recv()
        quad[2 * chunks + c].wait_recv()
        dy = value + crc[0, cut, :].astype(F32) + nrc[cut, :].astype(F32)
        rows_in = x[cut, :].astype(F32)
        center = rows_in - jnp.mean(rows_in, axis=-1, keepdims=True)
        rstd = lax.rsqrt(jnp.mean(center * center, axis=-1, keepdims=True) + EPS)
        hat = center * rstd
        gain_sum = gain_sum + jnp.sum(dy * hat, axis=0, keepdims=True)
        shift_sum = shift_sum + jnp.sum(dy, axis=0, keepdims=True)
        dh = dy * gain[...]
        inner = dh - jnp.mean(dh, axis=-1, keepdims=True) - hat * jnp.mean(dh * hat, axis=-1, keepdims=True)
        tgs[cut, :] = (gres[cut, :] + rstd * inner).astype(BF)
        r = rcopy(tgs.at[cut], tg.at[cut], tg_s.at[c], tg_r.at[c], swap_to)
        stay = pltpu.make_async_copy(tgs.at[cut], tg.at[cut], tg_l.at[c])
        tg_remote.append(r)
        tg_local.append(stay)

        @pl.when(jnp.logical_not(stays))
        def _(r=r):
            r.start()

        @pl.when(stays)
        def _(stay=stay):
            stay.start()

    small = v_in.shape[2]
    for k in range(nd):
        vmine[k] = v_in[k]
        vmine[k, 0:1, :] = gain_sum[:, k * small : (k + 1) * small]
        vmine[k, 1:2, :] = shift_sum[:, k * small : (k + 1) * small]
    vec = []
    for k in range(1, nd):
        c = rcopy(vmine.at[offset(k)], vrc.at[k], v_s.at[k], v_r.at[k], (seq, offset(k)))
        c.start()
        vec.append(c)
        sends.append(c)

    s2(1)
    s2(2)
    s6(0)
    s1(3)
    total = vmine[me]
    for k, c in enumerate(vec):
        c.wait_recv()
        total = total + vrc[k + 1]
    vz[seq] = total
    z_copies = []
    for i, dev in enumerate((near_to, far_to, third_to)):
        c = rcopy(vz.at[seq], vz.at[seq], vz_s.at[i], vz_r.at[i], dev)
        c.start()
        z_copies.append(c)
        sends.append(c)
    s3(1)
    s3(2)
    s2(3)
    s4(1)
    s4(2)
    s3(3)
    s5(1)
    s5(2)
    s4(3)
    s6(1)
    s6(2)
    s5(3)
    for c in z_copies:
        c.wait_recv()
    total = vz[0]
    for i in range(1, ns):
        total = total + vz[i]
    vout[...] = total
    for a in range(3):
        s7(a)

    @pl.when(jnp.logical_not(stays))
    def _():
        out_remote.wait()
        for c in tg_remote:
            c.wait()

    @pl.when(stays)
    def _():
        out_local.wait()
        for c in tg_local:
            c.wait()

    for c in sends:
        c.wait_send()


def back(ga, qkv, att, lse, starts, n1t, wf, x, gres, gain, v_in, res, dwr, dwe, dwo, ns, nd, heads, d):
    n_rows, width = x.shape
    n, group, ncol, chunks = n_rows * ns, width // 4, nd // 2, 4
    any_, vmem = pl.BlockSpec(memory_space=pl.ANY), pl.BlockSpec(memory_space=pltpu.VMEM)
    dma = lambda *shape: pltpu.SemaphoreType.DMA(shape)
    one = pltpu.SemaphoreType.DMA
    sds = jax.ShapeDtypeStruct
    sizes = [(t.shape[0] // ncol, t.shape[1]) for t in (dwr, dwe, dwo)] + [(width // ncol, 3 * group)]
    vm = lambda dtype, *shape: pltpu.VMEM(shape, dtype)
    slots = max(11, nd)
    rr, cc = width // nd, 3 * group
    return pl.pallas_call(
        functools.partial(back_kernel, ns=ns, nd=nd, heads=heads, d=d, bq=n_rows // 2, bk=n_rows, chunks=chunks),
        in_specs=[vmem] * 11 + [any_] * 4,
        out_specs=[any_, any_, vmem, vmem, vmem, any_, vmem],
        out_shape=[
            sds(x.shape, BF), sds(x.shape, BF), sds((rr, 3 * width), BF), sds((rr, width), BF),
            sds((rr, 2 * dwe.shape[1]), BF), sds(sizes[0], BF), sds(v_in.shape[1:], F32),
        ],
        scratch_shapes=[
            vm(BF, n, group), vm(BF, group, n), vm(BF, group, n), vm(BF, group, n), vm(F32, group, n),
            vm(F32, heads // 2, 2, n), vm(BF, n, 3 * group), vm(BF, width, 3 * group),
            vm(BF, 2 * rr, cc), vm(BF, 2 * rr, cc), vm(BF, 2 * rr, cc), vm(BF, 2 * rr, cc), vm(BF, 2, rr, cc),
            vm(BF, 2, n_rows, width), vm(BF, 2, n_rows, width), vm(BF, n_rows, width), vm(BF, n_rows, width),
            vm(BF, n_rows, width), vm(F32, *v_in.shape), vm(F32, *v_in.shape), vm(F32, ns, *v_in.shape[1:]),
            [vm(BF, r, c) for r, c in sizes],
            [vm(BF, 2, r // 2, c) for r, c in sizes],
            [vm(BF, 4, r // 2, c) if nd == 8 else vm(BF, ncol - 1, r, c) for r, c in sizes],
            [vm(BF, 2, r // 2, c) for r, c in sizes],
            [vm(BF, r, c // 2) for r, c in sizes[:3]], [vm(BF, r, c // 2) for r, c in sizes[:3]],
            [vm(F32, r, c // 2) for r, c in sizes[:3]],
            [vm(BF, r, c // 4) for r, c in sizes[:3]], [vm(BF, r, c // 4) for r, c in sizes[:3]],
            [vm(BF, r, c) for r, c in sizes[:3]], [vm(BF, r // 2, c) for r, c in sizes[:3]],
            dma(4), dma(4), one, dma(4, slots), dma(4, slots), dma(4, 4),
            dma(3 * chunks), dma(3 * chunks), one, one, one, dma(chunks), dma(chunks), dma(chunks),
            dma(nd), dma(nd), dma(3), dma(3),
        ],
        compiler_params=pltpu.CompilerParams(
            collective_id=1, has_side_effects=True, vmem_limit_bytes=60 << 20
        ),
        cost_estimate=pl.CostEstimate(
            flops=20 * n * n * d * heads, bytes_accessed=60_000_000, transcendentals=n * n * heads
        ),
    )(ga, qkv, att, lse, starts, n1t, wf, x, gres, gain, v_in, res, dwr, dwe, dwo)


def layer_normalize(values, gain, shift):
    center = values - jnp.mean(values, axis=-1, keepdims=True)
    spread = jnp.mean(center * center, axis=-1, keepdims=True)
    return center * lax.rsqrt(spread + EPS) * gain + shift


def smooth_gate(values):
    return jax.nn.gelu(values, approximate=True)


def rows(array, start, size):
    return lax.dynamic_slice_in_dim(array, start, size, 0)


def cols(array, start, size):
    return lax.dynamic_slice_in_dim(array, start, size, 1)


def put(array, piece, row, col):
    return lax.dynamic_update_slice(array, piece, (row, col))


def bf_round(x):
    return lax.reduce_precision(x, 8, 7)


class Links:
    def __init__(self, ns, nd):
        self.ns, self.nd = ns, nd

    def go(self, array, target):
        pairs = []
        for s in range(self.ns):
            for d in range(self.nd):
                ts, td = target(s, d)
                pairs.append((s * self.nd + d, ts * self.nd + td))
        return lax.ppermute(array, ("seq", "dp"), pairs)

    def dp(self, array, k):
        return self.go(array, lambda s, d: (s, d ^ k))

    def core(self, array):
        return self.dp(array, 1)

    def near(self, array):
        return self.go(array, lambda s, d: (s ^ 1, d))

    def far(self, array):
        return self.go(array, lambda s, d: (s ^ 2, d))

    def both(self, array):
        return self.go(array, lambda s, d: (s ^ 1, d ^ 1))

    def swap(self, array):
        return self.go(array, lambda s, d: (2 * (d % 2) + s % 2, d - d % 2 + s // 2))


def on_device(
    tokens, lengths, cotangent, mixer_input, mixer_output, expand_weight, reduce_weight,
    first_gain, first_shift, second_gain, second_shift, output_bias, expand_bias, reduce_bias,
):
    ns, nd = lax.axis_size("seq"), lax.axis_size("dp")
    links = Links(ns, nd)
    seq, me = lax.axis_index("seq"), lax.axis_index("dp")
    half, near_bit, core = seq // 2, seq % 2, me % 2
    column = me // 2
    member = 2 * core + near_bit
    n_rows, width = tokens.shape[1:]
    slots = n_rows * ns
    head_dim = width // HEADS
    hidden = reduce_weight.shape[0] * nd
    group = width // 4
    my_heads = HEADS // 4

    lengths_row = jnp.where(half == core, lengths[0], links.core(lengths)[0])
    entry = jnp.arange(lengths_row.shape[0])
    ends = jnp.sum(jnp.where(entry[None, :] <= entry[:, None], lengths_row[None, :], 0), axis=1)
    place = jnp.arange(slots, dtype=jnp.int32)
    passed = place[:, None] >= ends[None, :]
    starts = jnp.max(jnp.where(passed, ends[None, :], 0), axis=1)
    starts = jnp.where(place < ends[-1], starts, place).reshape(1, slots)
    live = (member * n_rows + jnp.arange(n_rows, dtype=jnp.int32) < ends[-1]).astype(F32)

    small, small_rows = width // nd, mixer_input.shape[0]
    wide = hidden // nd
    vectors = jnp.concatenate(
        [first_gain, first_shift, second_gain, second_shift, output_bias, reduce_bias, expand_bias]
    ).reshape(-1, small)
    vectors = jnp.concatenate([vectors, jnp.zeros((-vectors.shape[0] % 16, small), BF)])
    by_core = expand_weight.reshape(small_rows, nd // 2, 2, wide).transpose(2, 0, 1, 3)
    by_core = by_core.reshape(2, small_rows, hidden // 2)
    (
        x_low, grad_low, twin_grad, normed_t, input_full, output_full, expand_half, reduce_half, vectors,
        qkv, attended, logsum, attention,
    ) = front(
        tokens[0], cotangent[0], mixer_input, mixer_output, by_core, reduce_weight, vectors,
        starts, ns, nd, my_heads, head_dim,
    )
    twin_attention = links.core(attention)
    vectors = vectors.astype(F32)
    gain_one, _, gain_two, shift_two, output_add, reduce_add = (vectors[:, i].reshape(-1) for i in range(6))
    n_wide = wide // small
    expand_add = vectors[:, 6 : 6 + n_wide].reshape(nd // 2, 2, wide)
    expand_add = lax.dynamic_index_in_dim(expand_add, core, 1, keepdims=False).reshape(-1)

    inputs = x_low.astype(F32)
    resid = inputs + mm(attention, output_full) + output_add
    normed_two = layer_normalize(resid, gain_two, shift_two).astype(BF)
    normed_two = jnp.concatenate([normed_two, links.core(normed_two)])
    expanded = mm(normed_two, expand_half) + expand_add
    active = smooth_gate(expanded).astype(BF)
    reduced = mm(active, reduce_half)
    twin_part = links.core(reduced[n_rows:].astype(BF)).astype(F32)
    result = (resid + reduced[:n_rows] + twin_part + reduce_add).astype(BF)

    twin_live = ((member ^ 2) * n_rows + jnp.arange(n_rows, dtype=jnp.int32) < ends[-1]).astype(F32)
    grad_result = grad_low.astype(F32) * live[:, None]
    result_low = jnp.concatenate([grad_result.astype(BF), (twin_grad.astype(F32) * twin_live[:, None]).astype(BF)])
    reduce_term = mm_left(active, result_low).astype(BF)
    reduce_bias_sum = jnp.sum(grad_result, axis=0)
    grad_active = mm_right(result_low, reduce_half)
    _, gate_back = jax.vjp(smooth_gate, expanded)
    grad_expanded = gate_back(grad_active)[0]
    expand_bias_sum = jnp.sum(grad_expanded, axis=0)
    expanded_low = grad_expanded.astype(BF)
    expand_term = mm_left(normed_two, expanded_low).astype(BF)
    grad_normed = mm_right(expanded_low, expand_half)
    grad_normed_two = grad_normed[:n_rows] + links.core(grad_normed[n_rows:].astype(BF)).astype(F32)
    _, second_back = jax.vjp(layer_normalize, resid, gain_two, shift_two)
    resid_part, gain_two_sum, shift_two_sum = second_back(grad_normed_two)
    grad_resid = grad_result + resid_part
    output_bias_sum = jnp.sum(grad_resid, axis=0)
    resid_low = grad_resid.astype(BF)
    grad_attention = mm_right(resid_low, output_full).astype(BF)
    both_low = jnp.concatenate([resid_low, links.core(resid_low)])
    both_low = cols(both_low, core * (width // 2), width // 2)
    output_term = mm_left(jnp.concatenate([attention, twin_attention]), both_low).astype(BF)

    sums = jnp.stack([gain_two_sum, shift_two_sum, output_bias_sum, reduce_bias_sum])
    sums = sums.reshape(4, nd, small).transpose(1, 0, 2)
    wide_sum = expand_bias_sum.reshape(nd // 2, 1, n_wide, small)
    parity = jnp.arange(2).reshape(1, 2, 1, 1)
    wide_sum = jnp.where(parity == core, wide_sum, 0.0).reshape(nd, n_wide, small)
    pad = -(6 + n_wide) % 8
    sums = jnp.concatenate([jnp.zeros((nd, 2, small)), sums, wide_sum, jnp.zeros((nd, pad, small))], axis=1)

    layer_output, tokens_gradient, input_sum, output_sum, expand_sum, reduce_sum, sums = back(
        grad_attention, qkv, attended, logsum, starts, normed_t, input_full, x_low, grad_resid,
        gain_one.reshape(1, width), sums, result, reduce_term, expand_term, output_term,
        ns, nd, my_heads, head_dim,
    )
    return (
        layer_output[None],
        tokens_gradient.astype(F32)[None],
        input_sum.astype(F32),
        output_sum.astype(F32),
        expand_sum.astype(F32),
        reduce_sum.astype(F32),
        sums[0],
        sums[1],
        sums[2],
        sums[3],
        sums[4],
        sums[6 : 6 + n_wide].reshape(-1),
        sums[5],
    )


def solution(mesh):
    row, vec = P("dp", None), P("dp")
    act = P("dp", "seq", None)
    return jax.shard_map(
        on_device,
        mesh=mesh,
        in_specs=(act, row, act, row, row, row, row, vec, vec, vec, vec, vec, vec, vec),
        out_specs=(act, act, row, row, row, row, vec, vec, vec, vec, vec, vec, vec),
        check_vma=False,
    )
```

```python
import functools

import jax
import jax.numpy as jnp
from jax import lax
from jax.experimental import pallas as pl
from jax.experimental.pallas import tpu as pltpu
from jax.sharding import PartitionSpec as P

HEADS = 16
EPS = 1e-05
NEG = -1e30
F32 = jnp.float32
BF = jnp.bfloat16


def _dot(a, b, ca, cb):
    return lax.dot_general(a, b, (((ca,), (cb,)), ((), ())), preferred_element_type=F32)


def mm(a, b):
    return _dot(a, b, 1, 0)


def mm_left(a, b):
    return _dot(a, b, 0, 0)


def mm_right(a, b):
    return _dot(a, b, 1, 1)


MESH = pl.DeviceIdType.MESH


def front_kernel(
    tok, cot, win, wo, we, wr, vec, st,
    x_ref, g_ref, gp_ref, n1t, wf, wof, wef, wrf, vecs, qkv, att, lse, attn,
    n1, qt, vt, win_s, win_r, vec_s, vec_r, tok_s, tok_r, tok_l, near_s, near_r, core_s, core_r, fwd_s, fwd_r,
    cot_s, cot_r, cot_l, gp_s, gp_r, own_l, w_s, w_r, move_s, move_r, move_l,
    *, ns, nd, heads, d, bq, bk, chunks,
):
    seq, me = lax.axis_index("seq"), lax.axis_index("dp")
    half, nearb, core = seq // 2, seq % 2, me % 2
    member = 2 * core + nearb
    n_rows, width = tok.shape
    group = width // 4
    small_rows = win.shape[0]
    stays = half == core
    swap_to = (2 * core + nearb, me - core + half)
    near_to = (seq + 1 - 2 * nearb, me)
    core_to = (seq, me + 1 - 2 * core)

    def offset(k):
        out = me
        bit = 1
        while bit <= k:
            if k & bit:
                out = out + bit - 2 * bit * ((me // bit) % 2)
            bit *= 2
        return out

    def rcopy(src, dst, ss, rs, dev):
        return pltpu.make_async_remote_copy(
            src_ref=src, dst_ref=dst, send_sem=ss, recv_sem=rs, device_id=dev, device_id_type=MESH
        )

    barrier = pltpu.get_barrier_semaphore()

    def hello(dev):
        pl.semaphore_signal(barrier, inc=1, device_id=dev, device_id_type=MESH)

    for k in range(1, nd):
        hello((seq, offset(k)))
    hello(near_to)
    hello((near_to[0], core_to[1]))

    @pl.when(jnp.logical_not(stays))
    def _():
        hello(swap_to)
        pl.semaphore_wait(barrier, nd + 2)

    @pl.when(stays)
    def _():
        pl.semaphore_wait(barrier, nd + 1)

    sends = []

    step = n_rows // chunks
    tok_remote, tok_local = [], []
    for c in range(chunks):
        cut = pl.ds(c * step, step)
        tok_remote.append(rcopy(tok.at[cut], x_ref.at[cut], tok_s.at[c], tok_r.at[c], swap_to))
        tok_local.append(pltpu.make_async_copy(tok.at[cut], x_ref.at[cut], tok_l.at[c]))

    @pl.when(jnp.logical_not(stays))
    def _():
        for c in tok_remote:
            c.start()

    @pl.when(stays)
    def _():
        for c in tok_local:
            c.start()

    vec_copies, win_copies, own_copies = [], [], []
    for k in range(1, nd):
        c = rcopy(vec, vecs.at[me], vec_s.at[k], vec_r.at[k], (seq, offset(k)))
        c.start()
        vec_copies.append(c)
    c = pltpu.make_async_copy(vec, vecs.at[me], own_l.at[0])
    c.start()
    vec_copies.append(c)
    my_rows = pl.ds(pl.multiple_of(me * small_rows, small_rows), small_rows)
    for k in range(nd):
        target = 2 * (core if k % 2 == 0 else 1 - core) + nearb
        for i in range(3):
            src = win.at[:, pl.ds(pl.multiple_of(i * width + target * group, 128), group)]
            dst = wf.at[my_rows, pl.ds(i * group, group)]
            if k == 0:
                c = pltpu.make_async_copy(src, dst, own_l.at[1 + i])
            else:
                c = rcopy(src, dst, win_s.at[k, i], win_r.at[k, i], (seq, offset(k)))
            c.start()
            win_copies.append(c)

    pairs = ((wo, wof), (we, wef), (wr, wrf))

    def source(a, k):
        return we.at[core if k % 2 == 0 else 1 - core] if a == 1 else pairs[a][0]

    def at(a, k, part=None):
        high = pairs[a][0].shape[-2]
        row = (offset(k) // 2 if a == 2 else offset(k)) * high
        if part is None:
            return pairs[a][1].at[pl.ds(pl.multiple_of(row, high), high)]
        return pairs[a][1].at[pl.ds(pl.multiple_of(row + part * (high // 2), high // 2), high // 2)]

    held = {}

    def send(a, slot, src, dst, k):
        c = rcopy(src, dst, w_s.at[a, slot], w_r.at[a, slot], (seq, offset(k)))
        c.start()
        held[a, slot] = c

    direct = (2, 3, 4, 5) if nd == 8 else range(2, nd)

    def weights_start(a):
        for k in direct:
            if k % 2 == 0 or a == 1:
                send(a, k, source(a, k), at(a, 0), k)
        if a < 2:
            send(a, 1, source(a, 1), at(a, 0), 1)
        c = pltpu.make_async_copy(source(a, 0), at(a, 0), own_l.at[4 + a])
        c.start()
        held[a, "own"] = c

    def weights_forward(a):
        for k in direct:
            if k % 2 == 0 or a == 1:
                held[a, k].wait_recv()
                if nd == 8:
                    send(a, 8 + k, at(a, k, k // 4), at(a, k, k // 4), 6 - k // 2 * 2)
                if a == 0:
                    send(a, k + 1 if nd > 8 else 14 + k // 2, at(a, k), at(a, k), 1)

    def weights_last(a):
        if nd == 8 and a == 0:
            for part, k in ((0, 2), (1, 4)):
                held[a, 8 + k].wait_recv()
                send(a, 3 + 2 * part, at(a, 6, part), at(a, 6, part), 1)

    def weights_end(a):
        held[a, "own"].wait()
        waited = set(direct) if a else {k for k in direct if k % 2 == 0}
        if nd == 8 and a == 0:
            waited |= {10, 12}
        for (b, slot), c in held.items():
            if b == a and slot != "own":
                if slot not in waited:
                    c.wait_recv()
                c.wait_send()

    for c in vec_copies[:-1]:
        c.wait_recv()
        sends.append(c)
    vec_copies[-1].wait()

    def vector(i):
        return jnp.concatenate([vecs[k, i : i + 1, :] for k in range(nd)], axis=1).astype(F32)

    gain, shift = vector(0), vector(1)
    near_copies, core_copies = [], []
    for c in range(chunks):
        cut = pl.ds(c * step, step)

        @pl.when(jnp.logical_not(stays))
        def _(c=c):
            tok_remote[c].wait_recv()

        @pl.when(stays)
        def _(c=c):
            tok_local[c].wait()

        value = x_ref[cut, :].astype(F32)
        center = value - jnp.mean(value, axis=-1, keepdims=True)
        spread = jnp.mean(center * center, axis=-1, keepdims=True)
        place = pl.ds(pl.multiple_of(member * n_rows + c * step, step), step)
        n1[place, :] = (center * lax.rsqrt(spread + EPS) * gain + shift).astype(BF)
        r = rcopy(n1.at[place], n1.at[place], near_s.at[c], near_r.at[c], near_to)
        r.start()
        near_copies.append(r)
        r = rcopy(n1.at[place], n1.at[place], core_s.at[c], core_r.at[c], core_to)
        r.start()
        core_copies.append(r)

    for c in win_copies[:3]:
        c.wait()
    for c in win_copies[3:]:
        c.wait_recv()
        sends.append(c)
    arrays = (0, 1) if nd == 8 else (0, 1, 2)
    for a in arrays:
        weights_start(a)

    def project(block, c=None):
        size = n_rows if c is None else step
        place = pl.ds(pl.multiple_of(block * n_rows + (0 if c is None else c * step), size), size)
        mixed = _dot(n1[place, :], wf[...], 1, 0).astype(BF)
        qkv[place, :] = mixed
        n1t[:, place] = jnp.transpose(n1[place, :])
        qt[:, place] = jnp.transpose(mixed[:, :group])
        vt[:, place] = jnp.transpose(mixed[:, 2 * group :])

    project(member)
    for c in core_copies:
        c.wait_recv()
        sends.append(c)
    twin = 2 * (1 - core) + nearb
    project(twin)
    fwd_copies = []
    beside = 2 * core + 1 - nearb
    across = 2 * (1 - core) + 1 - nearb
    for c in range(chunks):
        near_copies[c].wait_recv()
        sends.append(near_copies[c])
        place = pl.ds(pl.multiple_of(beside * n_rows + c * step, step), step)
        r = rcopy(n1.at[place], n1.at[place], fwd_s.at[c], fwd_r.at[c], core_to)
        r.start()
        fwd_copies.append(r)
    project(beside)
    for c in fwd_copies:
        c.wait_recv()
        sends.append(c)
    project(across)

    cot_remote = rcopy(cot, g_ref, cot_s, cot_r, swap_to)
    cot_local = pltpu.make_async_copy(cot, g_ref, cot_l)

    @pl.when(jnp.logical_not(stays))
    def _():
        cot_remote.start()

    @pl.when(stays)
    def _():
        cot_local.start()

    n = ns * n_rows
    scale = d**-0.5
    w = 2 * d
    moves = []
    for i in range(n // bq):
        cs = slice(i * bq, (i + 1) * bq)

        def pair(p, carry, i=i, cs=cs):
            lanes = pl.ds(pl.multiple_of(p * w, w), w)
            key_lanes = pl.ds(pl.multiple_of(group + p * w, w), w)
            outs = []
            for h in range(2):
                row = lax.broadcasted_iota(jnp.int32, (w, bq), 0)
                qm = jnp.where((row >= h * d) & (row < (h + 1) * d), qt[lanes, cs], jnp.zeros((), BF))
                m = jnp.full((1, bq), NEG, F32)
                l = jnp.zeros((1, bq), F32)
                acc = jnp.zeros((d, bq), F32)
                for j in range(0, (i + 1) * bq, bk):
                    s = _dot(qkv[j : j + bk, key_lanes], qm, 1, 0) * scale
                    key = lax.broadcasted_iota(jnp.int32, (bk, bq), 0) + j
                    ok = key >= st[:, cs]
                    if j + bk > i * bq:
                        ok = ok & (key <= lax.broadcasted_iota(jnp.int32, (bk, bq), 1) + i * bq)
                    s = jnp.where(ok, s, NEG)
                    mn = jnp.maximum(m, jnp.max(s, axis=0, keepdims=True))
                    e = jnp.exp(s - mn)
                    a = jnp.exp(m - mn)
                    l = a * l + jnp.sum(e, axis=0, keepdims=True)
                    rows_h = pl.ds(pl.multiple_of(p * w + h * d, d), d)
                    acc = a * acc + _dot(vt[rows_h, j : j + bk], e.astype(BF), 1, 0)
                    m = mn
                outs.append(acc / l)
                lse[p, h : h + 1, cs] = m + jnp.log(l)
            att[cs, lanes] = jnp.transpose(jnp.concatenate(outs, axis=0)).astype(BF)
            return carry

        lax.fori_loop(0, heads // 2, pair, 0)
        mine = attn.at[:, pl.ds(pl.multiple_of(member * group, group), group)]
        dev = (seq - nearb + i % 2, me - core + i // 2)
        r = rcopy(att.at[cs], mine, move_s.at[i], move_r.at[member], dev)
        keep = pltpu.make_async_copy(att.at[cs], mine, move_l)
        moves.append((r, keep))

        @pl.when(member != i)
        def _(r=r):
            r.start()

        @pl.when(member == i)
        def _(keep=keep):
            keep.start()

        if i in arrays:
            weights_forward(i)
    weights_last(0)

    @pl.when(jnp.logical_not(stays))
    def _():
        cot_remote.wait_recv()

    @pl.when(stays)
    def _():
        cot_local.wait()

    twin_cot = rcopy(g_ref, gp_ref, gp_s, gp_r, core_to)
    twin_cot.start()
    for a in arrays:
        weights_end(a)
    for i, (r, keep) in enumerate(moves):
        source = attn.at[:, pl.ds(i * group, group)]
        arrival = pltpu.make_async_copy(source, source, move_r.at[i])

        @pl.when(member != i)
        def _(r=r, arrival=arrival):
            r.wait_send()
            arrival.wait()

        @pl.when(member == i)
        def _(keep=keep):
            keep.wait()

    @pl.when(jnp.logical_not(stays))
    def _():
        cot_remote.wait_send()
        for c in tok_remote:
            c.wait_send()

    twin_cot.wait()
    for c in sends:
        c.wait_send()


def front(tok, cot, win, wo, we, wr, vec, starts, ns, nd, heads, d):
    n_rows, width = tok.shape
    n, group, chunks = n_rows * ns, width // 4, 4
    slots = 17 if nd == 8 else nd
    compact = lambda a: jax.ShapeDtypeStruct((a.shape[0] * (nd // 2), a.shape[1]), BF)
    any_, vmem = pl.BlockSpec(memory_space=pl.ANY), pl.BlockSpec(memory_space=pltpu.VMEM)
    full = lambda a: jax.ShapeDtypeStruct((a.shape[0] * nd, a.shape[1]), BF)
    dma = lambda *shape: pltpu.SemaphoreType.DMA(shape)
    sds = jax.ShapeDtypeStruct
    return pl.pallas_call(
        functools.partial(front_kernel, ns=ns, nd=nd, heads=heads, d=d, bq=n_rows, bk=n_rows, chunks=chunks),
        in_specs=[any_] * 7 + [vmem],
        out_specs=[vmem, any_, any_, vmem, vmem, any_, any_, any_, vmem, vmem, vmem, vmem, vmem],
        out_shape=[
            sds(tok.shape, BF), sds(tok.shape, BF), sds(tok.shape, BF), sds((width, n), BF), sds((width, 3 * group), BF),
            full(wo), sds((width, we.shape[2]), BF), sds((16, 128), BF) if nd == 8 else compact(wr), sds((nd, *vec.shape), BF), sds((n, 3 * group), BF),
            sds((n, group), BF), sds((heads // 2, 2, n), F32), sds(tok.shape, BF),
        ],
        scratch_shapes=[
            pltpu.VMEM((n, width), BF), pltpu.VMEM((group, n), BF), pltpu.VMEM((group, n), BF),
            dma(nd, 3), dma(nd, 3), dma(nd), dma(nd), dma(chunks), dma(chunks), dma(chunks),
            dma(chunks), dma(chunks), dma(chunks), dma(chunks), dma(chunks), dma(chunks),
            pltpu.SemaphoreType.DMA, pltpu.SemaphoreType.DMA, pltpu.SemaphoreType.DMA,
            pltpu.SemaphoreType.DMA, pltpu.SemaphoreType.DMA, dma(7), dma(3, slots), dma(3, slots), dma(4), dma(4), pltpu.SemaphoreType.DMA,
        ],
        compiler_params=pltpu.CompilerParams(
            collective_id=0, has_side_effects=True, vmem_limit_bytes=52 << 20
        ),
        cost_estimate=pl.CostEstimate(
            flops=8 * n * n * d * heads, bytes_accessed=60_000_000, transcendentals=n * n * heads
        ),
    )(tok, cot, win, wo, we, wr, vec, starts)


def middle_kernel(
    attn, wo, x, g, gp, weh, wr, vec, ebias, live,
    out, gres, ga, dwe, dwo, fw, vsum, esum,
    attb, wrh, resid, n2, tt, gl, expd, act, zw, r1, r2, stage, gr, xs_o, xr_o, xs_d, xr_d, xs_r,
    n2_s, n2_r, at_s, at_r, o_s, o_r, d_s, d_r, gr_s, gr_r, sw_s, sw_r, sw_l, w_s, w_r, w_l, a_s, a_r, g_l, dwe_l,
    *, nd,
):
    seq, me = lax.axis_index("seq"), lax.axis_index("dp")
    half, nearb, core = seq // 2, seq % 2, me % 2
    n_rows, width = x.shape
    both, block = 2 * n_rows, wr.shape[0]
    stays = half == core
    swap_to = (2 * core + nearb, me - core + half)
    core_to = (seq, me + 1 - 2 * core)
    column = me // 2
    x_to = (seq, me + 2 - 4 * (column % 2))
    y_to = (seq, me + 4 - 8 * (column // 2))

    def col(k):
        result = column
        if k & 1:
            result = result + 1 - 2 * (column % 2)
        if k & 2:
            result = result + 2 - 4 * (column // 2)
        return result

    def rcopy(src, dst, ss, rs, dev):
        return pltpu.make_async_remote_copy(
            src_ref=src, dst_ref=dst, send_sem=ss, recv_sem=rs, device_id=dev, device_id_type=MESH
        )

    def loop(total, size, body):
        def one(t, carry):
            body(pl.ds(pl.multiple_of(t * size, size), size))
            return carry

        lax.fori_loop(0, total // size, one, 0)

    barrier = pltpu.get_barrier_semaphore()

    def hello(dev):
        pl.semaphore_signal(barrier, inc=1, device_id=dev, device_id_type=MESH)

    for dev in (core_to, x_to, y_to):
        hello(dev)

    @pl.when(jnp.logical_not(stays))
    def _():
        hello(swap_to)
        pl.semaphore_wait(barrier, 4)

    @pl.when(stays)
    def _():
        pl.semaphore_wait(barrier, 3)

    sends = []

    def start(src, dst, ss, rs, dev):
        c = rcopy(src, dst, ss, rs, dev)
        c.start()
        sends.append(c)
        return c

    def owner(k, part=None):
        if part is None:
            return wrh.at[pl.ds(pl.multiple_of(col(k) * block, block), block)]
        low = block // 2
        return wrh.at[pl.ds(pl.multiple_of(col(k) * block + part * low, low), low)]

    w_x = start(wr, owner(0), w_s.at[0], w_r.at[0], x_to)
    w_y = start(wr, owner(0), w_s.at[1], w_r.at[1], y_to)
    w_own = pltpu.make_async_copy(wr, owner(0), w_l)
    w_own.start()
    at_copy = start(attn, attb, at_s, at_r, core_to)
    g_copies = [
        pltpu.make_async_copy(g, gl.at[pl.ds(0, n_rows)], g_l.at[0]),
        pltpu.make_async_copy(gp, gl.at[pl.ds(n_rows, n_rows)], g_l.at[1]),
    ]
    for c in g_copies:
        c.start()

    step = n_rows // 2
    cuts = [slice(c * step, (c + 1) * step) for c in range(2)]
    theirs = [slice(n_rows + c * step, n_rows + (c + 1) * step) for c in range(2)]
    gain, shift = vec[0:1, :], vec[1:2, :]
    n2_copies = []
    for c in range(2):
        cut = pl.ds(c * step, step)
        value = x[cut, :].astype(F32) + _dot(attn[cut, :], wo[...], 1, 0) + vec[2:3, :]
        resid[cut, :] = value
        center = value - jnp.mean(value, axis=-1, keepdims=True)
        spread = jnp.mean(center * center, axis=-1, keepdims=True)
        n2[cut, :] = (center * lax.rsqrt(spread + EPS) * gain + shift).astype(BF)
        n2_copies.append(
            start(n2.at[cut], n2.at[pl.ds(n_rows + c * step, step)], n2_s.at[c], n2_r.at[c], core_to)
        )
    for c in g_copies:
        c.wait()

    def mask(cut):
        gl[cut, :] = jnp.where(live[cut, :] > 0, gl[cut, :].astype(F32), 0.0).astype(BF)

    loop(both, 128, mask)
    for c in range(4):
        cut = slice(c * step, (c + 1) * step)
        tt[:, cut] = jnp.transpose(gl[cut, :])
    for c in n2_copies:
        c.wait_recv()

    part_copies = {}

    def part_send(slot, src, dst, dev):
        part_copies[slot] = start(src, dst, a_s.at[slot], a_r.at[slot], dev)

    upper, lower = pl.ds(0, width // 2), pl.ds(width // 2, width // 2)
    root, cubic = 0.7978845608028654, 0.044715
    for k in (3, 1, 2, 0):
        units = pl.ds(pl.multiple_of(col(k) * block, block), block)

        def expand(cut, k=k, units=units):
            u = _dot(n2[cut, :], weh[:, units], 1, 0) + ebias[:, units]
            expd[k, cut, :] = u
            t = jnp.tanh(root * (u + cubic * (u * u * u)))
            act[k, cut, :] = (0.5 * u * (1.0 + t)).astype(BF)

        loop(both, 256, expand)

        def reduce_grad(cut, k=k):
            zw[k, cut, :] = _dot(tt[cut, :], act[k], 1, 0).astype(BF)

        loop(width, 256, reduce_grad)
        if k == 3:
            part_send(1, zw.at[3, upper], r1.at[1], x_to)
            part_send(3, zw.at[3, lower], r1.at[3], y_to)
            w_x.wait_recv()
            w_fy = start(owner(1, 0), owner(1, 0), w_s.at[2], w_r.at[2], y_to)
            w_y.wait_recv()
            w_fx = start(owner(2, 1), owner(2, 1), w_s.at[3], w_r.at[3], x_to)
        elif k == 1:
            part_send(0, zw.at[1, upper], r1.at[0], x_to)
        elif k == 2:
            part_send(2, zw.at[2, lower], r1.at[2], y_to)

    for c in range(4):
        cut = slice(c * step, (c + 1) * step)
        tt[:, cut] = jnp.transpose(n2[cut, :])
    w_own.wait()
    w_fy.wait_recv()
    w_fx.wait_recv()

    def reduced(cut):
        value = _dot(act[0, cut, :], owner(0)[...], 1, 0)
        for k in range(1, 4):
            value = value + _dot(act[k, cut, :], owner(k)[...], 1, 0)
        return value

    o_copies = []
    for c in range(2):
        xs_o[cuts[c], :] = reduced(theirs[c]).astype(BF)
        cut = pl.ds(c * step, step)
        o_copies.append(start(xs_o.at[cut], xr_o.at[cut], o_s.at[c], o_r.at[c], core_to))
    swap_remote, swap_local = [], []
    for c in range(2):
        value = resid[cuts[c], :] + reduced(cuts[c]) + vec[3:4, :]
        o_copies[c].wait_recv()
        xs_r[cuts[c], :] = (value + xr_o[cuts[c], :].astype(F32)).astype(BF)
        cut = pl.ds(c * step, step)
        r = rcopy(xs_r.at[cut], out.at[cut], sw_s.at[c], sw_r.at[c], swap_to)
        stay = pltpu.make_async_copy(xs_r.at[cut], out.at[cut], sw_l.at[c])
        swap_remote.append(r)
        swap_local.append(stay)

        @pl.when(jnp.logical_not(stays))
        def _(r=r):
            r.start()

        @pl.when(stays)
        def _(stay=stay):
            stay.start()

    def forward(k, slot, first, index, dev):
        part_copies[slot].wait_recv()

        def add(cut):
            place = pl.ds(pl.multiple_of(cut.start + first, 128), 128)
            zw[k, place, :] = (zw[k, place, :].astype(F32) + r1[slot, cut, :].astype(F32)).astype(BF)

        loop(width // 2, 128, add)
        part_send(4 + index, zw.at[k, upper if first == 0 else lower], r2.at[index], dev)

    forward(2, 1, 0, 0, y_to)
    forward(1, 3, width // 2, 1, x_to)

    dwe_copies = []
    for i, k in enumerate((3, 1, 2, 0)):
        units = pl.ds(pl.multiple_of(col(k) * block, block), block)
        esum[:, units] = jnp.zeros((1, block), F32)

        def expand_back(cut, k=k, units=units):
            da = _dot(gl[cut, :], owner(k)[...], 1, 1)
            u = expd[k, cut, :]
            t = jnp.tanh(root * (u + cubic * (u * u * u)))
            slope = 0.5 * (1.0 + t) + 0.5 * u * (1.0 - t * t) * (root * (1.0 + 3.0 * cubic * (u * u)))
            da = da * slope
            esum[:, units] += jnp.sum(da, axis=0, keepdims=True)
            act[k, cut, :] = da.astype(BF)

        loop(both, 256, expand_back)
        if i >= 2:
            dwe_copies[i - 2].wait()

        def expand_grad(cut, k=k, i=i):
            stage[i % 2, cut, :] = _dot(tt[cut, :], act[k], 1, 0).astype(BF)

        loop(width, 256, expand_grad)
        c = pltpu.make_async_copy(stage.at[i % 2], dwe.at[:, units], dwe_l.at[i % 2])
        c.start()
        dwe_copies.append(c)

    def normed_grad(cut):
        value = None
        for k in range(4):
            units = pl.ds(pl.multiple_of(col(k) * block, block), block)
            one = _dot(act[k, cut, :], weh[:, units], 1, 1)
            value = one if value is None else value + one
        return value

    d_copies = []
    for c in range(2):
        xs_d[cuts[c], :] = normed_grad(theirs[c]).astype(BF)
        cut = pl.ds(c * step, step)
        d_copies.append(start(xs_d.at[cut], xr_d.at[cut], d_s.at[c], d_r.at[c], core_to))
    at_copy.wait_recv()
    for c in range(2):
        tt[:, cuts[c]] = jnp.transpose(attn[cuts[c], :])
        tt[:, theirs[c]] = jnp.transpose(attb[cuts[c], :])

    zero = jnp.zeros((1, width), F32)
    gain_sum, shift_sum, out_sum, red_sum = zero, zero, zero, zero
    gr_copies = []
    for c in range(2):
        dy = normed_grad(cuts[c])
        d_copies[c].wait_recv()
        dy = dy + xr_d[cuts[c], :].astype(F32)
        value = resid[cuts[c], :]
        center = value - jnp.mean(value, axis=-1, keepdims=True)
        rstd = lax.rsqrt(jnp.mean(center * center, axis=-1, keepdims=True) + EPS)
        hat = center * rstd
        gain_sum = gain_sum + jnp.sum(dy * hat, axis=0, keepdims=True)
        shift_sum = shift_sum + jnp.sum(dy, axis=0, keepdims=True)
        dh = dy * gain
        inner = dh - jnp.mean(dh, axis=-1, keepdims=True) - hat * jnp.mean(dh * hat, axis=-1, keepdims=True)
        base = gl[cuts[c], :].astype(F32)
        total = base + rstd * inner
        red_sum = red_sum + jnp.sum(base, axis=0, keepdims=True)
        out_sum = out_sum + jnp.sum(total, axis=0, keepdims=True)
        gres[cuts[c], :] = total
        low = total.astype(BF)
        gr[cuts[c], :] = low
        cut = pl.ds(c * step, step)
        gr_copies.append(start(gr.at[cut], gr.at[pl.ds(n_rows + c * step, step)], gr_s.at[c], gr_r.at[c], core_to))
        ga[cuts[c], :] = _dot(low, wo[...], 1, 1).astype(BF)
    vsum[0:1, :] = gain_sum
    vsum[1:2, :] = shift_sum
    vsum[2:3, :] = out_sum
    vsum[3:4, :] = red_sum
    vsum[4:8, :] = jnp.zeros((4, width), F32)
    for c in gr_copies:
        c.wait_recv()
    my_half = pl.ds(pl.multiple_of(core * (width // 2), width // 2), width // 2)

    def output_grad(cut):
        dwo[cut, :] = _dot(tt[cut, :], gr[:, my_half], 1, 0).astype(BF)

    loop(width, 256, output_grad)

    for slot in (0, 2, 4, 5):
        part_copies[slot].wait_recv()
    for part in range(2):

        def add(cut, part=part):
            place = pl.ds(pl.multiple_of(cut.start + part * (width // 2), 128), 128)
            fw[place, :] = (
                zw[0, place, :].astype(F32) + r1[2 * part, cut, :].astype(F32) + r2[part, cut, :].astype(F32)
            )

        loop(width // 2, 128, add)

    for c in dwe_copies[2:]:
        c.wait()

    @pl.when(jnp.logical_not(stays))
    def _():
        for c in swap_remote:
            c.wait()

    @pl.when(stays)
    def _():
        for c in swap_local:
            c.wait()

    for c in sends:
        c.wait_send()


def middle(attn, wo, x, g, gp, weh, wr, vec, ebias, live, nd):
    n_rows, width = x.shape
    block, own = wr.shape[0], weh.shape[1]
    any_, vmem = pl.BlockSpec(memory_space=pl.ANY), pl.BlockSpec(memory_space=pltpu.VMEM)
    dma = lambda *shape: pltpu.SemaphoreType.DMA(shape)
    one = pltpu.SemaphoreType.DMA
    sds = jax.ShapeDtypeStruct
    vm = lambda dtype, *shape: pltpu.VMEM(shape, dtype)
    both = 2 * n_rows
    return pl.pallas_call(
        functools.partial(middle_kernel, nd=nd),
        in_specs=[vmem, vmem, vmem, any_, any_, vmem, any_, vmem, vmem, vmem],
        out_specs=[any_, vmem, vmem, any_, vmem, vmem, vmem, vmem],
        out_shape=[
            sds(x.shape, BF), sds(x.shape, F32), sds(x.shape, BF), sds((width, own), BF),
            sds((width, width // 2), BF), sds((width, block), F32), sds((8, width), F32), sds((1, own), F32),
        ],
        scratch_shapes=[
            vm(BF, n_rows, width), vm(BF, own, width), vm(F32, n_rows, width), vm(BF, both, width),
            vm(BF, width, both), vm(BF, both, width), vm(F32, 4, both, block), vm(BF, 4, both, block),
            vm(BF, 4, width, block), vm(BF, 4, width // 2, block), vm(BF, 2, width // 2, block),
            vm(BF, 2, width, block), vm(BF, both, width), vm(BF, n_rows, width), vm(BF, n_rows, width),
            vm(BF, n_rows, width), vm(BF, n_rows, width), vm(BF, n_rows, width),
            dma(2), dma(2), one, one, dma(2), dma(2), dma(2), dma(2), dma(2), dma(2), dma(2), dma(2), dma(2),
            dma(4), dma(4), one, dma(6), dma(6), dma(2), dma(2),
        ],
        compiler_params=pltpu.CompilerParams(
            collective_id=2, has_side_effects=True, vmem_limit_bytes=60 << 20
        ),
        cost_estimate=pl.CostEstimate(
            flops=12 * both * width * own, bytes_accessed=40_000_000, transcendentals=2 * both * own
        ),
    )(attn, wo, x, g, gp, weh, wr, vec, ebias, live)


def back_kernel(
    ga, qkv, att, lse, st, n1t, wf, x, gres, gain, v_in, res, dwr, dwe, dwo,
    out, tg, insum, osum, esum, rsum, vout,
    go, qt, dot, kt, dqt, delta, gm, zin, far_in, tot, tot2, near_in, core_in, cst, crc, nst, nrc, tgs,
    vmine, vrc, vz, own, fwd, r1, r2, ns_st, ns_rc, keep, fs_st, fs_rc, fb, eb,
    move_s, move_r, move_l, a_s, a_r, a_l, d_s, d_r, out_s, out_r, out_l, tg_s, tg_r, tg_l, v_s, v_r, vz_s, vz_r,
    *, ns, nd, heads, d, bq, bk, chunks,
):
    seq, me = lax.axis_index("seq"), lax.axis_index("dp")
    half, nearb, core = seq // 2, seq % 2, me % 2
    member = 2 * core + nearb
    beside, twin, across = 2 * core + 1 - nearb, 2 * (1 - core) + nearb, 2 * (1 - core) + 1 - nearb
    n_rows, width = x.shape
    n, group, ncol = ns * n_rows, width // 4, nd // 2
    stays = half == core
    swap_to = (2 * core + nearb, me - core + half)
    near_to = (seq + 1 - 2 * nearb, me)
    far_to = (seq + 2 - 4 * half, me)
    third_to = (seq + 1 - 2 * nearb + 2 - 4 * half, me)
    core_to = (seq, me + 1 - 2 * core)

    def offset(k):
        result = me
        bit = 1
        while bit <= k:
            if k & bit:
                result = result + bit - 2 * bit * ((me // bit) % 2)
            bit *= 2
        return result

    def rcopy(src, dst, ss, rs, dev):
        return pltpu.make_async_remote_copy(
            src_ref=src, dst_ref=dst, send_sem=ss, recv_sem=rs, device_id=dev, device_id_type=MESH
        )

    def row_loop(total, size, body):
        size = 64 if total % 64 == 0 else size

        def one(t, carry):
            body(pl.multiple_of(t * size, size))
            return carry

        lax.fori_loop(0, total // size, one, 0)

    barrier = pltpu.get_barrier_semaphore()

    def hello(dev):
        pl.semaphore_signal(barrier, inc=1, device_id=dev, device_id_type=MESH)

    for k in range(1, nd):
        hello((seq, offset(k)))
    for dev in (near_to, far_to, third_to, (near_to[0], core_to[1])):
        hello(dev)

    @pl.when(jnp.logical_not(stays))
    def _():
        hello(swap_to)
        pl.semaphore_wait(barrier, nd + 4)

    @pl.when(stays)
    def _():
        pl.semaphore_wait(barrier, nd + 3)

    sends = []
    held = {}

    moves = []
    for i in range(4):
        src = ga.at[:, pl.ds(i * group, group)]
        mine = go.at[pl.ds(pl.multiple_of(member * n_rows, n_rows), n_rows)]
        dev = (seq - nearb + i % 2, me - core + i // 2)
        r = rcopy(src, mine, move_s.at[i], move_r.at[member], dev)
        stay = pltpu.make_async_copy(src, mine, move_l)
        moves.append((r, stay))

        @pl.when(member != i)
        def _(r=r):
            r.start()

        @pl.when(member == i)
        def _(stay=stay):
            stay.start()

    terms = (dwr, dwe, dwo, zin)
    pre = nd == 8
    high = [t.shape[0] // (1 if pre and a == 0 else ncol) for a, t in enumerate(terms)]
    wide = [t.shape[1] for t in terms]

    def block(a, kc, part=None):
        row = (offset(2 * kc) // 2) * high[a]
        if part is None:
            return terms[a].at[pl.ds(pl.multiple_of(row, high[a]), high[a])]
        low = high[a] // 2
        return terms[a].at[pl.ds(pl.multiple_of(row + part * low, low), low)]

    def send(a, slot, src, dst, dev):
        c = rcopy(src, dst, a_s.at[a, slot], a_r.at[a, slot], dev)
        c.start()
        held[a, slot] = c
        sends.append(c)

    def rows_at_once(total):
        return 64 if total % 64 == 0 else 16

    def lanes(first, size):
        return pl.ds(pl.multiple_of(first, 128), size)

    def s0(a):
        local = [pltpu.make_async_copy(block(a, 0), own[a], a_l.at[a, 0])]
        if nd == 8:
            x_to, y_to = (seq, offset(2)), (seq, offset(4))
            send(a, 0, block(a, 1, 0), r1[a].at[0], x_to)
            send(a, 2, block(a, 2, 1), r1[a].at[2], y_to)
            send(a, 1, block(a, 3, 0), r1[a].at[1], x_to)
            send(a, 3, block(a, 3, 1), r1[a].at[3], y_to)
            local.append(pltpu.make_async_copy(block(a, 2, 0), fwd[a].at[0], a_l.at[a, 1]))
            local.append(pltpu.make_async_copy(block(a, 1, 1), fwd[a].at[1], a_l.at[a, 2]))
        else:
            for kc in range(1, ncol):
                send(a, kc, block(a, kc), r1[a].at[kc - 1], (seq, offset(2 * kc)))
        for c in local:
            c.start()
        held[a, "local"] = local

    def s1(a):
        for c in held[a, "local"]:
            c.wait()
        span = rows_at_once(high[a] // 2)
        if nd == 8:
            for part, k in ((0, 4), (1, 2)):
                held[a, 1 + 2 * part].wait_recv()

                def add(t, part=part):
                    cut = pl.ds(t, rows_at_once(span))
                    fwd[a][part, cut, :] = (
                        fwd[a][part, cut, :].astype(F32) + r1[a][1 + 2 * part, cut, :].astype(F32)
                    ).astype(BF)

                row_loop(high[a] // 2, 16, add)
                send(a, 4 + part, fwd[a].at[part], r2[a].at[part], (seq, offset(k)))

    def s2(a):
        c, low = wide[a], high[a] // 2
        if pre and a == 0:
            pass
        elif nd == 8:
            for slot in (0, 2, 4, 5):
                held[a, slot].wait_recv()
        else:
            for kc in range(1, ncol):
                held[a, kc].wait_recv()

        span = rows_at_once(low)

        def total(part, t, cs):
            cut = pl.ds(part * low + t, span)
            if pre and a == 0:
                return dwr[cut, cs]
            value = own[a][cut, cs].astype(F32)
            if nd == 8:
                return (
                    value
                    + r1[a][2 * part, pl.ds(t, span), cs].astype(F32)
                    + r2[a][part, pl.ds(t, span), cs].astype(F32)
                )
            for kc in range(1, ncol):
                value = value + r1[a][kc - 1, cut, cs].astype(F32)
            return value

        for part in range(2):

            def add(t, part=part):
                cut = pl.ds(part * low + t, span)
                if a == 3:
                    tot[cut, :] = total(part, t, slice(None)).astype(BF)
                else:
                    keep[a][cut, :] = total(part, t, lanes(nearb * (c // 2), c // 2))
                    ns_st[a][cut, :] = total(part, t, lanes((1 - nearb) * (c // 2), c // 2)).astype(BF)

            row_loop(low, 16, add)
        if a == 3:
            send(a, 6, tot, far_in, far_to)
        else:
            send(a, 6, ns_st[a], ns_rc[a], near_to)

    def s3(a):
        c, span = wide[a], rows_at_once(high[a])
        held[a, 6].wait_recv()
        if a == 3:

            def add(t):
                cut = pl.ds(t, rows_at_once(span))
                tot2[cut, :] = (tot[cut, :].astype(F32) + far_in[cut, :].astype(F32)).astype(BF)

            row_loop(high[a], 16, add)
            send(a, 7, tot2, near_in, near_to)
            return

        def add(t):
            cut, cs = pl.ds(t, rows_at_once(high[a])), lanes((1 - half) * (c // 4), c // 4)
            fs_st[a][cut, :] = (keep[a][cut, cs] + ns_rc[a][cut, cs].astype(F32)).astype(BF)

        row_loop(high[a], 16, add)
        send(a, 7, fs_st[a], fs_rc[a], far_to)

    def s4(a):
        c = wide[a]
        held[a, 7].wait_recv()
        low = high[a] // 2
        theirs = pl.ds(pl.multiple_of((1 - core) * low, low), low)
        if a == 3:
            send(a, 8, tot2.at[theirs], core_in.at[0], core_to)
            send(a, 9, near_in.at[theirs], core_in.at[1], core_to)
            return
        place = lanes(nearb * (c // 2) + half * (c // 4), c // 4)

        def add(t):
            cut, cs = pl.ds(t, rows_at_once(high[a])), lanes(half * (c // 4), c // 4)
            value = keep[a][cut, cs] + ns_rc[a][cut, cs].astype(F32) + fs_rc[a][cut, :].astype(F32)
            fb[a][cut, place] = value.astype(BF)

        row_loop(high[a], 16, add)
        send(a, 8, fb[a].at[:, place], fb[a].at[:, place], far_to)

    def s5(a):
        c = wide[a]
        held[a, 8].wait_recv()
        low = high[a] // 2
        ours = pl.ds(pl.multiple_of(core * low, low), low)
        if a == 3:
            held[a, 9].wait_recv()
            for which, value in (
                (member, tot2[ours, :]), (beside, near_in[ours, :]), (twin, core_in[0]), (across, core_in[1])
            ):
                for i in range(3):
                    insum[:, lanes(i * width + which * group, group)] = value[:, i * group : (i + 1) * group]
            return
        place = lanes(nearb * (c // 2), c // 2)
        send(a, 9, fb[a].at[:, place], fb[a].at[:, place], near_to)

    def s6(a):
        held[a, 9].wait_recv()
        low = high[a] // 2
        theirs = pl.ds(pl.multiple_of((1 - core) * low, low), low)
        if a == 0:
            c = pltpu.make_async_copy(fb[a], rsum, a_l.at[a, 3])
            c.start()
            held[a, "last"] = c
        else:
            send(a, 10, fb[a].at[theirs], eb[a], core_to)

    def s7(a):
        if a == 0:
            held[a, "last"].wait()
            return
        held[a, 10].wait_recv()
        low = high[a] // 2
        ours = pl.ds(pl.multiple_of(core * low, low), low)
        if a == 2:
            size = wide[a]
            osum[:, lanes(core * size, size)] = fb[a][ours, :]
            osum[:, lanes((1 - core) * size, size)] = eb[a][...]
        else:
            size = wide[a] // ncol
            for i in range(ncol):
                cs = slice(i * size, (i + 1) * size)
                a0, a1 = fb[a][ours, cs], eb[a][:, cs]
                esum[:, 2 * i * size : (2 * i + 1) * size] = jnp.where(core == 0, a0, a1)
                esum[:, (2 * i + 1) * size : (2 * i + 2) * size] = jnp.where(core == 0, a1, a0)

    for a in (1, 2) if pre else (0, 1, 2):
        s0(a)
    if not pre:
        out_remote = rcopy(res, out, out_s, out_r, swap_to)
        out_local = pltpu.make_async_copy(res, out, out_l)

        @pl.when(jnp.logical_not(stays))
        def _():
            out_remote.start()

        @pl.when(stays)
        def _():
            out_local.start()

    w, scale = 2 * d, d**-0.5
    for i in range(4):
        cut = slice(i * n_rows, (i + 1) * n_rows)
        qt[:, cut] = jnp.transpose(qkv[cut, :group])
        kt[:, cut] = jnp.transpose(qkv[cut, group : 2 * group])
    dqt[...] = jnp.zeros_like(dqt)
    for i in range(4):
        cut = slice(i * n_rows, (i + 1) * n_rows)
        landing = go.at[pl.ds(i * n_rows, n_rows)]
        arrival = pltpu.make_async_copy(landing, landing, move_r.at[i])
        r, stay = moves[i]

        @pl.when(member != i)
        def _(r=r, arrival=arrival):
            arrival.wait()
            r.wait_send()

        @pl.when(member == i)
        def _(stay=stay):
            stay.wait()

    if pre:
        s2(0)
    for i in range(4):
        cut = slice(i * n_rows, (i + 1) * n_rows)
        dot[:, cut] = jnp.transpose(go[cut, :])
        prod = jnp.transpose(go[cut, :].astype(F32) * att[cut, :].astype(F32))
        for h in range(heads):
            delta[h // 2, h % 2 : h % 2 + 1, cut] = jnp.sum(prod[h * d : (h + 1) * d], axis=0, keepdims=True)

    zero = jnp.zeros((), BF)
    for j in range(0, n, bk):

        def pair(p, carry, j=j):
            at = lambda first: pl.ds(pl.multiple_of(first + p * w, w), w)
            kb, vb = qkv[j : j + bk, at(group)], qkv[j : j + bk, at(2 * group)]
            dk = jnp.zeros((bk, w), F32)
            dv = jnp.zeros((bk, w), F32)
            row = lax.broadcasted_iota(jnp.int32, (w, bq), 0)
            lane = lax.broadcasted_iota(jnp.int32, (bq, w), 1)
            for i in range(j // bq, n // bq):
                cs = slice(i * bq, (i + 1) * bq)
                key = lax.broadcasted_iota(jnp.int32, (bk, bq), 0) + j
                ok = key >= st[:, cs]
                if j + bk > i * bq:
                    ok = ok & (key <= lax.broadcasted_iota(jnp.int32, (bk, bq), 1) + i * bq)
                for h in range(2):
                    rows_h = (row >= h * d) & (row < (h + 1) * d)
                    lanes_h = (lane >= h * d) & (lane < (h + 1) * d)
                    s = _dot(kb, jnp.where(rows_h, qt[at(0), cs], zero), 1, 0) * scale
                    s = jnp.where(ok, s, NEG)
                    e = jnp.exp(s - lse[p, h : h + 1, cs])
                    dp = _dot(vb, jnp.where(rows_h, dot[at(0), cs], zero), 1, 0)
                    ds = (e * (dp - delta[p, h : h + 1, cs])).astype(BF)
                    dv = dv + _dot(e.astype(BF), jnp.where(lanes_h, go[cs, at(0)], zero), 1, 0)
                    dk = dk + _dot(ds, jnp.where(lanes_h, qkv[cs, at(0)], zero), 1, 0)
                    head = pl.ds(pl.multiple_of(p * w + h * d, d), d)
                    dqt[head, cs] += _dot(kt[head, j : j + bk], ds, 1, 0)
            gm[j : j + bk, at(group)] = (dk * scale).astype(BF)
            gm[j : j + bk, at(2 * group)] = dv.astype(BF)
            return carry

        lax.fori_loop(0, heads // 2, pair, 0)
        if pre:
            if j == 0:
                s3(0)
            elif j == bk:
                s1(1)
                s1(2)
            elif j == 2 * bk:
                s4(0)
        elif j == 0:
            s1(0)
        elif j == bk:
            s2(0)
        elif j == 2 * bk:
            s3(0)
    for i in range(4):
        cut = slice(i * n_rows, (i + 1) * n_rows)
        gm[cut, :group] = (jnp.transpose(dqt[:, cut]) * scale).astype(BF)

    step = n_rows // chunks

    def term(b, c):
        cut = pl.ds(pl.multiple_of(b * n_rows + c * step, step), step)
        return _dot(gm[cut, :], wf[...], 1, 1)

    quad = {}

    def quad_send(slot, src, dst, dev):
        c = rcopy(src, dst, d_s.at[slot], d_r.at[slot], dev)
        c.start()
        quad[slot] = c
        sends.append(c)

    for which, b in ((1, across), (0, twin)):
        for c in range(chunks):
            cut = pl.ds(c * step, step)
            cst[which, cut, :] = term(b, c).astype(BF)
            quad_send(which * chunks + c, cst.at[which, cut], crc.at[which, cut], core_to)
    for c in range(chunks):
        cut = pl.ds(c * step, step)
        value = term(beside, c)
        quad[chunks + c].wait_recv()
        nst[cut, :] = (value + crc[1, cut, :].astype(F32)).astype(BF)
        quad_send(2 * chunks + c, nst.at[cut], nrc.at[cut], near_to)

    if pre:
        s2(1)
        s2(2)
    else:
        s1(1)
        s1(2)
        s4(0)
    for i in range(4):
        cut = slice(i * group, (i + 1) * group)
        zin[cut, :] = _dot(n1t[cut, :], gm[...], 1, 0).astype(BF)
    s0(3)
    s5(0)
    if pre:
        s1(3)
        s3(1)
        s3(2)

    tg_remote, tg_local = [], []
    gain_sum = jnp.zeros((1, width), F32)
    shift_sum = jnp.zeros((1, width), F32)
    for c in range(chunks):
        cut = pl.ds(c * step, step)
        value = term(member, c)
        quad[c].wait_recv()
        quad[2 * chunks + c].wait_recv()
        dy = value + crc[0, cut, :].astype(F32) + nrc[cut, :].astype(F32)
        rows_in = x[cut, :].astype(F32)
        center = rows_in - jnp.mean(rows_in, axis=-1, keepdims=True)
        rstd = lax.rsqrt(jnp.mean(center * center, axis=-1, keepdims=True) + EPS)
        hat = center * rstd
        gain_sum = gain_sum + jnp.sum(dy * hat, axis=0, keepdims=True)
        shift_sum = shift_sum + jnp.sum(dy, axis=0, keepdims=True)
        dh = dy * gain[...]
        inner = dh - jnp.mean(dh, axis=-1, keepdims=True) - hat * jnp.mean(dh * hat, axis=-1, keepdims=True)
        tgs[cut, :] = (gres[cut, :] + rstd * inner).astype(BF)
        r = rcopy(tgs.at[cut], tg.at[cut], tg_s.at[c], tg_r.at[c], swap_to)
        stay = pltpu.make_async_copy(tgs.at[cut], tg.at[cut], tg_l.at[c])
        tg_remote.append(r)
        tg_local.append(stay)

        @pl.when(jnp.logical_not(stays))
        def _(r=r):
            r.start()

        @pl.when(stays)
        def _(stay=stay):
            stay.start()

    small = v_in.shape[2]
    for k in range(nd):
        vmine[k] = v_in[k]
        vmine[k, 0:1, :] = gain_sum[:, k * small : (k + 1) * small]
        vmine[k, 1:2, :] = shift_sum[:, k * small : (k + 1) * small]
    vec = []
    for k in range(1, nd):
        c = rcopy(vmine.at[offset(k)], vrc.at[k], v_s.at[k], v_r.at[k], (seq, offset(k)))
        c.start()
        vec.append(c)
        sends.append(c)

    if pre:
        s2(3)
        s4(1)
        s4(2)
    else:
        s2(1)
        s2(2)
        s6(0)
        s1(3)
    total = vmine[me]
    for k, c in enumerate(vec):
        c.wait_recv()
        total = total + vrc[k + 1]
    vz[seq] = total
    z_copies = []
    for i, dev in enumerate((near_to, far_to, third_to)):
        c = rcopy(vz.at[seq], vz.at[seq], vz_s.at[i], vz_r.at[i], dev)
        c.start()
        z_copies.append(c)
        sends.append(c)
    if pre:
        s6(0)
    else:
        s3(1)
        s3(2)
        s2(3)
        s4(1)
        s4(2)
    s3(3)
    s5(1)
    s5(2)
    s4(3)
    s6(1)
    s6(2)
    s5(3)
    for c in z_copies:
        c.wait_recv()
    total = vz[0]
    for i in range(1, ns):
        total = total + vz[i]
    vout[...] = total
    for a in range(3):
        s7(a)

    @pl.when(jnp.logical_not(stays))
    def _():
        if not pre:
            out_remote.wait()
        for c in tg_remote:
            c.wait()

    @pl.when(stays)
    def _():
        if not pre:
            out_local.wait()
        for c in tg_local:
            c.wait()

    for c in sends:
        c.wait_send()


def back(ga, qkv, att, lse, starts, n1t, wf, x, gres, gain, v_in, res, dwr, dwe, dwo, ns, nd, heads, d):
    n_rows, width = x.shape
    n, group, ncol, chunks = n_rows * ns, width // 4, nd // 2, 4
    any_, vmem = pl.BlockSpec(memory_space=pl.ANY), pl.BlockSpec(memory_space=pltpu.VMEM)
    dma = lambda *shape: pltpu.SemaphoreType.DMA(shape)
    one = pltpu.SemaphoreType.DMA
    sds = jax.ShapeDtypeStruct
    pre = nd == 8
    sizes = [(t.shape[0] // ncol, t.shape[1]) for t in (dwr, dwe, dwo)] + [(width // ncol, 3 * group)]
    plane = list(sizes)
    if pre:
        sizes[0], plane[0] = dwr.shape, (32, 128)
    vm = lambda dtype, *shape: pltpu.VMEM(shape, dtype)
    slots = max(11, nd)
    rr, cc = width // nd, 3 * group
    return pl.pallas_call(
        functools.partial(back_kernel, ns=ns, nd=nd, heads=heads, d=d, bq=n_rows // 2, bk=n_rows, chunks=chunks),
        in_specs=[vmem] * 11 + [any_, vmem if pre else any_, any_, any_],
        out_specs=[any_, any_, vmem, vmem, vmem, any_, vmem],
        out_shape=[
            sds(res.shape, BF), sds(x.shape, BF), sds((rr, 3 * width), BF), sds((rr, width), BF),
            sds((rr, 2 * dwe.shape[1]), BF), sds(sizes[0], BF), sds(v_in.shape[1:], F32),
        ],
        scratch_shapes=[
            vm(BF, n, group), vm(BF, group, n), vm(BF, group, n), vm(BF, group, n), vm(F32, group, n),
            vm(F32, heads // 2, 2, n), vm(BF, n, 3 * group), vm(BF, width, 3 * group),
            vm(BF, 2 * rr, cc), vm(BF, 2 * rr, cc), vm(BF, 2 * rr, cc), vm(BF, 2 * rr, cc), vm(BF, 2, rr, cc),
            vm(BF, 2, n_rows, width), vm(BF, 2, n_rows, width), vm(BF, n_rows, width), vm(BF, n_rows, width),
            vm(BF, n_rows, width), vm(F32, *v_in.shape), vm(F32, *v_in.shape), vm(F32, ns, *v_in.shape[1:]),
            [vm(BF, r, c) for r, c in plane],
            [vm(BF, 2, r // 2, c) for r, c in plane],
            [vm(BF, 4, r // 2, c) if nd == 8 else vm(BF, ncol - 1, r, c) for r, c in plane],
            [vm(BF, 2, r // 2, c) for r, c in plane],
            [vm(BF, r, c // 2) for r, c in sizes[:3]], [vm(BF, r, c // 2) for r, c in sizes[:3]],
            [vm(F32, r, c // 2) for r, c in sizes[:3]],
            [vm(BF, r, c // 4) for r, c in sizes[:3]], [vm(BF, r, c // 4) for r, c in sizes[:3]],
            [vm(BF, r, c) for r, c in sizes[:3]], [vm(BF, r // 2, c) for r, c in sizes[:3]],
            dma(4), dma(4), one, dma(4, slots), dma(4, slots), dma(4, 4),
            dma(3 * chunks), dma(3 * chunks), one, one, one, dma(chunks), dma(chunks), dma(chunks),
            dma(nd), dma(nd), dma(3), dma(3),
        ],
        compiler_params=pltpu.CompilerParams(
            collective_id=1, has_side_effects=True, vmem_limit_bytes=60 << 20
        ),
        cost_estimate=pl.CostEstimate(
            flops=20 * n * n * d * heads, bytes_accessed=60_000_000, transcendentals=n * n * heads
        ),
    )(ga, qkv, att, lse, starts, n1t, wf, x, gres, gain, v_in, res, dwr, dwe, dwo)


def layer_normalize(values, gain, shift):
    center = values - jnp.mean(values, axis=-1, keepdims=True)
    spread = jnp.mean(center * center, axis=-1, keepdims=True)
    return center * lax.rsqrt(spread + EPS) * gain + shift


def smooth_gate(values):
    return jax.nn.gelu(values, approximate=True)


def rows(array, start, size):
    return lax.dynamic_slice_in_dim(array, start, size, 0)


def cols(array, start, size):
    return lax.dynamic_slice_in_dim(array, start, size, 1)


def put(array, piece, row, col):
    return lax.dynamic_update_slice(array, piece, (row, col))


def bf_round(x):
    return lax.reduce_precision(x, 8, 7)


class Links:
    def __init__(self, ns, nd):
        self.ns, self.nd = ns, nd

    def go(self, array, target):
        pairs = []
        for s in range(self.ns):
            for d in range(self.nd):
                ts, td = target(s, d)
                pairs.append((s * self.nd + d, ts * self.nd + td))
        return lax.ppermute(array, ("seq", "dp"), pairs)

    def dp(self, array, k):
        return self.go(array, lambda s, d: (s, d ^ k))

    def core(self, array):
        return self.dp(array, 1)

    def near(self, array):
        return self.go(array, lambda s, d: (s ^ 1, d))

    def far(self, array):
        return self.go(array, lambda s, d: (s ^ 2, d))

    def both(self, array):
        return self.go(array, lambda s, d: (s ^ 1, d ^ 1))

    def swap(self, array):
        return self.go(array, lambda s, d: (2 * (d % 2) + s % 2, d - d % 2 + s // 2))


def on_device(
    tokens, lengths, cotangent, mixer_input, mixer_output, expand_weight, reduce_weight,
    first_gain, first_shift, second_gain, second_shift, output_bias, expand_bias, reduce_bias,
):
    ns, nd = lax.axis_size("seq"), lax.axis_size("dp")
    links = Links(ns, nd)
    seq, me = lax.axis_index("seq"), lax.axis_index("dp")
    half, near_bit, core = seq // 2, seq % 2, me % 2
    column = me // 2
    member = 2 * core + near_bit
    n_rows, width = tokens.shape[1:]
    slots = n_rows * ns
    head_dim = width // HEADS
    hidden = reduce_weight.shape[0] * nd
    group = width // 4
    my_heads = HEADS // 4

    lengths_row = jnp.where(half == core, lengths[0], links.core(lengths)[0])
    entry = jnp.arange(lengths_row.shape[0])
    ends = jnp.sum(jnp.where(entry[None, :] <= entry[:, None], lengths_row[None, :], 0), axis=1)
    place = jnp.arange(slots, dtype=jnp.int32)
    passed = place[:, None] >= ends[None, :]
    starts = jnp.max(jnp.where(passed, ends[None, :], 0), axis=1)
    starts = jnp.where(place < ends[-1], starts, place).reshape(1, slots)
    live = (member * n_rows + jnp.arange(n_rows, dtype=jnp.int32) < ends[-1]).astype(F32)

    small, small_rows = width // nd, mixer_input.shape[0]
    wide = hidden // nd
    vectors = jnp.concatenate(
        [first_gain, first_shift, second_gain, second_shift, output_bias, reduce_bias, expand_bias]
    ).reshape(-1, small)
    vectors = jnp.concatenate([vectors, jnp.zeros((-vectors.shape[0] % 16, small), BF)])
    by_core = expand_weight.reshape(small_rows, nd // 2, 2, wide).transpose(2, 0, 1, 3)
    by_core = by_core.reshape(2, small_rows, hidden // 2)
    (
        x_low, grad_low, twin_grad, normed_t, input_full, output_full, expand_half, reduce_half, vectors,
        qkv, attended, logsum, attention,
    ) = front(
        tokens[0], cotangent[0], mixer_input, mixer_output, by_core, reduce_weight, vectors,
        starts, ns, nd, my_heads, head_dim,
    )
    vectors = vectors.astype(F32)
    gain_one, _, gain_two, shift_two, output_add, reduce_add = (vectors[:, i].reshape(-1) for i in range(6))
    n_wide = wide // small
    expand_add = vectors[:, 6 : 6 + n_wide].reshape(nd // 2, 2, wide)
    expand_add = lax.dynamic_index_in_dim(expand_add, core, 1, keepdims=False).reshape(-1)

    twin_live = ((member ^ 2) * n_rows + jnp.arange(n_rows, dtype=jnp.int32) < ends[-1]).astype(F32)
    if nd == 8:
        vec = jnp.stack([gain_two, shift_two, output_add, reduce_add])
        vec = jnp.concatenate([vec, jnp.zeros_like(vec)])
        both_live = jnp.concatenate([live, twin_live])[:, None]
        result, grad_resid, grad_attention, expand_term, output_term, reduce_term, row_sums, wide_sums = middle(
            attention, output_full, x_low, grad_low, twin_grad, expand_half, reduce_weight,
            vec, expand_add[None], both_live, nd,
        )
        gain_two_sum, shift_two_sum, output_bias_sum, reduce_bias_sum = (row_sums[i] for i in range(4))
        expand_bias_sum = wide_sums[0]
        layer_output, result = result, jnp.zeros((16, 128), BF)
    else:
        twin_attention = links.core(attention)
        inputs = x_low.astype(F32)
        resid = inputs + mm(attention, output_full) + output_add
        normed_two = layer_normalize(resid, gain_two, shift_two).astype(BF)
        normed_two = jnp.concatenate([normed_two, links.core(normed_two)])
        expanded = mm(normed_two, expand_half) + expand_add
        active = smooth_gate(expanded).astype(BF)
        reduced = mm(active, reduce_half)
        twin_part = links.core(reduced[n_rows:].astype(BF)).astype(F32)
        result = (resid + reduced[:n_rows] + twin_part + reduce_add).astype(BF)
        grad_result = grad_low.astype(F32) * live[:, None]
        result_low = jnp.concatenate([grad_result.astype(BF), (twin_grad.astype(F32) * twin_live[:, None]).astype(BF)])
        reduce_term = mm_left(active, result_low).astype(BF)
        reduce_bias_sum = jnp.sum(grad_result, axis=0)
        grad_active = mm_right(result_low, reduce_half)
        _, gate_back = jax.vjp(smooth_gate, expanded)
        grad_expanded = gate_back(grad_active)[0]
        expand_bias_sum = jnp.sum(grad_expanded, axis=0)
        expanded_low = grad_expanded.astype(BF)
        expand_term = mm_left(normed_two, expanded_low).astype(BF)
        grad_normed = mm_right(expanded_low, expand_half)
        grad_normed_two = grad_normed[:n_rows] + links.core(grad_normed[n_rows:].astype(BF)).astype(F32)
        _, second_back = jax.vjp(layer_normalize, resid, gain_two, shift_two)
        resid_part, gain_two_sum, shift_two_sum = second_back(grad_normed_two)
        grad_resid = grad_result + resid_part
        output_bias_sum = jnp.sum(grad_resid, axis=0)
        resid_low = grad_resid.astype(BF)
        grad_attention = mm_right(resid_low, output_full).astype(BF)
        both_low = jnp.concatenate([resid_low, links.core(resid_low)])
        both_low = cols(both_low, core * (width // 2), width // 2)
        output_term = mm_left(jnp.concatenate([attention, twin_attention]), both_low).astype(BF)

    sums = jnp.stack([gain_two_sum, shift_two_sum, output_bias_sum, reduce_bias_sum])
    sums = sums.reshape(4, nd, small).transpose(1, 0, 2)
    wide_sum = expand_bias_sum.reshape(nd // 2, 1, n_wide, small)
    parity = jnp.arange(2).reshape(1, 2, 1, 1)
    wide_sum = jnp.where(parity == core, wide_sum, 0.0).reshape(nd, n_wide, small)
    pad = -(6 + n_wide) % 8
    sums = jnp.concatenate([jnp.zeros((nd, 2, small)), sums, wide_sum, jnp.zeros((nd, pad, small))], axis=1)

    swapped, tokens_gradient, input_sum, output_sum, expand_sum, reduce_sum, sums = back(
        grad_attention, qkv, attended, logsum, starts, normed_t, input_full, x_low, grad_resid,
        gain_one.reshape(1, width), sums, result, reduce_term, expand_term, output_term,
        ns, nd, my_heads, head_dim,
    )
    if nd == 8:
        reduce_sum = reduce_sum.T
    else:
        layer_output = swapped
    return (
        layer_output[None],
        tokens_gradient.astype(F32)[None],
        input_sum.astype(F32),
        output_sum.astype(F32),
        expand_sum.astype(F32),
        reduce_sum.astype(F32),
        sums[0],
        sums[1],
        sums[2],
        sums[3],
        sums[4],
        sums[6 : 6 + n_wide].reshape(-1),
        sums[5],
    )


def solution(mesh):
    row, vec = P("dp", None), P("dp")
    act = P("dp", "seq", None)
    return jax.shard_map(
        on_device,
        mesh=mesh,
        in_specs=(act, row, act, row, row, row, row, vec, vec, vec, vec, vec, vec, vec),
        out_specs=(act, act, row, row, row, row, vec, vec, vec, vec, vec, vec, vec),
        check_vma=False,
    )
```

```python
import functools

import jax
import jax.numpy as jnp
from jax import lax
from jax.experimental import pallas as pl
from jax.experimental.pallas import tpu as pltpu
from jax.sharding import PartitionSpec as P

HEADS = 16
EPS = 1e-05
NEG = -1e30
F32 = jnp.float32
BF = jnp.bfloat16


def _dot(a, b, ca, cb):
    return lax.dot_general(a, b, (((ca,), (cb,)), ((), ())), preferred_element_type=F32)


def mm(a, b):
    return _dot(a, b, 1, 0)


def mm_left(a, b):
    return _dot(a, b, 0, 0)


def mm_right(a, b):
    return _dot(a, b, 1, 1)


MESH = pl.DeviceIdType.MESH


def front_kernel(
    tok, cot, win, wo, we, wr, vec, st,
    x_ref, gg_ref, n1t, wf, wof, wef, wrf, vecs, qkv, att, lse, attn,
    n1, qt, vt, win_s, win_r, vec_s, vec_r, tok_s, tok_r, tok_l, near_s, near_r, core_s, core_r, fwd_s, fwd_r,
    cot_s, cot_r, cot_l, gp_s, gp_r, own_l, w_s, w_r, move_s, move_r, move_l,
    *, ns, nd, heads, d, bq, bk, chunks,
):
    seq, me = lax.axis_index("seq"), lax.axis_index("dp")
    half, nearb, core = seq // 2, seq % 2, me % 2
    member = 2 * core + nearb
    n_rows, width = tok.shape
    g_ref, gp_ref = gg_ref.at[pl.ds(0, n_rows)], gg_ref.at[pl.ds(n_rows, n_rows)]
    group = width // 4
    small_rows = win.shape[0]
    stays = half == core
    swap_to = (2 * core + nearb, me - core + half)
    near_to = (seq + 1 - 2 * nearb, me)
    core_to = (seq, me + 1 - 2 * core)

    def offset(k):
        out = me
        bit = 1
        while bit <= k:
            if k & bit:
                out = out + bit - 2 * bit * ((me // bit) % 2)
            bit *= 2
        return out

    def rcopy(src, dst, ss, rs, dev):
        return pltpu.make_async_remote_copy(
            src_ref=src, dst_ref=dst, send_sem=ss, recv_sem=rs, device_id=dev, device_id_type=MESH
        )

    barrier = pltpu.get_barrier_semaphore()

    def hello(dev):
        pl.semaphore_signal(barrier, inc=1, device_id=dev, device_id_type=MESH)

    for k in range(1, nd):
        hello((seq, offset(k)))
    hello(near_to)
    hello((near_to[0], core_to[1]))

    @pl.when(jnp.logical_not(stays))
    def _():
        hello(swap_to)
        pl.semaphore_wait(barrier, nd + 2)

    @pl.when(stays)
    def _():
        pl.semaphore_wait(barrier, nd + 1)

    sends = []

    step = n_rows // chunks
    tok_remote, tok_local = [], []
    for c in range(chunks):
        cut = pl.ds(c * step, step)
        tok_remote.append(rcopy(tok.at[cut], x_ref.at[cut], tok_s.at[c], tok_r.at[c], swap_to))
        tok_local.append(pltpu.make_async_copy(tok.at[cut], x_ref.at[cut], tok_l.at[c]))

    @pl.when(jnp.logical_not(stays))
    def _():
        for c in tok_remote:
            c.start()

    @pl.when(stays)
    def _():
        for c in tok_local:
            c.start()

    vec_copies, win_copies, own_copies = [], [], []
    for k in range(1, nd):
        c = rcopy(vec, vecs.at[me], vec_s.at[k], vec_r.at[k], (seq, offset(k)))
        c.start()
        vec_copies.append(c)
    c = pltpu.make_async_copy(vec, vecs.at[me], own_l.at[0])
    c.start()
    vec_copies.append(c)
    my_rows = pl.ds(pl.multiple_of(me * small_rows, small_rows), small_rows)
    for k in range(nd):
        target = 2 * (core if k % 2 == 0 else 1 - core) + nearb
        for i in range(3):
            src = win.at[:, pl.ds(pl.multiple_of(i * width + target * group, 128), group)]
            dst = wf.at[my_rows, pl.ds(i * group, group)]
            if k == 0:
                c = pltpu.make_async_copy(src, dst, own_l.at[1 + i])
            else:
                c = rcopy(src, dst, win_s.at[k, i], win_r.at[k, i], (seq, offset(k)))
            c.start()
            win_copies.append(c)

    pairs = ((wo, wof), (we, wef), (wr, wrf))

    split = len(we.shape) == 2

    def source(a, k):
        return we.at[core if k % 2 == 0 else 1 - core] if a == 1 else pairs[a][0]

    def blocks(k, dst):
        size = wef.shape[1] // (nd // 2)
        which = core if k % 2 == 0 else 1 - core
        for i in range(nd // 2):
            src = we.at[:, pl.ds(pl.multiple_of((2 * i + which) * size, 128), size)]
            yield src, dst.at[:, pl.ds(i * size, size)]

    def at(a, k, part=None):
        high = pairs[a][0].shape[-2]
        row = (offset(k) // 2 if a == 2 else offset(k)) * high
        if part is None:
            return pairs[a][1].at[pl.ds(pl.multiple_of(row, high), high)]
        return pairs[a][1].at[pl.ds(pl.multiple_of(row + part * (high // 2), high // 2), high // 2)]

    held = {}

    def send(a, slot, src, dst, k):
        c = rcopy(src, dst, w_s.at[a, slot], w_r.at[a, slot], (seq, offset(k)))
        c.start()
        held[a, slot] = c

    def send_shard(a, k):
        if a != 1 or not split:
            send(a, k, source(a, k), at(a, 0), k)
            return
        dev = (seq, offset(k))
        for src, dst in blocks(k, at(a, 0)):
            rcopy(src, dst, w_s.at[a, k], w_r.at[a, k], dev).start()
        held[a, k] = rcopy(at(a, 0), at(a, 0), w_s.at[a, k], w_r.at[a, k], dev)

    direct = (2, 3, 4, 5) if nd == 8 else range(2, nd)

    def weights_start(a):
        for k in direct:
            if k % 2 == 0 or a == 1:
                send_shard(a, k)
        if a < 2:
            send_shard(a, 1)
        if a == 1 and split:
            for src, dst in blocks(0, at(a, 0)):
                pltpu.make_async_copy(src, dst, own_l.at[4 + a]).start()
            held[a, "own"] = pltpu.make_async_copy(at(a, 0), at(a, 0), own_l.at[4 + a])
        else:
            c = pltpu.make_async_copy(source(a, 0), at(a, 0), own_l.at[4 + a])
            c.start()
            held[a, "own"] = c

    def weights_forward(a):
        for k in direct:
            if k % 2 == 0 or a == 1:
                held[a, k].wait_recv()
                if nd == 8 and a < 2:
                    send(a, 8 + k, at(a, k, k // 4), at(a, k, k // 4), 6 - k // 2 * 2)
                if a == 0:
                    send(a, k + 1 if nd > 8 else 14 + k // 2, at(a, k), at(a, k), 1)

    def weights_last(a):
        if nd == 8 and a == 0:
            for part, k in ((0, 2), (1, 4)):
                held[a, 8 + k].wait_recv()
                send(a, 3 + 2 * part, at(a, 6, part), at(a, 6, part), 1)

    def weights_end(a):
        held[a, "own"].wait()
        waited = set(direct) if a else {k for k in direct if k % 2 == 0}
        if nd == 8 and a == 0:
            waited |= {10, 12}
        for (b, slot), c in held.items():
            if b == a and slot != "own":
                if slot not in waited:
                    c.wait_recv()
                c.wait_send()

    for a in range(3):
        weights_start(a)

    for c in vec_copies[:-1]:
        c.wait_recv()
        sends.append(c)
    vec_copies[-1].wait()

    def vector(i):
        return jnp.concatenate([vecs[k, i : i + 1, :] for k in range(nd)], axis=1).astype(F32)

    gain, shift = vector(0), vector(1)
    near_copies, core_copies = [], []
    for c in range(chunks):
        cut = pl.ds(c * step, step)

        @pl.when(jnp.logical_not(stays))
        def _(c=c):
            tok_remote[c].wait_recv()

        @pl.when(stays)
        def _(c=c):
            tok_local[c].wait()

        value = x_ref[cut, :].astype(F32)
        center = value - jnp.mean(value, axis=-1, keepdims=True)
        spread = jnp.mean(center * center, axis=-1, keepdims=True)
        place = pl.ds(pl.multiple_of(member * n_rows + c * step, step), step)
        n1[place, :] = (center * lax.rsqrt(spread + EPS) * gain + shift).astype(BF)
        r = rcopy(n1.at[place], n1.at[place], near_s.at[c], near_r.at[c], near_to)
        r.start()
        near_copies.append(r)
        r = rcopy(n1.at[place], n1.at[place], core_s.at[c], core_r.at[c], core_to)
        r.start()
        core_copies.append(r)

    for c in win_copies[:3]:
        c.wait()
    for c in win_copies[3:]:
        c.wait_recv()
        sends.append(c)

    def project(block, c=None):
        size = n_rows if c is None else step
        place = pl.ds(pl.multiple_of(block * n_rows + (0 if c is None else c * step), size), size)
        mixed = _dot(n1[place, :], wf[...], 1, 0).astype(BF)
        qkv[place, :] = mixed
        n1t[:, place] = jnp.transpose(n1[place, :])
        qt[:, place] = jnp.transpose(mixed[:, :group])
        vt[:, place] = jnp.transpose(mixed[:, 2 * group :])

    project(member)
    for c in core_copies:
        c.wait_recv()
        sends.append(c)
    twin = 2 * (1 - core) + nearb
    project(twin)
    fwd_copies = []
    beside = 2 * core + 1 - nearb
    across = 2 * (1 - core) + 1 - nearb
    for c in range(chunks):
        near_copies[c].wait_recv()
        sends.append(near_copies[c])
        place = pl.ds(pl.multiple_of(beside * n_rows + c * step, step), step)
        r = rcopy(n1.at[place], n1.at[place], fwd_s.at[c], fwd_r.at[c], core_to)
        r.start()
        fwd_copies.append(r)
    project(beside)
    for c in fwd_copies:
        c.wait_recv()
        sends.append(c)
    project(across)

    cot_remote = rcopy(cot, g_ref, cot_s, cot_r, swap_to)
    cot_local = pltpu.make_async_copy(cot, g_ref, cot_l)

    @pl.when(jnp.logical_not(stays))
    def _():
        cot_remote.start()

    @pl.when(stays)
    def _():
        cot_local.start()

    n = ns * n_rows
    scale = d**-0.5
    w = 2 * d
    moves = []
    for i in range(n // bq):
        cs = slice(i * bq, (i + 1) * bq)

        def pair(p, carry, i=i, cs=cs):
            lanes = pl.ds(pl.multiple_of(p * w, w), w)
            key_lanes = pl.ds(pl.multiple_of(group + p * w, w), w)
            outs = []
            for h in range(2):
                row = lax.broadcasted_iota(jnp.int32, (w, bq), 0)
                qm = jnp.where((row >= h * d) & (row < (h + 1) * d), qt[lanes, cs], jnp.zeros((), BF))
                m = jnp.full((1, bq), NEG, F32)
                l = jnp.zeros((1, bq), F32)
                acc = jnp.zeros((d, bq), F32)
                for j in range(0, (i + 1) * bq, bk):
                    s = _dot(qkv[j : j + bk, key_lanes], qm, 1, 0) * scale
                    key = lax.broadcasted_iota(jnp.int32, (bk, bq), 0) + j
                    ok = key >= st[:, cs]
                    if j + bk > i * bq:
                        ok = ok & (key <= lax.broadcasted_iota(jnp.int32, (bk, bq), 1) + i * bq)
                    s = jnp.where(ok, s, NEG)
                    mn = jnp.maximum(m, jnp.max(s, axis=0, keepdims=True))
                    e = jnp.exp(s - mn)
                    a = jnp.exp(m - mn)
                    l = a * l + jnp.sum(e, axis=0, keepdims=True)
                    rows_h = pl.ds(pl.multiple_of(p * w + h * d, d), d)
                    acc = a * acc + _dot(vt[rows_h, j : j + bk], e.astype(BF), 1, 0)
                    m = mn
                outs.append(acc / l)
                lse[p, h : h + 1, cs] = m + jnp.log(l)
            att[cs, lanes] = jnp.transpose(jnp.concatenate(outs, axis=0)).astype(BF)
            return carry

        lax.fori_loop(0, heads // 2, pair, 0)
        mine = attn.at[:, pl.ds(pl.multiple_of(member * group, group), group)]
        dev = (seq - nearb + i % 2, me - core + i // 2)
        r = rcopy(att.at[cs], mine, move_s.at[i], move_r.at[member], dev)
        keep = pltpu.make_async_copy(att.at[cs], mine, move_l)
        moves.append((r, keep))

        @pl.when(member != i)
        def _(r=r):
            r.start()

        @pl.when(member == i)
        def _(keep=keep):
            keep.start()

        if i < 3:
            weights_forward(i)
    weights_last(0)

    @pl.when(jnp.logical_not(stays))
    def _():
        cot_remote.wait_recv()

    @pl.when(stays)
    def _():
        cot_local.wait()

    twin_cot = rcopy(g_ref, gp_ref, gp_s, gp_r, core_to)
    twin_cot.start()
    for a in range(3):
        weights_end(a)
    for i, (r, keep) in enumerate(moves):
        source = attn.at[:, pl.ds(i * group, group)]
        arrival = pltpu.make_async_copy(source, source, move_r.at[i])

        @pl.when(member != i)
        def _(r=r, arrival=arrival):
            r.wait_send()
            arrival.wait()

        @pl.when(member == i)
        def _(keep=keep):
            keep.wait()

    @pl.when(jnp.logical_not(stays))
    def _():
        cot_remote.wait_send()
        for c in tok_remote:
            c.wait_send()

    twin_cot.wait()
    for c in sends:
        c.wait_send()


def front(tok, cot, win, wo, we, wr, vec, starts, ns, nd, heads, d):
    n_rows, width = tok.shape
    n, group, chunks = n_rows * ns, width // 4, 4
    slots = 17 if nd == 8 else nd
    compact = lambda a: jax.ShapeDtypeStruct((a.shape[0] * (nd // 2), a.shape[1]), BF)
    any_, vmem = pl.BlockSpec(memory_space=pl.ANY), pl.BlockSpec(memory_space=pltpu.VMEM)
    full = lambda a: jax.ShapeDtypeStruct((a.shape[0] * nd, a.shape[1]), BF)
    dma = lambda *shape: pltpu.SemaphoreType.DMA(shape)
    sds = jax.ShapeDtypeStruct
    return pl.pallas_call(
        functools.partial(front_kernel, ns=ns, nd=nd, heads=heads, d=d, bq=n_rows, bk=n_rows, chunks=chunks),
        in_specs=[any_] * 7 + [vmem],
        out_specs=[vmem, any_, vmem, vmem, any_, any_, any_, vmem, vmem, vmem, vmem, vmem],
        out_shape=[
            sds(tok.shape, BF), sds((2 * n_rows, width), BF), sds((width, n), BF), sds((width, 3 * group), BF),
            full(wo), sds((width, we.shape[1] // 2 if len(we.shape) == 2 else we.shape[2]), BF), compact(wr), sds((nd, *vec.shape), BF), sds((n, 3 * group), BF),
            sds((n, group), BF), sds((heads // 2, 2, n), F32), sds(tok.shape, BF),
        ],
        scratch_shapes=[
            pltpu.VMEM((n, width), BF), pltpu.VMEM((group, n), BF), pltpu.VMEM((group, n), BF),
            dma(nd, 3), dma(nd, 3), dma(nd), dma(nd), dma(chunks), dma(chunks), dma(chunks),
            dma(chunks), dma(chunks), dma(chunks), dma(chunks), dma(chunks), dma(chunks),
            pltpu.SemaphoreType.DMA, pltpu.SemaphoreType.DMA, pltpu.SemaphoreType.DMA,
            pltpu.SemaphoreType.DMA, pltpu.SemaphoreType.DMA, dma(7), dma(3, slots), dma(3, slots), dma(4), dma(4), pltpu.SemaphoreType.DMA,
        ],
        compiler_params=pltpu.CompilerParams(
            collective_id=0, has_side_effects=True, vmem_limit_bytes=52 << 20
        ),
        cost_estimate=pl.CostEstimate(
            flops=8 * n * n * d * heads, bytes_accessed=60_000_000, transcendentals=n * n * heads
        ),
    )(tok, cot, win, wo, we, wr, vec, starts)


def middle_kernel(
    attn, wo, x, gl, weh, wrf, vec, ebias,
    out, gres, ga, fe, dwo, fq, vsum, esum,
    attb, wrh, resid, n2, tt, slope, act, zw, r1, r2, ws, e1, e2, gr, gs, xs_o, xr_o, xr_d, n_rc, f_rc,
    n2_s, n2_r, at_s, at_r, o_s, o_r, d_s, d_r, gr_s, gr_r, sw_s, sw_r, sw_l, a_s, a_r, e_s, e_r, z_s, z_r, w_s, w_r, w_l,
    *, nd,
):
    seq, me = lax.axis_index("seq"), lax.axis_index("dp")
    half, nearb, core = seq // 2, seq % 2, me % 2
    n_rows, width = x.shape
    both, block, ncol = 2 * n_rows, wrf.shape[0] // (nd // 2), nd // 2
    stays = half == core
    swap_to = (2 * core + nearb, me - core + half)
    core_to = (seq, me + 1 - 2 * core)
    column = me // 2
    x_to = (seq, me + 2 - 4 * (column % 2))
    y_to = (seq, me + 4 - 8 * (column // 2))

    def col(k):
        result = column
        if k & 1:
            result = result + 1 - 2 * (column % 2)
        if k & 2:
            result = result + 2 - 4 * (column // 2)
        return result

    def rcopy(src, dst, ss, rs, dev):
        return pltpu.make_async_remote_copy(
            src_ref=src, dst_ref=dst, send_sem=ss, recv_sem=rs, device_id=dev, device_id_type=MESH
        )

    def loop(total, size, body):
        def one(t, carry):
            body(pl.ds(pl.multiple_of(t * size, size), size))
            return carry

        lax.fori_loop(0, total // size, one, 0)

    barrier = pltpu.get_barrier_semaphore()

    def hello(dev):
        pl.semaphore_signal(barrier, inc=1, device_id=dev, device_id_type=MESH)

    near_to = (seq + 1 - 2 * nearb, me)
    far_to = (seq + 2 - 4 * half, me)
    for dev in (core_to, x_to, y_to, near_to, far_to):
        hello(dev)

    @pl.when(jnp.logical_not(stays))
    def _():
        hello(swap_to)
        pl.semaphore_wait(barrier, 6)

    @pl.when(stays)
    def _():
        pl.semaphore_wait(barrier, 5)

    sends = []

    def start(src, dst, ss, rs, dev):
        c = rcopy(src, dst, ss, rs, dev)
        c.start()
        sends.append(c)
        return c

    def owner(k, first, size):
        return pl.ds(pl.multiple_of(col(k) * block + first, block // 2), size)

    w_parts = []
    for i, (k, dev) in enumerate(((1, y_to), (2, x_to))):
        place = owner(k, i * (block // 2), block // 2)
        w_parts.append(start(wrf.at[place], wrh.at[place], w_s.at[i], w_r.at[i], dev))
    w_local = []
    for k in range(3):
        place = owner(k, 0, block)
        c = pltpu.make_async_copy(wrf.at[place], wrh.at[place], w_l.at[k])
        c.start()
        w_local.append(c)
    at_copy = start(attn, attb, at_s, at_r, core_to)

    step = n_rows // 2
    cuts = [slice(c * step, (c + 1) * step) for c in range(2)]
    theirs = [slice(n_rows + c * step, n_rows + (c + 1) * step) for c in range(2)]
    gain, shift = vec[0:1, :], vec[1:2, :]
    n2_copies = []
    for c in range(2):
        cut = pl.ds(c * step, step)
        value = x[cut, :].astype(F32) + _dot(attn[cut, :], wo[...], 1, 0) + vec[2:3, :]
        resid[cut, :] = value
        center = value - jnp.mean(value, axis=-1, keepdims=True)
        spread = jnp.mean(center * center, axis=-1, keepdims=True)
        n2[cut, :] = (center * lax.rsqrt(spread + EPS) * gain + shift).astype(BF)
        n2_copies.append(
            start(n2.at[cut], n2.at[pl.ds(n_rows + c * step, step)], n2_s.at[c], n2_r.at[c], core_to)
        )
    for c in range(4):
        cut = slice(c * step, (c + 1) * step)
        tt[:, cut] = jnp.transpose(gl[cut, :])
    for c in n2_copies:
        c.wait_recv()

    part_copies = {}

    def part_send(slot, src, dst, dev):
        c = rcopy(src, dst, a_s.at[slot], a_r.at[slot], dev)
        c.start()
        part_copies[slot] = c
        if slot not in (1, 3):
            sends.append(c)

    upper, lower = pl.ds(0, width // 2), pl.ds(width // 2, width // 2)
    root, cubic = 0.7978845608028654, 0.044715
    for k in (3, 1, 2, 0):
        f = col(k)
        units = pl.ds(pl.multiple_of(f * block, block), block)

        def expand(cut, f=f, units=units):
            u = _dot(n2[cut, :], weh[:, units], 1, 0) + ebias[:, units]
            t = jnp.tanh(root * (u + cubic * (u * u * u)))
            act[f, cut, :] = (0.5 * u * (1.0 + t)).astype(BF)
            rise = root * (1.0 + 3.0 * cubic * (u * u))
            slope[f, cut, :] = (0.5 * (1.0 + t) + 0.5 * u * (1.0 - t * t) * rise).astype(BF)

        loop(both, 256, expand)

        def reduce_grad(cut, f=f):
            zw[f, cut, :] = _dot(tt[cut, :], act[f], 1, 0).astype(BF)

        loop(width, 256, reduce_grad)
        if k == 3:
            part_send(1, zw.at[f, upper], r1.at[1], x_to)
            part_send(3, zw.at[f, lower], r1.at[3], y_to)
        elif k == 1:
            part_send(0, zw.at[f, upper], r1.at[0], x_to)
        elif k == 2:
            part_send(2, zw.at[f, lower], r1.at[2], y_to)

    for c in range(4):
        cut = slice(c * step, (c + 1) * step)
        tt[:, cut] = jnp.transpose(n2[cut, :])

    for c in w_local:
        c.wait()
    for c in w_parts:
        c.wait_recv()

    def reduced(cut):
        value = _dot(act[0, cut, :], wrh[:block, :], 1, 0)
        for f in range(1, ncol):
            value = value + _dot(act[f, cut, :], wrh[f * block : (f + 1) * block, :], 1, 0)
        return value

    o_copies = []
    for c in range(2):
        xs_o[cuts[c], :] = reduced(theirs[c]).astype(BF)
        cut = pl.ds(c * step, step)
        o_copies.append(rcopy(xs_o.at[cut], xr_o.at[cut], o_s.at[c], o_r.at[c], core_to))
        o_copies[c].start()
    swap_remote, swap_local = [], []
    for c in range(2):
        value = resid[cuts[c], :] + reduced(cuts[c]) + vec[3:4, :]
        o_copies[c].wait_recv()
        xr_o[cuts[c], :] = (value + xr_o[cuts[c], :].astype(F32)).astype(BF)
        cut = pl.ds(c * step, step)
        r = rcopy(xr_o.at[cut], out.at[cut], sw_s.at[c], sw_r.at[c], swap_to)
        stay = pltpu.make_async_copy(xr_o.at[cut], out.at[cut], sw_l.at[c])
        swap_remote.append(r)
        swap_local.append(stay)

        @pl.when(jnp.logical_not(stays))
        def _(r=r):
            r.start()

        @pl.when(stays)
        def _(stay=stay):
            stay.start()

    def forward(k, slot, first, index, dev):
        part_copies[slot].wait_recv()
        f = col(k)

        def add(cut):
            place = pl.ds(pl.multiple_of(cut.start + first, 128), 128)
            zw[f, place, :] = (zw[f, place, :].astype(F32) + r1[slot, cut, :].astype(F32)).astype(BF)

        loop(width // 2, 128, add)
        part_send(4 + index, zw.at[f, upper if first == 0 else lower], r2.at[index], dev)

    forward(2, 1, 0, 0, y_to)
    forward(1, 3, width // 2, 1, x_to)

    spare = col(3)
    q2, q4 = block // 2, block // 4

    def lanes(first, size):
        return pl.ds(pl.multiple_of(first, 128), size)

    z_copies = []

    def plane_total(start_row, cs):
        place = pl.ds(start_row, 128)

        def of(part):
            cut = pl.ds(pl.multiple_of(start_row - part * (width // 2), 128), 128)
            return r1[2 * part, cut, cs].astype(F32) + r2[part, cut, cs].astype(F32)

        return place, lambda part: zw[column, place, cs].astype(F32) + of(part)

    def plane_sum():
        for slot in (0, 2, 4, 5):
            part_copies[slot].wait_recv()
        part_copies[1].wait_send()
        part_copies[3].wait_send()
        for part in range(2):

            def add(cut, part=part):
                row = pl.multiple_of(cut.start + part * (width // 2), 128)
                place, total = plane_total(row, lanes((1 - nearb) * q2, q2))
                zw[spare, place, :q2] = total(part).astype(BF)

            loop(width // 2, 128, add)
        z_copies.append(start(zw.at[spare, :, pl.ds(0, q2)], n_rc, z_s.at[0], z_r.at[0], near_to))

    def near_sum():
        z_copies[0].wait_recv()
        for part in range(2):

            def add(cut, part=part):
                row = pl.multiple_of(cut.start + part * (width // 2), 128)
                place, total = plane_total(row, lanes(nearb * q2 + (1 - half) * q4, q4))
                value = total(part) + n_rc[place, lanes((1 - half) * q4, q4)].astype(F32)
                zw[spare, place, q2 : q2 + q4] = value.astype(BF)

            loop(width // 2, 128, add)
        z_copies.append(start(zw.at[spare, :, pl.ds(q2, q4)], f_rc, z_s.at[1], z_r.at[1], far_to))

    low = width // ncol // 2
    e_copies = {}

    def shard(k, part):
        return pl.ds(pl.multiple_of(col(k) * (2 * low) + part * low, low), low)

    def e_send(f, slot, src, dst, dev):
        e_copies[f, slot] = start(src, dst, e_s.at[f, slot], e_r.at[f, slot], dev)

    for f in range(ncol):
        units = slice(f * block, (f + 1) * block)
        esum[:, units] = jnp.zeros((1, block), F32)

        def expand_back(cut, f=f, units=units):
            da = _dot(gl[cut, :], wrh[units, :], 1, 1) * slope[f, cut, :].astype(F32)
            esum[:, units] += jnp.sum(da, axis=0, keepdims=True)
            act[f, cut, :] = da.astype(BF)

        loop(both, 256, expand_back)

        def expand_grad(cut, f=f):
            ws[f, cut, :] = _dot(tt[cut, :], act[f], 1, 0).astype(BF)

        loop(width, 256, expand_grad)
        e_send(f, 1, ws.at[f, shard(3, 0)], e1.at[f, 1], x_to)
        e_send(f, 3, ws.at[f, shard(3, 1)], e1.at[f, 3], y_to)
        e_send(f, 0, ws.at[f, shard(1, 0)], e1.at[f, 0], x_to)
        e_send(f, 2, ws.at[f, shard(2, 1)], e1.at[f, 2], y_to)

        if f == 1:
            plane_sum()
        elif f == 3:
            near_sum()

    def e_forward(f):
        for index, (k, dev) in enumerate(((2, y_to), (1, x_to))):
            e_copies[f, 1 + 2 * index].wait_recv()
            place = shard(k, index)
            ws[f, place, :] = (ws[f, place, :].astype(F32) + e1[f, 1 + 2 * index].astype(F32)).astype(BF)
            e_send(f, 4 + index, ws.at[f, place], e2.at[f, index], dev)

    def normed_grad(cut):
        value = None
        for f in range(ncol):
            one = _dot(act[f, cut, :], weh[:, f * block : (f + 1) * block], 1, 1)
            value = one if value is None else value + one
        return value

    d_copies = []
    for c in range(2):
        o_copies[c].wait_send()
        xs_o[cuts[c], :] = normed_grad(theirs[c]).astype(BF)
        cut = pl.ds(c * step, step)
        d_copies.append(start(xs_o.at[cut], xr_d.at[cut], d_s.at[c], d_r.at[c], core_to))
    e_forward(0)
    at_copy.wait_recv()
    for c in range(2):
        tt[:, cuts[c]] = jnp.transpose(attn[cuts[c], :])
        tt[:, theirs[c]] = jnp.transpose(attb[cuts[c], :])

    zero = jnp.zeros((1, width), F32)
    gain_sum, shift_sum, out_sum, red_sum = zero, zero, zero, zero
    gr_copies = []
    for c in range(2):
        dy = normed_grad(cuts[c])
        d_copies[c].wait_recv()
        dy = dy + xr_d[cuts[c], :].astype(F32)
        value = resid[cuts[c], :]
        center = value - jnp.mean(value, axis=-1, keepdims=True)
        rstd = lax.rsqrt(jnp.mean(center * center, axis=-1, keepdims=True) + EPS)
        hat = center * rstd
        gain_sum = gain_sum + jnp.sum(dy * hat, axis=0, keepdims=True)
        shift_sum = shift_sum + jnp.sum(dy, axis=0, keepdims=True)
        dh = dy * gain
        inner = dh - jnp.mean(dh, axis=-1, keepdims=True) - hat * jnp.mean(dh * hat, axis=-1, keepdims=True)
        base = gl[cuts[c], :].astype(F32)
        total = base + rstd * inner
        red_sum = red_sum + jnp.sum(base, axis=0, keepdims=True)
        out_sum = out_sum + jnp.sum(total, axis=0, keepdims=True)
        gres[cuts[c], :] = total
        low_rows = total.astype(BF)
        left, right = low_rows[:, : width // 2], low_rows[:, width // 2 :]
        gr[cuts[c], :] = jnp.where(core == 0, left, right)
        gs[cuts[c], :] = jnp.where(core == 0, right, left)
        cut = pl.ds(c * step, step)
        gr_copies.append(start(gs.at[cut], gr.at[pl.ds(n_rows + c * step, step)], gr_s.at[c], gr_r.at[c], core_to))
        ga[cuts[c], :] = _dot(low_rows, wo[...], 1, 1).astype(BF)
        e_forward(1 + c)
    vsum[0:1, :] = gain_sum
    vsum[1:2, :] = shift_sum
    vsum[2:3, :] = out_sum
    vsum[3:4, :] = red_sum
    vsum[4:8, :] = jnp.zeros((4, width), F32)
    for c in gr_copies:
        c.wait_recv()
    def output_grad(cut):
        dwo[cut, :] = _dot(tt[cut, :], gr[...], 1, 0).astype(BF)

    loop(width, 256, output_grad)
    e_forward(3)

    for f in range(ncol):
        for part in range(2):
            e_copies[f, 2 * part].wait_recv()
            e_copies[f, 4 + part].wait_recv()
            fe[part * low : (part + 1) * low, f * block : (f + 1) * block] = (
                ws[f, shard(0, part), :].astype(F32)
                + e1[f, 2 * part].astype(F32)
                + e2[f, part].astype(F32)
            )

    z_copies[1].wait_recv()

    for part in range(2):

        def quarter(cut, part=part):
            row = pl.multiple_of(cut.start + part * (width // 2), 128)
            place, total = plane_total(row, lanes(nearb * q2 + half * q4, q4))
            value = total(part) + n_rc[place, lanes(half * q4, q4)].astype(F32) + f_rc[place, :].astype(F32)
            fq[place, :] = value.astype(BF)

        loop(width // 2, 128, quarter)

    @pl.when(jnp.logical_not(stays))
    def _():
        for c in swap_remote:
            c.wait()

    @pl.when(stays)
    def _():
        for c in swap_local:
            c.wait()

    for c in sends:
        c.wait_send()


def middle(attn, wo, x, gl, weh, wrf, vec, ebias, nd):
    n_rows, width = x.shape
    own, ncol = weh.shape[1], nd // 2
    block = own // ncol
    any_, vmem = pl.BlockSpec(memory_space=pl.ANY), pl.BlockSpec(memory_space=pltpu.VMEM)
    dma = lambda *shape: pltpu.SemaphoreType.DMA(shape)
    one = pltpu.SemaphoreType.DMA
    sds = jax.ShapeDtypeStruct
    vm = lambda dtype, *shape: pltpu.VMEM(shape, dtype)
    both = 2 * n_rows
    return pl.pallas_call(
        functools.partial(middle_kernel, nd=nd),
        in_specs=[vmem] * 5 + [any_, vmem, vmem],
        out_specs=[any_, vmem, vmem, vmem, vmem, vmem, vmem, vmem],
        out_shape=[
            sds(x.shape, BF), sds(x.shape, F32), sds(x.shape, BF), sds((width // ncol, own), F32),
            sds((width, width // 2), BF), sds((width, block // 4), BF), sds((8, width), F32), sds((1, own), F32),
        ],
        scratch_shapes=[
            vm(BF, n_rows, width), vm(BF, own, width), vm(F32, n_rows, width), vm(BF, both, width),
            vm(BF, width, both), vm(BF, ncol, both, block), vm(BF, ncol, both, block),
            vm(BF, ncol, width, block), vm(BF, 4, width // 2, block), vm(BF, 2, width // 2, block),
            vm(BF, ncol, width, block), vm(BF, ncol, 4, width // ncol // 2, block),
            vm(BF, ncol, 2, width // ncol // 2, block), vm(BF, both, width // 2), vm(BF, n_rows, width // 2),
            vm(BF, n_rows, width), vm(BF, n_rows, width), vm(BF, n_rows, width),
            vm(BF, width, block // 2), vm(BF, width, block // 4),
            dma(2), dma(2), one, one, dma(2), dma(2), dma(2), dma(2), dma(2), dma(2), dma(2), dma(2), dma(2),
            dma(6), dma(6), dma(ncol, 6), dma(ncol, 6), dma(2), dma(2), dma(2), dma(2), dma(3),
        ],
        compiler_params=pltpu.CompilerParams(
            collective_id=2, has_side_effects=True, vmem_limit_bytes=61 << 20
        ),
        cost_estimate=pl.CostEstimate(
            flops=12 * both * width * own, bytes_accessed=40_000_000, transcendentals=2 * both * own
        ),
    )(attn, wo, x, gl, weh, wrf, vec, ebias)


def back_kernel(
    ga, qkv, att, lse, st, n1t, wf, x, gres, gain, v_in, res, dwr, dwe, dwo,
    out, tg, insum, osum, esum, rsum, vout,
    go, qt, dot, kt, dqt, delta, gm, zin, far_in, tot, tot2, near_in, core_in, cst, crc, nst, nrc, tgs,
    vmine, vrc, vz, own, fwd, r1, r2, ns_st, ns_rc, keep, fs_st, fs_rc, fb, eb, sum_two,
    move_s, move_r, move_l, a_s, a_r, a_l, d_s, d_r, out_s, out_r, out_l, tg_s, tg_r, tg_l, v_s, v_r, vz_s, vz_r, l_s, l_r,
    *, ns, nd, heads, d, bq, bk, chunks,
):
    seq, me = lax.axis_index("seq"), lax.axis_index("dp")
    half, nearb, core = seq // 2, seq % 2, me % 2
    member = 2 * core + nearb
    beside, twin, across = 2 * core + 1 - nearb, 2 * (1 - core) + nearb, 2 * (1 - core) + 1 - nearb
    n_rows, width = x.shape
    n, group, ncol = ns * n_rows, width // 4, nd // 2
    stays = half == core
    swap_to = (2 * core + nearb, me - core + half)
    near_to = (seq + 1 - 2 * nearb, me)
    far_to = (seq + 2 - 4 * half, me)
    third_to = (seq + 1 - 2 * nearb + 2 - 4 * half, me)
    core_to = (seq, me + 1 - 2 * core)

    def offset(k):
        result = me
        bit = 1
        while bit <= k:
            if k & bit:
                result = result + bit - 2 * bit * ((me // bit) % 2)
            bit *= 2
        return result

    def rcopy(src, dst, ss, rs, dev):
        return pltpu.make_async_remote_copy(
            src_ref=src, dst_ref=dst, send_sem=ss, recv_sem=rs, device_id=dev, device_id_type=MESH
        )

    def row_loop(total, size, body):
        size = 64 if total % 64 == 0 else size

        def one(t, carry):
            body(pl.multiple_of(t * size, size))
            return carry

        lax.fori_loop(0, total // size, one, 0)

    barrier = pltpu.get_barrier_semaphore()

    def hello(dev):
        pl.semaphore_signal(barrier, inc=1, device_id=dev, device_id_type=MESH)

    for k in range(1, nd):
        hello((seq, offset(k)))
    for dev in (near_to, far_to, third_to, (near_to[0], core_to[1])):
        hello(dev)

    @pl.when(jnp.logical_not(stays))
    def _():
        hello(swap_to)
        pl.semaphore_wait(barrier, nd + 4)

    @pl.when(stays)
    def _():
        pl.semaphore_wait(barrier, nd + 3)

    sends = []
    held = {}

    moves = []
    for i in range(4):
        src = ga.at[:, pl.ds(i * group, group)]
        mine = go.at[pl.ds(pl.multiple_of(member * n_rows, n_rows), n_rows)]
        dev = (seq - nearb + i % 2, me - core + i // 2)
        r = rcopy(src, mine, move_s.at[i], move_r.at[member], dev)
        stay = pltpu.make_async_copy(src, mine, move_l)
        moves.append((r, stay))

        @pl.when(member != i)
        def _(r=r):
            r.start()

        @pl.when(member == i)
        def _(stay=stay):
            stay.start()

    terms = (dwr, dwe, dwo, zin)
    pre = nd == 8
    high = [t.shape[0] // (1 if pre and a < 2 else ncol) for a, t in enumerate(terms)]
    wide = [t.shape[1] * (4 if pre and a == 0 else 1) for a, t in enumerate(terms)]

    def block(a, kc, part=None):
        row = (offset(2 * kc) // 2) * high[a]
        if part is None:
            return terms[a].at[pl.ds(pl.multiple_of(row, high[a]), high[a])]
        low = high[a] // 2
        return terms[a].at[pl.ds(pl.multiple_of(row + part * low, low), low)]

    def send(a, slot, src, dst, dev):
        c = rcopy(src, dst, a_s.at[a, slot], a_r.at[a, slot], dev)
        c.start()
        held[a, slot] = c
        sends.append(c)

    def rows_at_once(total):
        return 64 if total % 64 == 0 else 16

    def lanes(first, size):
        return pl.ds(pl.multiple_of(first, 128), size)

    def s0(a):
        local = [pltpu.make_async_copy(block(a, 0), own[a], a_l.at[a, 0])]
        if nd == 8:
            x_to, y_to = (seq, offset(2)), (seq, offset(4))
            send(a, 0, block(a, 1, 0), r1[a].at[0], x_to)
            send(a, 2, block(a, 2, 1), r1[a].at[2], y_to)
            send(a, 1, block(a, 3, 0), r1[a].at[1], x_to)
            send(a, 3, block(a, 3, 1), r1[a].at[3], y_to)
            local.append(pltpu.make_async_copy(block(a, 2, 0), fwd[a].at[0], a_l.at[a, 1]))
            local.append(pltpu.make_async_copy(block(a, 1, 1), fwd[a].at[1], a_l.at[a, 2]))
        else:
            for kc in range(1, ncol):
                send(a, kc, block(a, kc), r1[a].at[kc - 1], (seq, offset(2 * kc)))
        for c in local:
            c.start()
        held[a, "local"] = local

    def s1(a):
        for c in held[a, "local"]:
            c.wait()
        span = rows_at_once(high[a] // 2)
        if nd == 8:
            for part, k in ((0, 4), (1, 2)):
                held[a, 1 + 2 * part].wait_recv()

                def add(t, part=part):
                    cut = pl.ds(t, rows_at_once(span))
                    fwd[a][part, cut, :] = (
                        fwd[a][part, cut, :].astype(F32) + r1[a][1 + 2 * part, cut, :].astype(F32)
                    ).astype(BF)

                row_loop(high[a] // 2, 16, add)
                send(a, 4 + part, fwd[a].at[part], r2[a].at[part], (seq, offset(k)))

    def s2(a):
        c, low = wide[a], high[a] // 2
        if pre and a < 2:
            pass
        elif nd == 8:
            for slot in (0, 2, 4, 5):
                held[a, slot].wait_recv()
        else:
            for kc in range(1, ncol):
                held[a, kc].wait_recv()

        span = rows_at_once(low)

        def total(part, t, cs):
            cut = pl.ds(part * low + t, span)
            if pre and a == 1:
                return terms[a][cut, cs]
            value = own[a][cut, cs].astype(F32)
            if nd == 8:
                return (
                    value
                    + r1[a][2 * part, pl.ds(t, span), cs].astype(F32)
                    + r2[a][part, pl.ds(t, span), cs].astype(F32)
                )
            for kc in range(1, ncol):
                value = value + r1[a][kc - 1, cut, cs].astype(F32)
            return value

        for part in range(2):

            def add(t, part=part):
                cut = pl.ds(part * low + t, span)
                if a == 3:
                    tot[cut, :] = total(part, t, slice(None)).astype(BF)
                else:
                    keep[a][cut, :] = total(part, t, lanes(nearb * (c // 2), c // 2))
                    ns_st[a][cut, :] = total(part, t, lanes((1 - nearb) * (c // 2), c // 2)).astype(BF)

            row_loop(low, 16, add)
        if a == 3:
            send(a, 6, tot, far_in, far_to)
        else:
            send(a, 6, ns_st[a], ns_rc[a], near_to)

    def s3(a):
        c, span = wide[a], rows_at_once(high[a])
        held[a, 6].wait_recv()
        if a == 3:

            def add(t):
                cut = pl.ds(t, rows_at_once(span))
                tot2[cut, :] = (tot[cut, :].astype(F32) + far_in[cut, :].astype(F32)).astype(BF)

            row_loop(high[a], 16, add)
            send(a, 7, tot2, near_in, near_to)
            return

        def add(t):
            cut, cs = pl.ds(t, rows_at_once(high[a])), lanes((1 - half) * (c // 4), c // 4)
            fs_st[a][cut, :] = (keep[a][cut, cs] + ns_rc[a][cut, cs].astype(F32)).astype(BF)

        row_loop(high[a], 16, add)
        send(a, 7, fs_st[a], fs_rc[a], far_to)

    def s4(a):
        c = wide[a]
        if not (pre and a == 0):
            held[a, 7].wait_recv()
        low = high[a] // 2
        theirs = pl.ds(pl.multiple_of((1 - core) * low, low), low)
        if a == 3:
            send(a, 8, tot2.at[theirs], core_in.at[0], core_to)
            send(a, 9, near_in.at[theirs], core_in.at[1], core_to)
            return
        place = lanes(nearb * (c // 2) + half * (c // 4), c // 4)

        def add(t):
            cut, cs = pl.ds(t, rows_at_once(high[a])), lanes(half * (c // 4), c // 4)
            if pre and a == 0:
                fb[a][cut, place] = dwr[cut, :]
                return
            value = keep[a][cut, cs] + ns_rc[a][cut, cs].astype(F32) + fs_rc[a][cut, :].astype(F32)
            fb[a][cut, place] = value.astype(BF)

        row_loop(high[a], 16, add)
        send(a, 8, fb[a].at[:, place], fb[a].at[:, place], far_to)

    def s5(a):
        c = wide[a]
        held[a, 8].wait_recv()
        low = high[a] // 2
        ours = pl.ds(pl.multiple_of(core * low, low), low)
        if a == 3:
            held[a, 9].wait_recv()
            for which, value in (
                (member, tot2[ours, :]), (beside, near_in[ours, :]), (twin, core_in[0]), (across, core_in[1])
            ):
                for i in range(3):
                    insum[:, lanes(i * width + which * group, group)] = value[:, i * group : (i + 1) * group]
            return
        place = lanes(nearb * (c // 2), c // 2)
        send(a, 9, fb[a].at[:, place], fb[a].at[:, place], near_to)

    def s6(a):
        if pre and a > 0:
            l5(a)
        else:
            held[a, 9].wait_recv()
        low = high[a] // 2
        theirs = pl.ds(pl.multiple_of((1 - core) * low, low), low)
        if a == 0:
            if pre:
                return
            c = pltpu.make_async_copy(fb[a], rsum, a_l.at[a, 3])
            c.start()
            held[a, "last"] = c
        else:
            send(a, 10, fb[a].at[theirs], eb[a], core_to)

    def s7(a):
        if a == 0:
            if pre:
                rsum[...] = jnp.transpose(fb[a][...])
            else:
                held[a, "last"].wait()
            return
        held[a, 10].wait_recv()
        low = high[a] // 2
        ours = pl.ds(pl.multiple_of(core * low, low), low)
        if a == 2:
            size = wide[a]
            osum[:, lanes(core * size, size)] = fb[a][ours, :]
            osum[:, lanes((1 - core) * size, size)] = eb[a][...]
        else:
            size = wide[a] // ncol
            for i in range(ncol):
                cs = slice(i * size, (i + 1) * size)
                a0, a1 = fb[a][ours, cs], eb[a][:, cs]
                esum[:, 2 * i * size : (2 * i + 1) * size] = jnp.where(core == 0, a0, a1)
                esum[:, (2 * i + 1) * size : (2 * i + 2) * size] = jnp.where(core == 0, a1, a0)

    outer = nearb == half

    def line_copies(a, part):
        cs = slice(part * (wide[a] // 2), (part + 1) * (wide[a] // 2))
        make = lambda i, src, dst, dev: rcopy(
            src.at[:, cs], dst.at[:, cs], l_s.at[a - 1, 3 * part + i], l_r.at[a - 1, 3 * part + i], dev
        )
        return (
            make(0, ns_st[a], ns_rc[a], near_to),
            make(1, ns_st[a], fs_rc[a], third_to),
            make(2, fb[a], fb[a], near_to),
        )

    def l2(a):
        if a == 2:
            for slot in (0, 2, 4, 5):
                held[a, slot].wait_recv()
            low = high[a] // 2
            for part in range(2):
                cut = slice(part * low, (part + 1) * low)
                sum_two[cut, :] = (
                    own[a][cut, :].astype(F32) + r1[a][2 * part].astype(F32) + r2[a][part].astype(F32)
                )
        plane = terms[1] if a == 1 else sum_two

        @pl.when(outer)
        def _():
            for part in range(2):
                cs = slice(part * (wide[a] // 2), (part + 1) * (wide[a] // 2))

                def add(t, cs=cs):
                    cut = pl.ds(t, 64)
                    ns_st[a][cut, cs] = plane[cut, cs].astype(BF)

                row_loop(high[a], 64, add)
                line_copies(a, part)[0].start()

    def l3(a, part):
        plane = terms[1] if a == 1 else sum_two
        cs = slice(part * (wide[a] // 2), (part + 1) * (wide[a] // 2))

        @pl.when(jnp.logical_not(outer))
        def _():
            line_copies(a, part)[0].wait_recv()

            def add(t):
                cut = pl.ds(t, 64)
                ns_st[a][cut, cs] = (plane[cut, cs] + ns_rc[a][cut, cs].astype(F32)).astype(BF)

            row_loop(high[a], 64, add)
            line_copies(a, part)[1].start()

    def l4(a, part):
        cs = slice(part * (wide[a] // 2), (part + 1) * (wide[a] // 2))

        @pl.when(jnp.logical_not(outer))
        def _():
            line_copies(a, part)[1].wait_recv()

            def add(t):
                cut = pl.ds(t, 64)
                fb[a][cut, cs] = (ns_st[a][cut, cs].astype(F32) + fs_rc[a][cut, cs].astype(F32)).astype(BF)

            row_loop(high[a], 64, add)
            line_copies(a, part)[2].start()

    def l5(a):
        @pl.when(outer)
        def _():
            for part in range(2):
                line_copies(a, part)[2].wait_recv()

    def line_end(a):
        for part in range(2):
            copies = line_copies(a, part)

            @pl.when(outer)
            def _(copies=copies):
                copies[0].wait_send()

            @pl.when(jnp.logical_not(outer))
            def _(copies=copies):
                copies[1].wait_send()
                copies[2].wait_send()

    for a in (2,) if pre else (0, 1, 2):
        s0(a)
    if pre:
        s4(0)
    if not pre:
        out_remote = rcopy(res, out, out_s, out_r, swap_to)
        out_local = pltpu.make_async_copy(res, out, out_l)

        @pl.when(jnp.logical_not(stays))
        def _():
            out_remote.start()

        @pl.when(stays)
        def _():
            out_local.start()

    w, scale = 2 * d, d**-0.5
    for i in range(4):
        cut = slice(i * n_rows, (i + 1) * n_rows)
        qt[:, cut] = jnp.transpose(qkv[cut, :group])
        kt[:, cut] = jnp.transpose(qkv[cut, group : 2 * group])
    dqt[...] = jnp.zeros_like(dqt)
    for i in range(4):
        cut = slice(i * n_rows, (i + 1) * n_rows)
        landing = go.at[pl.ds(i * n_rows, n_rows)]
        arrival = pltpu.make_async_copy(landing, landing, move_r.at[i])
        r, stay = moves[i]

        @pl.when(member != i)
        def _(r=r, arrival=arrival):
            arrival.wait()
            r.wait_send()

        @pl.when(member == i)
        def _(stay=stay):
            stay.wait()

    if pre:
        l2(1)
    for i in range(4):
        cut = slice(i * n_rows, (i + 1) * n_rows)
        dot[:, cut] = jnp.transpose(go[cut, :])
        prod = jnp.transpose(go[cut, :].astype(F32) * att[cut, :].astype(F32))
        for h in range(heads):
            delta[h // 2, h % 2 : h % 2 + 1, cut] = jnp.sum(prod[h * d : (h + 1) * d], axis=0, keepdims=True)

    zero = jnp.zeros((), BF)
    for j in range(0, n, bk):

        def pair(p, carry, j=j):
            at = lambda first: pl.ds(pl.multiple_of(first + p * w, w), w)
            kb, vb = qkv[j : j + bk, at(group)], qkv[j : j + bk, at(2 * group)]
            dk = jnp.zeros((bk, w), F32)
            dv = jnp.zeros((bk, w), F32)
            row = lax.broadcasted_iota(jnp.int32, (w, bq), 0)
            lane = lax.broadcasted_iota(jnp.int32, (bq, w), 1)
            for i in range(j // bq, n // bq):
                cs = slice(i * bq, (i + 1) * bq)
                key = lax.broadcasted_iota(jnp.int32, (bk, bq), 0) + j
                ok = key >= st[:, cs]
                if j + bk > i * bq:
                    ok = ok & (key <= lax.broadcasted_iota(jnp.int32, (bk, bq), 1) + i * bq)
                for h in range(2):
                    rows_h = (row >= h * d) & (row < (h + 1) * d)
                    lanes_h = (lane >= h * d) & (lane < (h + 1) * d)
                    s = _dot(kb, jnp.where(rows_h, qt[at(0), cs], zero), 1, 0) * scale
                    s = jnp.where(ok, s, NEG)
                    e = jnp.exp(s - lse[p, h : h + 1, cs])
                    dp = _dot(vb, jnp.where(rows_h, dot[at(0), cs], zero), 1, 0)
                    ds = (e * (dp - delta[p, h : h + 1, cs])).astype(BF)
                    dv = dv + _dot(e.astype(BF), jnp.where(lanes_h, go[cs, at(0)], zero), 1, 0)
                    dk = dk + _dot(ds, jnp.where(lanes_h, qkv[cs, at(0)], zero), 1, 0)
                    head = pl.ds(pl.multiple_of(p * w + h * d, d), d)
                    dqt[head, cs] += _dot(kt[head, j : j + bk], ds, 1, 0)
            gm[j : j + bk, at(group)] = (dk * scale).astype(BF)
            gm[j : j + bk, at(2 * group)] = dv.astype(BF)
            return carry

        lax.fori_loop(0, heads // 2, pair, 0)
        if pre:
            if j == 0:
                l3(1, 0)
                s5(0)
                s1(2)
            elif j == bk:
                l3(1, 1)
                l4(1, 0)
                l2(2)
            elif j == 2 * bk:
                s6(0)
            else:
                l3(2, 0)
                l3(2, 1)
                l4(1, 1)
        elif j == 0:
            s1(0)
        elif j == bk:
            s2(0)
        elif j == 2 * bk:
            s3(0)
    for i in range(4):
        cut = slice(i * n_rows, (i + 1) * n_rows)
        gm[cut, :group] = (jnp.transpose(dqt[:, cut]) * scale).astype(BF)

    def input_grad():
        for i in range(4):
            cut = slice(i * group, (i + 1) * group)
            zin[cut, :] = _dot(n1t[cut, :], gm[...], 1, 0).astype(BF)
        s0(3)

    if pre:
        input_grad()

    step = n_rows // chunks

    def term(b, c):
        cut = pl.ds(pl.multiple_of(b * n_rows + c * step, step), step)
        return _dot(gm[cut, :], wf[...], 1, 1)

    quad = {}

    def quad_send(slot, src, dst, dev):
        c = rcopy(src, dst, d_s.at[slot], d_r.at[slot], dev)
        c.start()
        quad[slot] = c
        sends.append(c)

    for which, b in ((1, across), (0, twin)):
        for c in range(chunks):
            cut = pl.ds(c * step, step)
            cst[which, cut, :] = term(b, c).astype(BF)
            quad_send(which * chunks + c, cst.at[which, cut], crc.at[which, cut], core_to)
    for c in range(chunks):
        cut = pl.ds(c * step, step)
        value = term(beside, c)
        quad[chunks + c].wait_recv()
        nst[cut, :] = (value + crc[1, cut, :].astype(F32)).astype(BF)
        quad_send(2 * chunks + c, nst.at[cut], nrc.at[cut], near_to)

    if not pre:
        s1(1)
        s1(2)
        s4(0)
    if pre:
        l4(2, 0)
        l4(2, 1)
        s1(3)
        s2(3)
    else:
        input_grad()
        s5(0)

    tg_remote, tg_local = [], []
    gain_sum = jnp.zeros((1, width), F32)
    shift_sum = jnp.zeros((1, width), F32)
    for c in range(chunks):
        cut = pl.ds(c * step, step)
        value = term(member, c)
        quad[c].wait_recv()
        quad[2 * chunks + c].wait_recv()
        dy = value + crc[0, cut, :].astype(F32) + nrc[cut, :].astype(F32)
        rows_in = x[cut, :].astype(F32)
        center = rows_in - jnp.mean(rows_in, axis=-1, keepdims=True)
        rstd = lax.rsqrt(jnp.mean(center * center, axis=-1, keepdims=True) + EPS)
        hat = center * rstd
        gain_sum = gain_sum + jnp.sum(dy * hat, axis=0, keepdims=True)
        shift_sum = shift_sum + jnp.sum(dy, axis=0, keepdims=True)
        dh = dy * gain[...]
        inner = dh - jnp.mean(dh, axis=-1, keepdims=True) - hat * jnp.mean(dh * hat, axis=-1, keepdims=True)
        tgs[cut, :] = (gres[cut, :] + rstd * inner).astype(BF)
        r = rcopy(tgs.at[cut], tg.at[cut], tg_s.at[c], tg_r.at[c], swap_to)
        stay = pltpu.make_async_copy(tgs.at[cut], tg.at[cut], tg_l.at[c])
        tg_remote.append(r)
        tg_local.append(stay)

        @pl.when(jnp.logical_not(stays))
        def _(r=r):
            r.start()

        @pl.when(stays)
        def _(stay=stay):
            stay.start()

    small = v_in.shape[2]
    for k in range(nd):
        vmine[k] = v_in[k]
        vmine[k, 0:1, :] = gain_sum[:, k * small : (k + 1) * small]
        vmine[k, 1:2, :] = shift_sum[:, k * small : (k + 1) * small]
    vec = []
    for k in range(1, nd):
        c = rcopy(vmine.at[offset(k)], vrc.at[k], v_s.at[k], v_r.at[k], (seq, offset(k)))
        c.start()
        vec.append(c)
        sends.append(c)

    if not pre:
        s2(1)
        s2(2)
        s6(0)
        s1(3)
    total = vmine[me]
    for k, c in enumerate(vec):
        c.wait_recv()
        total = total + vrc[k + 1]
    vz[seq] = total
    z_copies = []
    for i, dev in enumerate((near_to, far_to, third_to)):
        c = rcopy(vz.at[seq], vz.at[seq], vz_s.at[i], vz_r.at[i], dev)
        c.start()
        z_copies.append(c)
        sends.append(c)
    if not pre:
        s3(1)
        s3(2)
        s2(3)
        s4(1)
        s4(2)
    s3(3)
    if not pre:
        s5(1)
        s5(2)
    s6(1)
    s6(2)
    s4(3)
    if pre:
        s7(0)
    s5(3)
    for c in z_copies:
        c.wait_recv()
    total = vz[0]
    for i in range(1, ns):
        total = total + vz[i]
    vout[...] = total
    for a in (1, 2) if pre else (0, 1, 2):
        s7(a)

    @pl.when(jnp.logical_not(stays))
    def _():
        if not pre:
            out_remote.wait()
        for c in tg_remote:
            c.wait()

    @pl.when(stays)
    def _():
        if not pre:
            out_local.wait()
        for c in tg_local:
            c.wait()

    for c in sends:
        c.wait_send()
    if pre:
        line_end(1)
        line_end(2)


def back(ga, qkv, att, lse, starts, n1t, wf, x, gres, gain, v_in, res, dwr, dwe, dwo, ns, nd, heads, d):
    n_rows, width = x.shape
    n, group, ncol, chunks = n_rows * ns, width // 4, nd // 2, 4
    any_, vmem = pl.BlockSpec(memory_space=pl.ANY), pl.BlockSpec(memory_space=pltpu.VMEM)
    dma = lambda *shape: pltpu.SemaphoreType.DMA(shape)
    one = pltpu.SemaphoreType.DMA
    sds = jax.ShapeDtypeStruct
    pre = nd == 8
    sizes = [(t.shape[0] // ncol, t.shape[1]) for t in (dwr, dwe, dwo)] + [(width // ncol, 3 * group)]
    plane = list(sizes)
    if pre:
        sizes[0], plane[0] = (width, 4 * dwr.shape[1]), (32, 128)
        sizes[1], plane[1] = dwe.shape, (32, 128)
    vm = lambda dtype, *shape: pltpu.VMEM(shape, dtype)

    def line(shift):
        if pre:
            return [(16, 128), *sizes[1:3]]
        return [(r, c >> shift) for r, c in sizes[:3]]

    slots = max(11, nd)
    rr, cc = width // nd, 3 * group
    return pl.pallas_call(
        functools.partial(back_kernel, ns=ns, nd=nd, heads=heads, d=d, bq=n_rows // 2, bk=n_rows, chunks=chunks),
        in_specs=[vmem] * 11 + [any_] + [vmem if pre else any_] * 2 + [any_],
        out_specs=[any_, any_, vmem, vmem, vmem, vmem if pre else any_, vmem],
        out_shape=[
            sds(res.shape, BF), sds(x.shape, BF), sds((rr, 3 * width), BF), sds((rr, width), BF),
            sds((rr, 2 * dwe.shape[1]), BF), sds(sizes[0][::-1] if pre else sizes[0], BF), sds(v_in.shape[1:], F32),
        ],
        scratch_shapes=[
            vm(BF, n, group), vm(BF, group, n), vm(BF, group, n), vm(BF, group, n), vm(F32, group, n),
            vm(F32, heads // 2, 2, n), vm(BF, n, 3 * group), vm(BF, width, 3 * group),
            vm(BF, 2 * rr, cc), vm(BF, 2 * rr, cc), vm(BF, 2 * rr, cc), vm(BF, 2 * rr, cc), vm(BF, 2, rr, cc),
            vm(BF, 2, n_rows, width), vm(BF, 2, n_rows, width), vm(BF, n_rows, width), vm(BF, n_rows, width),
            vm(BF, n_rows, width), vm(F32, *v_in.shape), vm(F32, *v_in.shape), vm(F32, ns, *v_in.shape[1:]),
            [vm(BF, r, c) for r, c in plane],
            [vm(BF, 2, r // 2, c) for r, c in plane],
            [vm(BF, 4, r // 2, c) if nd == 8 else vm(BF, ncol - 1, r, c) for r, c in plane],
            [vm(BF, 2, r // 2, c) for r, c in plane],
            [vm(BF, r, c) for r, c in line(1)], [vm(BF, r, c) for r, c in line(1)],
            [vm(F32, r, c // 2) if not pre else vm(F32, 8, 128) for r, c in sizes[:3]],
            [vm(BF, r, c // 4) if not pre else vm(BF, 16, 128) for r, c in sizes[:3]],
            [vm(BF, r, c) for r, c in line(2)],
            [vm(BF, r, c) for r, c in sizes[:3]], [vm(BF, r // 2, c) for r, c in sizes[:3]],
            vm(F32, *sizes[2]) if pre else vm(F32, 8, 128),
            dma(4), dma(4), one, dma(4, slots), dma(4, slots), dma(4, 4),
            dma(3 * chunks), dma(3 * chunks), one, one, one, dma(chunks), dma(chunks), dma(chunks),
            dma(nd), dma(nd), dma(3), dma(3), dma(2, 6), dma(2, 6),
        ],
        compiler_params=pltpu.CompilerParams(
            collective_id=1, has_side_effects=True, vmem_limit_bytes=60 << 20
        ),
        cost_estimate=pl.CostEstimate(
            flops=20 * n * n * d * heads, bytes_accessed=60_000_000, transcendentals=n * n * heads
        ),
    )(ga, qkv, att, lse, starts, n1t, wf, x, gres, gain, v_in, res, dwr, dwe, dwo)


def layer_normalize(values, gain, shift):
    center = values - jnp.mean(values, axis=-1, keepdims=True)
    spread = jnp.mean(center * center, axis=-1, keepdims=True)
    return center * lax.rsqrt(spread + EPS) * gain + shift


def smooth_gate(values):
    return jax.nn.gelu(values, approximate=True)


def rows(array, start, size):
    return lax.dynamic_slice_in_dim(array, start, size, 0)


def cols(array, start, size):
    return lax.dynamic_slice_in_dim(array, start, size, 1)


def put(array, piece, row, col):
    return lax.dynamic_update_slice(array, piece, (row, col))


def bf_round(x):
    return lax.reduce_precision(x, 8, 7)


class Links:
    def __init__(self, ns, nd):
        self.ns, self.nd = ns, nd

    def go(self, array, target):
        pairs = []
        for s in range(self.ns):
            for d in range(self.nd):
                ts, td = target(s, d)
                pairs.append((s * self.nd + d, ts * self.nd + td))
        return lax.ppermute(array, ("seq", "dp"), pairs)

    def dp(self, array, k):
        return self.go(array, lambda s, d: (s, d ^ k))

    def core(self, array):
        return self.dp(array, 1)

    def near(self, array):
        return self.go(array, lambda s, d: (s ^ 1, d))

    def far(self, array):
        return self.go(array, lambda s, d: (s ^ 2, d))

    def both(self, array):
        return self.go(array, lambda s, d: (s ^ 1, d ^ 1))

    def swap(self, array):
        return self.go(array, lambda s, d: (2 * (d % 2) + s % 2, d - d % 2 + s // 2))


def on_device(
    tokens, lengths, cotangent, mixer_input, mixer_output, expand_weight, reduce_weight,
    first_gain, first_shift, second_gain, second_shift, output_bias, expand_bias, reduce_bias,
):
    ns, nd = lax.axis_size("seq"), lax.axis_size("dp")
    links = Links(ns, nd)
    seq, me = lax.axis_index("seq"), lax.axis_index("dp")
    half, near_bit, core = seq // 2, seq % 2, me % 2
    column = me // 2
    member = 2 * core + near_bit
    n_rows, width = tokens.shape[1:]
    slots = n_rows * ns
    head_dim = width // HEADS
    hidden = reduce_weight.shape[0] * nd
    group = width // 4
    my_heads = HEADS // 4

    lengths_row = jnp.where(half == core, lengths[0], links.core(lengths)[0])
    entry = jnp.arange(lengths_row.shape[0])
    ends = jnp.sum(jnp.where(entry[None, :] <= entry[:, None], lengths_row[None, :], 0), axis=1)
    place = jnp.arange(slots, dtype=jnp.int32)
    passed = place[:, None] >= ends[None, :]
    starts = jnp.max(jnp.where(passed, ends[None, :], 0), axis=1)
    starts = jnp.where(place < ends[-1], starts, place).reshape(1, slots)
    live = (member * n_rows + jnp.arange(n_rows, dtype=jnp.int32) < ends[-1]).astype(F32)

    small, small_rows = width // nd, mixer_input.shape[0]
    wide = hidden // nd
    vectors = [first_gain, first_shift, second_gain, second_shift, output_bias, reduce_bias]
    vectors = [v[None] for v in vectors] + [expand_bias.reshape(-1, small)]
    vectors = jnp.concatenate([*vectors, jnp.zeros((16 - 6 - wide // small, small), BF)])
    by_core = expand_weight
    if wide % 128:
        by_core = expand_weight.reshape(small_rows, nd // 2, 2, wide).transpose(2, 0, 1, 3)
        by_core = by_core.reshape(2, small_rows, hidden // 2)
    (
        x_low, both_grad, normed_t, input_full, output_full, expand_half, reduce_half, vectors,
        qkv, attended, logsum, attention,
    ) = front(
        tokens[0], cotangent[0], mixer_input, mixer_output, by_core, reduce_weight, vectors,
        starts, ns, nd, my_heads, head_dim,
    )
    vectors = vectors.astype(F32)
    gain_one, _, gain_two, shift_two, output_add, reduce_add = (vectors[:, i].reshape(-1) for i in range(6))
    n_wide = wide // small
    expand_add = vectors[:, 6 : 6 + n_wide].reshape(nd // 2, 2, wide)
    expand_add = lax.dynamic_index_in_dim(expand_add, core, 1, keepdims=False).reshape(-1)

    twin_live = ((member ^ 2) * n_rows + jnp.arange(n_rows, dtype=jnp.int32) < ends[-1]).astype(F32)
    if nd == 8:
        vec = jnp.stack([gain_two, shift_two, output_add, reduce_add])
        vec = jnp.concatenate([vec, jnp.zeros_like(vec)])
        both_live = jnp.concatenate([live, twin_live])[:, None]
        both_grad = jnp.where(both_live > 0, both_grad, jnp.zeros((), BF))
        result, grad_resid, grad_attention, expand_term, output_term, reduce_term, row_sums, wide_sums = middle(
            attention, output_full, x_low, both_grad, expand_half, reduce_half, vec, expand_add[None], nd,
        )
        gain_two_sum, shift_two_sum, output_bias_sum, reduce_bias_sum = (row_sums[i] for i in range(4))
        expand_bias_sum = wide_sums[0]
        layer_output, result = result, jnp.zeros((16, 128), BF)
    else:
        grad_low, twin_grad = both_grad[:n_rows], both_grad[n_rows:]
        twin_attention = links.core(attention)
        inputs = x_low.astype(F32)
        resid = inputs + mm(attention, output_full) + output_add
        normed_two = layer_normalize(resid, gain_two, shift_two).astype(BF)
        normed_two = jnp.concatenate([normed_two, links.core(normed_two)])
        expanded = mm(normed_two, expand_half) + expand_add
        active = smooth_gate(expanded).astype(BF)
        reduced = mm(active, reduce_half)
        twin_part = links.core(reduced[n_rows:].astype(BF)).astype(F32)
        result = (resid + reduced[:n_rows] + twin_part + reduce_add).astype(BF)
        grad_result = grad_low.astype(F32) * live[:, None]
        result_low = jnp.concatenate([grad_result.astype(BF), (twin_grad.astype(F32) * twin_live[:, None]).astype(BF)])
        reduce_term = mm_left(active, result_low).astype(BF)
        reduce_bias_sum = jnp.sum(grad_result, axis=0)
        grad_active = mm_right(result_low, reduce_half)
        _, gate_back = jax.vjp(smooth_gate, expanded)
        grad_expanded = gate_back(grad_active)[0]
        expand_bias_sum = jnp.sum(grad_expanded, axis=0)
        expanded_low = grad_expanded.astype(BF)
        expand_term = mm_left(normed_two, expanded_low).astype(BF)
        grad_normed = mm_right(expanded_low, expand_half)
        grad_normed_two = grad_normed[:n_rows] + links.core(grad_normed[n_rows:].astype(BF)).astype(F32)
        _, second_back = jax.vjp(layer_normalize, resid, gain_two, shift_two)
        resid_part, gain_two_sum, shift_two_sum = second_back(grad_normed_two)
        grad_resid = grad_result + resid_part
        output_bias_sum = jnp.sum(grad_resid, axis=0)
        resid_low = grad_resid.astype(BF)
        grad_attention = mm_right(resid_low, output_full).astype(BF)
        both_low = jnp.concatenate([resid_low, links.core(resid_low)])
        both_low = cols(both_low, core * (width // 2), width // 2)
        output_term = mm_left(jnp.concatenate([attention, twin_attention]), both_low).astype(BF)

    sums = jnp.stack([gain_two_sum, shift_two_sum, output_bias_sum, reduce_bias_sum])
    sums = sums.reshape(4, nd, small).transpose(1, 0, 2)
    wide_sum = expand_bias_sum.reshape(nd // 2, 1, n_wide, small)
    parity = jnp.arange(2).reshape(1, 2, 1, 1)
    wide_sum = jnp.where(parity == core, wide_sum, 0.0).reshape(nd, n_wide, small)
    pad = -(6 + n_wide) % 8
    sums = jnp.concatenate([jnp.zeros((nd, 2, small)), sums, wide_sum, jnp.zeros((nd, pad, small))], axis=1)

    swapped, tokens_gradient, input_sum, output_sum, expand_sum, reduce_sum, sums = back(
        grad_attention, qkv, attended, logsum, starts, normed_t, input_full, x_low, grad_resid,
        gain_one.reshape(1, width), sums, result, reduce_term, expand_term, output_term,
        ns, nd, my_heads, head_dim,
    )
    if nd != 8:
        layer_output = swapped
    return (
        layer_output[None],
        tokens_gradient.astype(F32)[None],
        input_sum.astype(F32),
        output_sum.astype(F32),
        expand_sum.astype(F32),
        reduce_sum.astype(F32),
        sums[0],
        sums[1],
        sums[2],
        sums[3],
        sums[4],
        sums[6 : 6 + n_wide].reshape(-1),
        sums[5],
    )


def solution(mesh):
    row, vec = P("dp", None), P("dp")
    act = P("dp", "seq", None)
    return jax.shard_map(
        on_device,
        mesh=mesh,
        in_specs=(act, row, act, row, row, row, row, vec, vec, vec, vec, vec, vec, vec),
        out_specs=(act, act, row, row, row, row, vec, vec, vec, vec, vec, vec, vec),
        check_vma=False,
    )
```

```python
import functools

import jax
import jax.numpy as jnp
from jax import lax
from jax.experimental import pallas as pl
from jax.experimental.pallas import tpu as pltpu
from jax.sharding import PartitionSpec as P

HEADS = 16
EPS = 1e-05
NEG = -1e30
F32 = jnp.float32
BF = jnp.bfloat16


def _dot(a, b, ca, cb):
    return lax.dot_general(a, b, (((ca,), (cb,)), ((), ())), preferred_element_type=F32)


def mm(a, b):
    return _dot(a, b, 1, 0)


def mm_left(a, b):
    return _dot(a, b, 0, 0)


def mm_right(a, b):
    return _dot(a, b, 1, 1)


MESH = pl.DeviceIdType.MESH


def front_kernel(
    tok, cot, win, wo, we, wr, vec, st,
    x_ref, gg_ref, n1t, wf, wof, wef, wrf, vecs, qkv, att, lse, attn,
    n1, qt, vt, win_s, win_r, vec_s, vec_r, tok_s, tok_r, tok_l, near_s, near_r, core_s, core_r, fwd_s, fwd_r,
    cot_s, cot_r, cot_l, gp_s, gp_r, own_l, w_s, w_r, move_s, move_r, move_l,
    *, ns, nd, heads, d, bq, bk, chunks,
):
    seq, me = lax.axis_index("seq"), lax.axis_index("dp")
    half, nearb, core = seq // 2, seq % 2, me % 2
    member = 2 * core + nearb
    n_rows, width = tok.shape
    g_ref, gp_ref = gg_ref.at[pl.ds(0, n_rows)], gg_ref.at[pl.ds(n_rows, n_rows)]
    group = width // 4
    small_rows = win.shape[0]
    stays = half == core
    swap_to = (2 * core + nearb, me - core + half)
    near_to = (seq + 1 - 2 * nearb, me)
    core_to = (seq, me + 1 - 2 * core)

    def offset(k):
        out = me
        bit = 1
        while bit <= k:
            if k & bit:
                out = out + bit - 2 * bit * ((me // bit) % 2)
            bit *= 2
        return out

    def rcopy(src, dst, ss, rs, dev):
        return pltpu.make_async_remote_copy(
            src_ref=src, dst_ref=dst, send_sem=ss, recv_sem=rs, device_id=dev, device_id_type=MESH
        )

    barrier = pltpu.get_barrier_semaphore()

    def hello(dev):
        pl.semaphore_signal(barrier, inc=1, device_id=dev, device_id_type=MESH)

    for k in range(1, nd):
        hello((seq, offset(k)))
    hello(near_to)
    hello((near_to[0], core_to[1]))

    @pl.when(jnp.logical_not(stays))
    def _():
        hello(swap_to)
        pl.semaphore_wait(barrier, nd + 2)

    @pl.when(stays)
    def _():
        pl.semaphore_wait(barrier, nd + 1)

    sends = []

    step = n_rows // chunks
    tok_remote, tok_local = [], []
    for c in range(chunks):
        cut = pl.ds(c * step, step)
        tok_remote.append(rcopy(tok.at[cut], x_ref.at[cut], tok_s.at[c], tok_r.at[c], swap_to))
        tok_local.append(pltpu.make_async_copy(tok.at[cut], x_ref.at[cut], tok_l.at[c]))

    @pl.when(jnp.logical_not(stays))
    def _():
        for c in tok_remote:
            c.start()

    @pl.when(stays)
    def _():
        for c in tok_local:
            c.start()

    vec_copies, win_copies, own_copies = [], [], []
    for k in range(1, nd):
        c = rcopy(vec, vecs.at[me], vec_s.at[k], vec_r.at[k], (seq, offset(k)))
        c.start()
        vec_copies.append(c)
    c = pltpu.make_async_copy(vec, vecs.at[me], own_l.at[0])
    c.start()
    vec_copies.append(c)
    my_rows = pl.ds(pl.multiple_of(me * small_rows, small_rows), small_rows)
    for k in range(nd):
        target = 2 * (core if k % 2 == 0 else 1 - core) + nearb
        for i in range(3):
            src = win.at[:, pl.ds(pl.multiple_of(i * width + target * group, 128), group)]
            dst = wf.at[my_rows, pl.ds(i * group, group)]
            if k == 0:
                c = pltpu.make_async_copy(src, dst, own_l.at[1 + i])
            else:
                c = rcopy(src, dst, win_s.at[k, i], win_r.at[k, i], (seq, offset(k)))
            c.start()
            win_copies.append(c)

    pairs = ((wo, wof), (we, wef), (wr, wrf))

    split = len(we.shape) == 2

    def source(a, k):
        return we.at[core if k % 2 == 0 else 1 - core] if a == 1 else pairs[a][0]

    def blocks(k, dst):
        size = wef.shape[1] // (nd // 2)
        which = core if k % 2 == 0 else 1 - core
        for i in range(nd // 2):
            src = we.at[:, pl.ds(pl.multiple_of((2 * i + which) * size, 128), size)]
            yield src, dst.at[:, pl.ds(i * size, size)]

    def at(a, k, part=None):
        high = pairs[a][0].shape[-2]
        row = (offset(k) // 2 if a == 2 else offset(k)) * high
        if part is None:
            return pairs[a][1].at[pl.ds(pl.multiple_of(row, high), high)]
        return pairs[a][1].at[pl.ds(pl.multiple_of(row + part * (high // 2), high // 2), high // 2)]

    held = {}

    def send(a, slot, src, dst, k):
        c = rcopy(src, dst, w_s.at[a, slot], w_r.at[a, slot], (seq, offset(k)))
        c.start()
        held[a, slot] = c

    def send_shard(a, k):
        if a != 1 or not split:
            send(a, k, source(a, k), at(a, 0), k)
            return
        dev = (seq, offset(k))
        for src, dst in blocks(k, at(a, 0)):
            rcopy(src, dst, w_s.at[a, k], w_r.at[a, k], dev).start()
        held[a, k] = rcopy(at(a, 0), at(a, 0), w_s.at[a, k], w_r.at[a, k], dev)

    direct = (2, 3, 4, 5) if nd == 8 else range(2, nd)

    def weights_start(a):
        for k in direct:
            if k % 2 == 0 or a == 1:
                send_shard(a, k)
        if a < 2:
            send_shard(a, 1)
        if a == 1 and split:
            for src, dst in blocks(0, at(a, 0)):
                pltpu.make_async_copy(src, dst, own_l.at[4 + a]).start()
            held[a, "own"] = pltpu.make_async_copy(at(a, 0), at(a, 0), own_l.at[4 + a])
        else:
            c = pltpu.make_async_copy(source(a, 0), at(a, 0), own_l.at[4 + a])
            c.start()
            held[a, "own"] = c

    def weights_forward(a):
        for k in direct:
            if k % 2 == 0 or a == 1:
                held[a, k].wait_recv()
                if nd == 8 and a < 2:
                    send(a, 8 + k, at(a, k, k // 4), at(a, k, k // 4), 6 - k // 2 * 2)
                if a == 0:
                    send(a, k + 1 if nd > 8 else 14 + k // 2, at(a, k), at(a, k), 1)

    def weights_last(a):
        if nd == 8 and a == 0:
            for part, k in ((0, 2), (1, 4)):
                held[a, 8 + k].wait_recv()
                send(a, 3 + 2 * part, at(a, 6, part), at(a, 6, part), 1)

    def weights_end(a):
        held[a, "own"].wait()
        waited = set(direct) if a else {k for k in direct if k % 2 == 0}
        if nd == 8 and a == 0:
            waited |= {10, 12}
        for (b, slot), c in held.items():
            if b == a and slot != "own":
                if slot not in waited:
                    c.wait_recv()
                c.wait_send()

    for a in range(3):
        weights_start(a)

    for c in vec_copies[:-1]:
        c.wait_recv()
        sends.append(c)
    vec_copies[-1].wait()

    def vector(i):
        return jnp.concatenate([vecs[k, i : i + 1, :] for k in range(nd)], axis=1).astype(F32)

    gain, shift = vector(0), vector(1)
    near_copies, core_copies = [], []
    for c in range(chunks):
        cut = pl.ds(c * step, step)

        @pl.when(jnp.logical_not(stays))
        def _(c=c):
            tok_remote[c].wait_recv()

        @pl.when(stays)
        def _(c=c):
            tok_local[c].wait()

        value = x_ref[cut, :].astype(F32)
        center = value - jnp.mean(value, axis=-1, keepdims=True)
        spread = jnp.mean(center * center, axis=-1, keepdims=True)
        place = pl.ds(pl.multiple_of(member * n_rows + c * step, step), step)
        n1[place, :] = (center * lax.rsqrt(spread + EPS) * gain + shift).astype(BF)
        r = rcopy(n1.at[place], n1.at[place], near_s.at[c], near_r.at[c], near_to)
        r.start()
        near_copies.append(r)
        r = rcopy(n1.at[place], n1.at[place], core_s.at[c], core_r.at[c], core_to)
        r.start()
        core_copies.append(r)

    for c in win_copies[:3]:
        c.wait()
    for c in win_copies[3:]:
        c.wait_recv()
        sends.append(c)

    def project(block, c=None):
        size = n_rows if c is None else step
        place = pl.ds(pl.multiple_of(block * n_rows + (0 if c is None else c * step), size), size)
        mixed = _dot(n1[place, :], wf[...], 1, 0).astype(BF)
        qkv[place, :] = mixed
        n1t[:, place] = jnp.transpose(n1[place, :])
        qt[:, place] = jnp.transpose(mixed[:, :group])
        vt[:, place] = jnp.transpose(mixed[:, 2 * group :])

    project(member)
    for c in core_copies:
        c.wait_recv()
        sends.append(c)
    twin = 2 * (1 - core) + nearb
    project(twin)
    fwd_copies = []
    beside = 2 * core + 1 - nearb
    across = 2 * (1 - core) + 1 - nearb
    for c in range(chunks):
        near_copies[c].wait_recv()
        sends.append(near_copies[c])
        place = pl.ds(pl.multiple_of(beside * n_rows + c * step, step), step)
        r = rcopy(n1.at[place], n1.at[place], fwd_s.at[c], fwd_r.at[c], core_to)
        r.start()
        fwd_copies.append(r)
    project(beside)
    for c in fwd_copies:
        c.wait_recv()
        sends.append(c)
    project(across)

    cot_remote = rcopy(cot, g_ref, cot_s, cot_r, swap_to)
    cot_local = pltpu.make_async_copy(cot, g_ref, cot_l)

    @pl.when(jnp.logical_not(stays))
    def _():
        cot_remote.start()

    @pl.when(stays)
    def _():
        cot_local.start()

    n = ns * n_rows
    scale = d**-0.5
    w = 2 * d
    moves = []
    for i in range(n // bq):
        cs = slice(i * bq, (i + 1) * bq)

        def pair(p, carry, i=i, cs=cs):
            lanes = pl.ds(pl.multiple_of(p * w, w), w)
            key_lanes = pl.ds(pl.multiple_of(group + p * w, w), w)
            outs = []
            for h in range(2):
                row = lax.broadcasted_iota(jnp.int32, (w, bq), 0)
                qm = jnp.where((row >= h * d) & (row < (h + 1) * d), qt[lanes, cs], jnp.zeros((), BF))
                m = jnp.full((1, bq), NEG, F32)
                l = jnp.zeros((1, bq), F32)
                acc = jnp.zeros((d, bq), F32)
                for j in range(0, (i + 1) * bq, bk):
                    s = _dot(qkv[j : j + bk, key_lanes], qm, 1, 0) * scale
                    key = lax.broadcasted_iota(jnp.int32, (bk, bq), 0) + j
                    ok = key >= st[:, cs]
                    if j + bk > i * bq:
                        ok = ok & (key <= lax.broadcasted_iota(jnp.int32, (bk, bq), 1) + i * bq)
                    s = jnp.where(ok, s, NEG)
                    mn = jnp.maximum(m, jnp.max(s, axis=0, keepdims=True))
                    e = jnp.exp(s - mn)
                    a = jnp.exp(m - mn)
                    l = a * l + jnp.sum(e, axis=0, keepdims=True)
                    rows_h = pl.ds(pl.multiple_of(p * w + h * d, d), d)
                    acc = a * acc + _dot(vt[rows_h, j : j + bk], e.astype(BF), 1, 0)
                    m = mn
                outs.append(acc / l)
                lse[p, h : h + 1, cs] = m + jnp.log(l)
            att[cs, lanes] = jnp.transpose(jnp.concatenate(outs, axis=0)).astype(BF)
            return carry

        lax.fori_loop(0, heads // 2, pair, 0)
        mine = attn.at[:, pl.ds(pl.multiple_of(member * group, group), group)]
        dev = (seq - nearb + i % 2, me - core + i // 2)
        r = rcopy(att.at[cs], mine, move_s.at[i], move_r.at[member], dev)
        keep = pltpu.make_async_copy(att.at[cs], mine, move_l)
        moves.append((r, keep))

        @pl.when(member != i)
        def _(r=r):
            r.start()

        @pl.when(member == i)
        def _(keep=keep):
            keep.start()

        if i < 3:
            weights_forward(i)
    weights_last(0)

    @pl.when(jnp.logical_not(stays))
    def _():
        cot_remote.wait_recv()

    @pl.when(stays)
    def _():
        cot_local.wait()

    twin_cot = rcopy(g_ref, gp_ref, gp_s, gp_r, core_to)
    twin_cot.start()
    for a in range(3):
        weights_end(a)
    for i, (r, keep) in enumerate(moves):
        source = attn.at[:, pl.ds(i * group, group)]
        arrival = pltpu.make_async_copy(source, source, move_r.at[i])

        @pl.when(member != i)
        def _(r=r, arrival=arrival):
            r.wait_send()
            arrival.wait()

        @pl.when(member == i)
        def _(keep=keep):
            keep.wait()

    @pl.when(jnp.logical_not(stays))
    def _():
        cot_remote.wait_send()
        for c in tok_remote:
            c.wait_send()

    twin_cot.wait()
    for c in sends:
        c.wait_send()


def front(tok, cot, win, wo, we, wr, vec, starts, ns, nd, heads, d):
    n_rows, width = tok.shape
    n, group, chunks = n_rows * ns, width // 4, 4
    slots = 17 if nd == 8 else nd
    compact = lambda a: jax.ShapeDtypeStruct((a.shape[0] * (nd // 2), a.shape[1]), BF)
    any_, vmem = pl.BlockSpec(memory_space=pl.ANY), pl.BlockSpec(memory_space=pltpu.VMEM)
    full = lambda a: jax.ShapeDtypeStruct((a.shape[0] * nd, a.shape[1]), BF)
    dma = lambda *shape: pltpu.SemaphoreType.DMA(shape)
    sds = jax.ShapeDtypeStruct
    return pl.pallas_call(
        functools.partial(front_kernel, ns=ns, nd=nd, heads=heads, d=d, bq=n_rows, bk=n_rows, chunks=chunks),
        in_specs=[any_] * 7 + [vmem],
        out_specs=[vmem, any_, vmem, vmem, any_, any_, any_, vmem, vmem, vmem, vmem, vmem],
        out_shape=[
            sds(tok.shape, BF), sds((2 * n_rows, width), BF), sds((width, n), BF), sds((width, 3 * group), BF),
            full(wo), sds((width, we.shape[1] // 2 if len(we.shape) == 2 else we.shape[2]), BF), compact(wr), sds((nd, *vec.shape), BF), sds((n, 3 * group), BF),
            sds((n, group), BF), sds((heads // 2, 2, n), F32), sds(tok.shape, BF),
        ],
        scratch_shapes=[
            pltpu.VMEM((n, width), BF), pltpu.VMEM((group, n), BF), pltpu.VMEM((group, n), BF),
            dma(nd, 3), dma(nd, 3), dma(nd), dma(nd), dma(chunks), dma(chunks), dma(chunks),
            dma(chunks), dma(chunks), dma(chunks), dma(chunks), dma(chunks), dma(chunks),
            pltpu.SemaphoreType.DMA, pltpu.SemaphoreType.DMA, pltpu.SemaphoreType.DMA,
            pltpu.SemaphoreType.DMA, pltpu.SemaphoreType.DMA, dma(7), dma(3, slots), dma(3, slots), dma(4), dma(4), pltpu.SemaphoreType.DMA,
        ],
        compiler_params=pltpu.CompilerParams(
            collective_id=0, has_side_effects=True, vmem_limit_bytes=52 << 20
        ),
        cost_estimate=pl.CostEstimate(
            flops=8 * n * n * d * heads, bytes_accessed=60_000_000, transcendentals=n * n * heads
        ),
    )(tok, cot, win, wo, we, wr, vec, starts)


def middle_kernel(
    attn, wo, x, gl, weh, wrf, vec, ebias,
    out, gres, ga, fe, dwo, fq, vsum, esum,
    attb, wrh, resid, n2, tt, slope, act, zw, r1, r2, ws, e1, e2, gr, gs, xs_o, xr_o, xr_d, n_rc, f_rc,
    n2_s, n2_r, at_s, at_r, o_s, o_r, d_s, d_r, gr_s, gr_r, sw_s, sw_r, sw_l, a_s, a_r, e_s, e_r, z_s, z_r, w_s, w_r, w_l,
    *, nd,
):
    seq, me = lax.axis_index("seq"), lax.axis_index("dp")
    half, nearb, core = seq // 2, seq % 2, me % 2
    n_rows, width = x.shape
    both, block, ncol = 2 * n_rows, wrf.shape[0] // (nd // 2), nd // 2
    stays = half == core
    swap_to = (2 * core + nearb, me - core + half)
    core_to = (seq, me + 1 - 2 * core)
    column = me // 2
    x_to = (seq, me + 2 - 4 * (column % 2))
    y_to = (seq, me + 4 - 8 * (column // 2))

    def col(k):
        result = column
        if k & 1:
            result = result + 1 - 2 * (column % 2)
        if k & 2:
            result = result + 2 - 4 * (column // 2)
        return result

    def rcopy(src, dst, ss, rs, dev):
        return pltpu.make_async_remote_copy(
            src_ref=src, dst_ref=dst, send_sem=ss, recv_sem=rs, device_id=dev, device_id_type=MESH
        )

    def loop(total, size, body):
        def one(t, carry):
            body(pl.ds(pl.multiple_of(t * size, size), size))
            return carry

        lax.fori_loop(0, total // size, one, 0)

    barrier = pltpu.get_barrier_semaphore()

    def hello(dev):
        pl.semaphore_signal(barrier, inc=1, device_id=dev, device_id_type=MESH)

    near_to = (seq + 1 - 2 * nearb, me)
    far_to = (seq + 2 - 4 * half, me)
    for dev in (core_to, x_to, y_to, near_to, far_to):
        hello(dev)

    @pl.when(jnp.logical_not(stays))
    def _():
        hello(swap_to)
        pl.semaphore_wait(barrier, 6)

    @pl.when(stays)
    def _():
        pl.semaphore_wait(barrier, 5)

    sends = []

    def start(src, dst, ss, rs, dev):
        c = rcopy(src, dst, ss, rs, dev)
        c.start()
        sends.append(c)
        return c

    def owner(k, first, size):
        return pl.ds(pl.multiple_of(col(k) * block + first, block // 2), size)

    w_parts = []
    for i, (k, dev) in enumerate(((1, y_to), (2, x_to))):
        place = owner(k, i * (block // 2), block // 2)
        w_parts.append(start(wrf.at[place], wrh.at[place], w_s.at[i], w_r.at[i], dev))
    w_local = []
    for k in range(3):
        place = owner(k, 0, block)
        c = pltpu.make_async_copy(wrf.at[place], wrh.at[place], w_l.at[k])
        c.start()
        w_local.append(c)
    at_copy = start(attn, attb, at_s, at_r, core_to)

    step = n_rows // 2
    cuts = [slice(c * step, (c + 1) * step) for c in range(2)]
    theirs = [slice(n_rows + c * step, n_rows + (c + 1) * step) for c in range(2)]
    gain, shift = vec[0:1, :], vec[1:2, :]
    n2_copies = []
    for c in range(2):
        cut = pl.ds(c * step, step)
        value = x[cut, :].astype(F32) + _dot(attn[cut, :], wo[...], 1, 0) + vec[2:3, :]
        resid[cut, :] = value
        center = value - jnp.mean(value, axis=-1, keepdims=True)
        spread = jnp.mean(center * center, axis=-1, keepdims=True)
        n2[cut, :] = (center * lax.rsqrt(spread + EPS) * gain + shift).astype(BF)
        n2_copies.append(
            start(n2.at[cut], n2.at[pl.ds(n_rows + c * step, step)], n2_s.at[c], n2_r.at[c], core_to)
        )
    for c in range(4):
        cut = slice(c * step, (c + 1) * step)
        tt[:, cut] = jnp.transpose(gl[cut, :])
    for c in n2_copies:
        c.wait_recv()

    part_copies = {}

    def part_send(slot, src, dst, dev):
        c = rcopy(src, dst, a_s.at[slot], a_r.at[slot], dev)
        c.start()
        part_copies[slot] = c
        if slot not in (1, 3):
            sends.append(c)

    upper, lower = pl.ds(0, width // 2), pl.ds(width // 2, width // 2)
    root, cubic = 0.7978845608028654, 0.044715
    for k in (3, 1, 2, 0):
        f = col(k)
        units = pl.ds(pl.multiple_of(f * block, block), block)

        def expand(cut, f=f, units=units):
            u = _dot(n2[cut, :], weh[:, units], 1, 0) + ebias[:, units]
            t = jnp.tanh(root * (u + cubic * (u * u * u)))
            act[f, cut, :] = (0.5 * u * (1.0 + t)).astype(BF)
            rise = root * (1.0 + 3.0 * cubic * (u * u))
            slope[f, cut, :] = (0.5 * (1.0 + t) + 0.5 * u * (1.0 - t * t) * rise).astype(BF)

        loop(both, 512, expand)

        def reduce_grad(cut, f=f):
            zw[f, cut, :] = _dot(tt[cut, :], act[f], 1, 0).astype(BF)

        loop(width, 512, reduce_grad)
        if k == 3:
            part_send(1, zw.at[f, upper], r1.at[1], x_to)
            part_send(3, zw.at[f, lower], r1.at[3], y_to)
        elif k == 1:
            part_send(0, zw.at[f, upper], r1.at[0], x_to)
        elif k == 2:
            part_send(2, zw.at[f, lower], r1.at[2], y_to)

    for c in range(4):
        cut = slice(c * step, (c + 1) * step)
        tt[:, cut] = jnp.transpose(n2[cut, :])

    for c in w_local:
        c.wait()
    for c in w_parts:
        c.wait_recv()

    def reduced(cut):
        value = _dot(act[0, cut, :], wrh[:block, :], 1, 0)
        for f in range(1, ncol):
            value = value + _dot(act[f, cut, :], wrh[f * block : (f + 1) * block, :], 1, 0)
        return value

    o_copies = []
    for c in range(2):
        xs_o[cuts[c], :] = reduced(theirs[c]).astype(BF)
        cut = pl.ds(c * step, step)
        o_copies.append(rcopy(xs_o.at[cut], xr_o.at[cut], o_s.at[c], o_r.at[c], core_to))
        o_copies[c].start()
    swap_remote, swap_local = [], []
    for c in range(2):
        value = resid[cuts[c], :] + reduced(cuts[c]) + vec[3:4, :]
        o_copies[c].wait_recv()
        xr_o[cuts[c], :] = (value + xr_o[cuts[c], :].astype(F32)).astype(BF)
        cut = pl.ds(c * step, step)
        r = rcopy(xr_o.at[cut], out.at[cut], sw_s.at[c], sw_r.at[c], swap_to)
        stay = pltpu.make_async_copy(xr_o.at[cut], out.at[cut], sw_l.at[c])
        swap_remote.append(r)
        swap_local.append(stay)

        @pl.when(jnp.logical_not(stays))
        def _(r=r):
            r.start()

        @pl.when(stays)
        def _(stay=stay):
            stay.start()

    def forward(k, slot, first, index, dev):
        part_copies[slot].wait_recv()
        f = col(k)

        def add(cut):
            place = pl.ds(pl.multiple_of(cut.start + first, 128), 128)
            zw[f, place, :] = (zw[f, place, :].astype(F32) + r1[slot, cut, :].astype(F32)).astype(BF)

        loop(width // 2, 128, add)
        part_send(4 + index, zw.at[f, upper if first == 0 else lower], r2.at[index], dev)

    forward(2, 1, 0, 0, y_to)
    forward(1, 3, width // 2, 1, x_to)

    spare = col(3)
    q2, q4 = block // 2, block // 4

    def lanes(first, size):
        return pl.ds(pl.multiple_of(first, 128), size)

    z_copies = []

    def plane_total(start_row, cs):
        place = pl.ds(start_row, 128)

        def of(part):
            cut = pl.ds(pl.multiple_of(start_row - part * (width // 2), 128), 128)
            return r1[2 * part, cut, cs].astype(F32) + r2[part, cut, cs].astype(F32)

        return place, lambda part: zw[column, place, cs].astype(F32) + of(part)

    def plane_sum():
        for slot in (0, 2, 4, 5):
            part_copies[slot].wait_recv()
        part_copies[1].wait_send()
        part_copies[3].wait_send()
        for part in range(2):

            def add(cut, part=part):
                row = pl.multiple_of(cut.start + part * (width // 2), 128)
                place, total = plane_total(row, lanes((1 - nearb) * q2, q2))
                zw[spare, place, :q2] = total(part).astype(BF)

            loop(width // 2, 128, add)
        z_copies.append(start(zw.at[spare, :, pl.ds(0, q2)], n_rc, z_s.at[0], z_r.at[0], near_to))

    def near_sum():
        z_copies[0].wait_recv()
        for part in range(2):

            def add(cut, part=part):
                row = pl.multiple_of(cut.start + part * (width // 2), 128)
                place, total = plane_total(row, lanes(nearb * q2 + (1 - half) * q4, q4))
                value = total(part) + n_rc[place, lanes((1 - half) * q4, q4)].astype(F32)
                zw[spare, place, q2 : q2 + q4] = value.astype(BF)

            loop(width // 2, 128, add)
        z_copies.append(start(zw.at[spare, :, pl.ds(q2, q4)], f_rc, z_s.at[1], z_r.at[1], far_to))

    low = width // ncol // 2
    e_copies = {}

    def shard(k, part):
        return pl.ds(pl.multiple_of(col(k) * (2 * low) + part * low, low), low)

    def e_send(f, slot, src, dst, dev):
        e_copies[f, slot] = start(src, dst, e_s.at[f, slot], e_r.at[f, slot], dev)

    for f in range(ncol):
        units = slice(f * block, (f + 1) * block)
        esum[:, units] = jnp.zeros((1, block), F32)

        def expand_back(cut, f=f, units=units):
            da = _dot(gl[cut, :], wrh[units, :], 1, 1) * slope[f, cut, :].astype(F32)
            esum[:, units] += jnp.sum(da, axis=0, keepdims=True)
            act[f, cut, :] = da.astype(BF)

        loop(both, 512, expand_back)

        def expand_grad(cut, f=f):
            ws[f, cut, :] = _dot(tt[cut, :], act[f], 1, 0).astype(BF)

        loop(width, 512, expand_grad)
        e_send(f, 1, ws.at[f, shard(3, 0)], e1.at[f, 1], x_to)
        e_send(f, 3, ws.at[f, shard(3, 1)], e1.at[f, 3], y_to)
        e_send(f, 0, ws.at[f, shard(1, 0)], e1.at[f, 0], x_to)
        e_send(f, 2, ws.at[f, shard(2, 1)], e1.at[f, 2], y_to)

        if f == 1:
            plane_sum()
        elif f == 3:
            near_sum()

    def e_forward(f):
        for index, (k, dev) in enumerate(((2, y_to), (1, x_to))):
            e_copies[f, 1 + 2 * index].wait_recv()
            place = shard(k, index)
            ws[f, place, :] = (ws[f, place, :].astype(F32) + e1[f, 1 + 2 * index].astype(F32)).astype(BF)
            e_send(f, 4 + index, ws.at[f, place], e2.at[f, index], dev)

    def normed_grad(cut):
        value = None
        for f in range(ncol):
            one = _dot(act[f, cut, :], weh[:, f * block : (f + 1) * block], 1, 1)
            value = one if value is None else value + one
        return value

    d_copies = []
    for c in range(2):
        o_copies[c].wait_send()
        xs_o[cuts[c], :] = normed_grad(theirs[c]).astype(BF)
        cut = pl.ds(c * step, step)
        d_copies.append(start(xs_o.at[cut], xr_d.at[cut], d_s.at[c], d_r.at[c], core_to))
    e_forward(0)
    at_copy.wait_recv()
    for c in range(2):
        tt[:, cuts[c]] = jnp.transpose(attn[cuts[c], :])
        tt[:, theirs[c]] = jnp.transpose(attb[cuts[c], :])

    zero = jnp.zeros((1, width), F32)
    gain_sum, shift_sum, out_sum, red_sum = zero, zero, zero, zero
    gr_copies = []
    for c in range(2):
        dy = normed_grad(cuts[c])
        d_copies[c].wait_recv()
        dy = dy + xr_d[cuts[c], :].astype(F32)
        value = resid[cuts[c], :]
        center = value - jnp.mean(value, axis=-1, keepdims=True)
        rstd = lax.rsqrt(jnp.mean(center * center, axis=-1, keepdims=True) + EPS)
        hat = center * rstd
        gain_sum = gain_sum + jnp.sum(dy * hat, axis=0, keepdims=True)
        shift_sum = shift_sum + jnp.sum(dy, axis=0, keepdims=True)
        dh = dy * gain
        inner = dh - jnp.mean(dh, axis=-1, keepdims=True) - hat * jnp.mean(dh * hat, axis=-1, keepdims=True)
        base = gl[cuts[c], :].astype(F32)
        total = base + rstd * inner
        red_sum = red_sum + jnp.sum(base, axis=0, keepdims=True)
        out_sum = out_sum + jnp.sum(total, axis=0, keepdims=True)
        gres[cuts[c], :] = total
        low_rows = total.astype(BF)
        left, right = low_rows[:, : width // 2], low_rows[:, width // 2 :]
        gr[cuts[c], :] = jnp.where(core == 0, left, right)
        gs[cuts[c], :] = jnp.where(core == 0, right, left)
        cut = pl.ds(c * step, step)
        gr_copies.append(start(gs.at[cut], gr.at[pl.ds(n_rows + c * step, step)], gr_s.at[c], gr_r.at[c], core_to))
        ga[cuts[c], :] = _dot(low_rows, wo[...], 1, 1).astype(BF)
        e_forward(1 + c)
    vsum[0:1, :] = gain_sum
    vsum[1:2, :] = shift_sum
    vsum[2:3, :] = out_sum
    vsum[3:4, :] = red_sum
    vsum[4:8, :] = jnp.zeros((4, width), F32)
    for c in gr_copies:
        c.wait_recv()
    def output_grad(cut):
        dwo[cut, :] = _dot(tt[cut, :], gr[...], 1, 0).astype(BF)

    loop(width, 512, output_grad)
    e_forward(3)

    for f in range(ncol):
        for part in range(2):
            e_copies[f, 2 * part].wait_recv()
            e_copies[f, 4 + part].wait_recv()
            fe[part * low : (part + 1) * low, f * block : (f + 1) * block] = (
                ws[f, shard(0, part), :].astype(F32)
                + e1[f, 2 * part].astype(F32)
                + e2[f, part].astype(F32)
            )

    z_copies[1].wait_recv()

    for part in range(2):

        def quarter(cut, part=part):
            row = pl.multiple_of(cut.start + part * (width // 2), 128)
            place, total = plane_total(row, lanes(nearb * q2 + half * q4, q4))
            value = total(part) + n_rc[place, lanes(half * q4, q4)].astype(F32) + f_rc[place, :].astype(F32)
            fq[place, :] = value.astype(BF)

        loop(width // 2, 128, quarter)

    @pl.when(jnp.logical_not(stays))
    def _():
        for c in swap_remote:
            c.wait()

    @pl.when(stays)
    def _():
        for c in swap_local:
            c.wait()

    for c in sends:
        c.wait_send()


def middle(attn, wo, x, gl, weh, wrf, vec, ebias, nd):
    n_rows, width = x.shape
    own, ncol = weh.shape[1], nd // 2
    block = own // ncol
    any_, vmem = pl.BlockSpec(memory_space=pl.ANY), pl.BlockSpec(memory_space=pltpu.VMEM)
    dma = lambda *shape: pltpu.SemaphoreType.DMA(shape)
    one = pltpu.SemaphoreType.DMA
    sds = jax.ShapeDtypeStruct
    vm = lambda dtype, *shape: pltpu.VMEM(shape, dtype)
    both = 2 * n_rows
    return pl.pallas_call(
        functools.partial(middle_kernel, nd=nd),
        in_specs=[vmem] * 5 + [any_, vmem, vmem],
        out_specs=[any_, vmem, vmem, vmem, vmem, vmem, vmem, vmem],
        out_shape=[
            sds(x.shape, BF), sds(x.shape, F32), sds(x.shape, BF), sds((width // ncol, own), F32),
            sds((width, width // 2), BF), sds((width, block // 4), BF), sds((8, width), F32), sds((1, own), F32),
        ],
        scratch_shapes=[
            vm(BF, n_rows, width), vm(BF, own, width), vm(F32, n_rows, width), vm(BF, both, width),
            vm(BF, width, both), vm(BF, ncol, both, block), vm(BF, ncol, both, block),
            vm(BF, ncol, width, block), vm(BF, 4, width // 2, block), vm(BF, 2, width // 2, block),
            vm(BF, ncol, width, block), vm(BF, ncol, 4, width // ncol // 2, block),
            vm(BF, ncol, 2, width // ncol // 2, block), vm(BF, both, width // 2), vm(BF, n_rows, width // 2),
            vm(BF, n_rows, width), vm(BF, n_rows, width), vm(BF, n_rows, width),
            vm(BF, width, block // 2), vm(BF, width, block // 4),
            dma(2), dma(2), one, one, dma(2), dma(2), dma(2), dma(2), dma(2), dma(2), dma(2), dma(2), dma(2),
            dma(6), dma(6), dma(ncol, 6), dma(ncol, 6), dma(2), dma(2), dma(2), dma(2), dma(3),
        ],
        compiler_params=pltpu.CompilerParams(
            collective_id=2, has_side_effects=True, vmem_limit_bytes=63 << 20
        ),
        cost_estimate=pl.CostEstimate(
            flops=12 * both * width * own, bytes_accessed=40_000_000, transcendentals=2 * both * own
        ),
    )(attn, wo, x, gl, weh, wrf, vec, ebias)


def back_kernel(
    ga, qkv, att, lse, st, n1t, wf, x, gres, gain, v_in, res, dwr, dwe, dwo,
    out, tg, insum, osum, esum, rsum, vout,
    go, qt, dot, kt, dqt, delta, gm, zin, far_in, tot, tot2, near_in, core_in, cst, crc, nst, nrc, tgs,
    vmine, vrc, vz, own, fwd, r1, r2, ns_st, ns_rc, keep, fs_st, fs_rc, fb, eb, sum_two,
    move_s, move_r, move_l, a_s, a_r, a_l, d_s, d_r, out_s, out_r, out_l, tg_s, tg_r, tg_l, v_s, v_r, vz_s, vz_r, l_s, l_r,
    *, ns, nd, heads, d, bq, bk, chunks,
):
    seq, me = lax.axis_index("seq"), lax.axis_index("dp")
    half, nearb, core = seq // 2, seq % 2, me % 2
    member = 2 * core + nearb
    beside, twin, across = 2 * core + 1 - nearb, 2 * (1 - core) + nearb, 2 * (1 - core) + 1 - nearb
    n_rows, width = x.shape
    n, group, ncol = ns * n_rows, width // 4, nd // 2
    stays = half == core
    swap_to = (2 * core + nearb, me - core + half)
    near_to = (seq + 1 - 2 * nearb, me)
    far_to = (seq + 2 - 4 * half, me)
    third_to = (seq + 1 - 2 * nearb + 2 - 4 * half, me)
    core_to = (seq, me + 1 - 2 * core)

    def offset(k):
        result = me
        bit = 1
        while bit <= k:
            if k & bit:
                result = result + bit - 2 * bit * ((me // bit) % 2)
            bit *= 2
        return result

    def rcopy(src, dst, ss, rs, dev):
        return pltpu.make_async_remote_copy(
            src_ref=src, dst_ref=dst, send_sem=ss, recv_sem=rs, device_id=dev, device_id_type=MESH
        )

    def row_loop(total, size, body):
        size = 64 if total % 64 == 0 else size

        def one(t, carry):
            body(pl.multiple_of(t * size, size))
            return carry

        lax.fori_loop(0, total // size, one, 0)

    barrier = pltpu.get_barrier_semaphore()

    def hello(dev):
        pl.semaphore_signal(barrier, inc=1, device_id=dev, device_id_type=MESH)

    for k in range(1, nd):
        hello((seq, offset(k)))
    for dev in (near_to, far_to, third_to, (near_to[0], core_to[1])):
        hello(dev)

    @pl.when(jnp.logical_not(stays))
    def _():
        hello(swap_to)
        pl.semaphore_wait(barrier, nd + 4)

    @pl.when(stays)
    def _():
        pl.semaphore_wait(barrier, nd + 3)

    sends = []
    held = {}

    moves = []
    for i in range(4):
        src = ga.at[:, pl.ds(i * group, group)]
        mine = go.at[pl.ds(pl.multiple_of(member * n_rows, n_rows), n_rows)]
        dev = (seq - nearb + i % 2, me - core + i // 2)
        r = rcopy(src, mine, move_s.at[i], move_r.at[member], dev)
        stay = pltpu.make_async_copy(src, mine, move_l)
        moves.append((r, stay))

        @pl.when(member != i)
        def _(r=r):
            r.start()

        @pl.when(member == i)
        def _(stay=stay):
            stay.start()

    terms = (dwr, dwe, dwo, zin)
    pre = nd == 8
    high = [t.shape[0] // (1 if pre and a < 2 else ncol) for a, t in enumerate(terms)]
    wide = [t.shape[1] * (4 if pre and a == 0 else 1) for a, t in enumerate(terms)]

    def block(a, kc, part=None):
        row = (offset(2 * kc) // 2) * high[a]
        if part is None:
            return terms[a].at[pl.ds(pl.multiple_of(row, high[a]), high[a])]
        low = high[a] // 2
        return terms[a].at[pl.ds(pl.multiple_of(row + part * low, low), low)]

    def send(a, slot, src, dst, dev):
        c = rcopy(src, dst, a_s.at[a, slot], a_r.at[a, slot], dev)
        c.start()
        held[a, slot] = c
        sends.append(c)

    def rows_at_once(total):
        return 64 if total % 64 == 0 else 16

    def lanes(first, size):
        return pl.ds(pl.multiple_of(first, 128), size)

    def s0(a):
        local = [pltpu.make_async_copy(block(a, 0), own[a], a_l.at[a, 0])]
        if nd == 8:
            x_to, y_to = (seq, offset(2)), (seq, offset(4))
            send(a, 0, block(a, 1, 0), r1[a].at[0], x_to)
            send(a, 2, block(a, 2, 1), r1[a].at[2], y_to)
            send(a, 1, block(a, 3, 0), r1[a].at[1], x_to)
            send(a, 3, block(a, 3, 1), r1[a].at[3], y_to)
            local.append(pltpu.make_async_copy(block(a, 2, 0), fwd[a].at[0], a_l.at[a, 1]))
            local.append(pltpu.make_async_copy(block(a, 1, 1), fwd[a].at[1], a_l.at[a, 2]))
        else:
            for kc in range(1, ncol):
                send(a, kc, block(a, kc), r1[a].at[kc - 1], (seq, offset(2 * kc)))
        for c in local:
            c.start()
        held[a, "local"] = local

    def s1(a):
        for c in held[a, "local"]:
            c.wait()
        span = rows_at_once(high[a] // 2)
        if nd == 8:
            for part, k in ((0, 4), (1, 2)):
                held[a, 1 + 2 * part].wait_recv()

                def add(t, part=part):
                    cut = pl.ds(t, rows_at_once(span))
                    fwd[a][part, cut, :] = (
                        fwd[a][part, cut, :].astype(F32) + r1[a][1 + 2 * part, cut, :].astype(F32)
                    ).astype(BF)

                row_loop(high[a] // 2, 16, add)
                send(a, 4 + part, fwd[a].at[part], r2[a].at[part], (seq, offset(k)))

    def s2(a):
        c, low = wide[a], high[a] // 2
        if pre and a < 2:
            pass
        elif nd == 8:
            for slot in (0, 2, 4, 5):
                held[a, slot].wait_recv()
        else:
            for kc in range(1, ncol):
                held[a, kc].wait_recv()

        span = rows_at_once(low)

        def total(part, t, cs):
            cut = pl.ds(part * low + t, span)
            if pre and a == 1:
                return terms[a][cut, cs]
            value = own[a][cut, cs].astype(F32)
            if nd == 8:
                return (
                    value
                    + r1[a][2 * part, pl.ds(t, span), cs].astype(F32)
                    + r2[a][part, pl.ds(t, span), cs].astype(F32)
                )
            for kc in range(1, ncol):
                value = value + r1[a][kc - 1, cut, cs].astype(F32)
            return value

        for part in range(2):

            def add(t, part=part):
                cut = pl.ds(part * low + t, span)
                if a == 3:
                    tot[cut, :] = total(part, t, slice(None)).astype(BF)
                else:
                    keep[a][cut, :] = total(part, t, lanes(nearb * (c // 2), c // 2))
                    ns_st[a][cut, :] = total(part, t, lanes((1 - nearb) * (c // 2), c // 2)).astype(BF)

            row_loop(low, 16, add)
        if a == 3:
            send(a, 6, tot, far_in, far_to)
        else:
            send(a, 6, ns_st[a], ns_rc[a], near_to)

    def s3(a):
        c, span = wide[a], rows_at_once(high[a])
        held[a, 6].wait_recv()
        if a == 3:

            def add(t):
                cut = pl.ds(t, rows_at_once(span))
                tot2[cut, :] = (tot[cut, :].astype(F32) + far_in[cut, :].astype(F32)).astype(BF)

            row_loop(high[a], 16, add)
            send(a, 7, tot2, near_in, near_to)
            return

        def add(t):
            cut, cs = pl.ds(t, rows_at_once(high[a])), lanes((1 - half) * (c // 4), c // 4)
            fs_st[a][cut, :] = (keep[a][cut, cs] + ns_rc[a][cut, cs].astype(F32)).astype(BF)

        row_loop(high[a], 16, add)
        send(a, 7, fs_st[a], fs_rc[a], far_to)

    def s4(a):
        c = wide[a]
        if not (pre and a == 0):
            held[a, 7].wait_recv()
        low = high[a] // 2
        theirs = pl.ds(pl.multiple_of((1 - core) * low, low), low)
        if a == 3:
            send(a, 8, tot2.at[theirs], core_in.at[0], core_to)
            send(a, 9, near_in.at[theirs], core_in.at[1], core_to)
            return
        place = lanes(nearb * (c // 2) + half * (c // 4), c // 4)

        def add(t):
            cut, cs = pl.ds(t, rows_at_once(high[a])), lanes(half * (c // 4), c // 4)
            if pre and a == 0:
                fb[a][cut, place] = dwr[cut, :]
                return
            value = keep[a][cut, cs] + ns_rc[a][cut, cs].astype(F32) + fs_rc[a][cut, :].astype(F32)
            fb[a][cut, place] = value.astype(BF)

        row_loop(high[a], 16, add)
        send(a, 8, fb[a].at[:, place], fb[a].at[:, place], far_to)

    def s5(a):
        c = wide[a]
        held[a, 8].wait_recv()
        low = high[a] // 2
        ours = pl.ds(pl.multiple_of(core * low, low), low)
        if a == 3:
            held[a, 9].wait_recv()
            for which, value in (
                (member, tot2[ours, :]), (beside, near_in[ours, :]), (twin, core_in[0]), (across, core_in[1])
            ):
                for i in range(3):
                    insum[:, lanes(i * width + which * group, group)] = value[:, i * group : (i + 1) * group]
            return
        place = lanes(nearb * (c // 2), c // 2)
        send(a, 9, fb[a].at[:, place], fb[a].at[:, place], near_to)

    def s6(a):
        if pre and a > 0:
            l5(a)
        else:
            held[a, 9].wait_recv()
        low = high[a] // 2
        theirs = pl.ds(pl.multiple_of((1 - core) * low, low), low)
        if a == 0:
            if pre:
                return
            c = pltpu.make_async_copy(fb[a], rsum, a_l.at[a, 3])
            c.start()
            held[a, "last"] = c
        else:
            send(a, 10, fb[a].at[theirs], eb[a], core_to)

    def s7(a):
        if a == 0:
            if pre:
                rsum[...] = jnp.transpose(fb[a][...])
            else:
                held[a, "last"].wait()
            return
        held[a, 10].wait_recv()
        low = high[a] // 2
        ours = pl.ds(pl.multiple_of(core * low, low), low)
        if a == 2:
            size = wide[a]
            osum[:, lanes(core * size, size)] = fb[a][ours, :]
            osum[:, lanes((1 - core) * size, size)] = eb[a][...]
        else:
            size = wide[a] // ncol
            for i in range(ncol):
                cs = slice(i * size, (i + 1) * size)
                a0, a1 = fb[a][ours, cs], eb[a][:, cs]
                esum[:, 2 * i * size : (2 * i + 1) * size] = jnp.where(core == 0, a0, a1)
                esum[:, (2 * i + 1) * size : (2 * i + 2) * size] = jnp.where(core == 0, a1, a0)

    outer = nearb == half

    def line_copies(a, part):
        cs = slice(part * (wide[a] // 2), (part + 1) * (wide[a] // 2))
        make = lambda i, src, dst, dev: rcopy(
            src.at[:, cs], dst.at[:, cs], l_s.at[a - 1, 3 * part + i], l_r.at[a - 1, 3 * part + i], dev
        )
        return (
            make(0, ns_st[a], ns_rc[a], near_to),
            make(1, ns_st[a], fs_rc[a], third_to),
            make(2, fb[a], fb[a], near_to),
        )

    def l2(a):
        if a == 2:
            for slot in (0, 2, 4, 5):
                held[a, slot].wait_recv()
            low = high[a] // 2
            for part in range(2):
                cut = slice(part * low, (part + 1) * low)
                sum_two[cut, :] = (
                    own[a][cut, :].astype(F32) + r1[a][2 * part].astype(F32) + r2[a][part].astype(F32)
                )
        plane = terms[1] if a == 1 else sum_two

        @pl.when(outer)
        def _():
            for part in range(2):
                cs = slice(part * (wide[a] // 2), (part + 1) * (wide[a] // 2))

                def add(t, cs=cs):
                    cut = pl.ds(t, 64)
                    ns_st[a][cut, cs] = plane[cut, cs].astype(BF)

                row_loop(high[a], 64, add)
                line_copies(a, part)[0].start()

    def l3(a, part):
        plane = terms[1] if a == 1 else sum_two
        cs = slice(part * (wide[a] // 2), (part + 1) * (wide[a] // 2))

        @pl.when(jnp.logical_not(outer))
        def _():
            line_copies(a, part)[0].wait_recv()

            def add(t):
                cut = pl.ds(t, 64)
                ns_st[a][cut, cs] = (plane[cut, cs] + ns_rc[a][cut, cs].astype(F32)).astype(BF)

            row_loop(high[a], 64, add)
            line_copies(a, part)[1].start()

    def l4(a, part):
        cs = slice(part * (wide[a] // 2), (part + 1) * (wide[a] // 2))

        @pl.when(jnp.logical_not(outer))
        def _():
            line_copies(a, part)[1].wait_recv()

            def add(t):
                cut = pl.ds(t, 64)
                fb[a][cut, cs] = (ns_st[a][cut, cs].astype(F32) + fs_rc[a][cut, cs].astype(F32)).astype(BF)

            row_loop(high[a], 64, add)
            line_copies(a, part)[2].start()

    def l5(a):
        @pl.when(outer)
        def _():
            for part in range(2):
                line_copies(a, part)[2].wait_recv()

    def line_end(a):
        for part in range(2):
            copies = line_copies(a, part)

            @pl.when(outer)
            def _(copies=copies):
                copies[0].wait_send()

            @pl.when(jnp.logical_not(outer))
            def _(copies=copies):
                copies[1].wait_send()
                copies[2].wait_send()

    for a in (2,) if pre else (0, 1, 2):
        s0(a)
    if pre:
        s4(0)
    if not pre:
        out_remote = rcopy(res, out, out_s, out_r, swap_to)
        out_local = pltpu.make_async_copy(res, out, out_l)

        @pl.when(jnp.logical_not(stays))
        def _():
            out_remote.start()

        @pl.when(stays)
        def _():
            out_local.start()

    w, scale = 2 * d, d**-0.5
    for i in range(4):
        cut = slice(i * n_rows, (i + 1) * n_rows)
        qt[:, cut] = jnp.transpose(qkv[cut, :group])
        kt[:, cut] = jnp.transpose(qkv[cut, group : 2 * group])
    dqt[...] = jnp.zeros_like(dqt)
    for i in range(4):
        cut = slice(i * n_rows, (i + 1) * n_rows)
        landing = go.at[pl.ds(i * n_rows, n_rows)]
        arrival = pltpu.make_async_copy(landing, landing, move_r.at[i])
        r, stay = moves[i]

        @pl.when(member != i)
        def _(r=r, arrival=arrival):
            arrival.wait()
            r.wait_send()

        @pl.when(member == i)
        def _(stay=stay):
            stay.wait()

    if pre:
        l2(1)
    for i in range(4):
        cut = slice(i * n_rows, (i + 1) * n_rows)
        dot[:, cut] = jnp.transpose(go[cut, :])
        prod = jnp.transpose(go[cut, :].astype(F32) * att[cut, :].astype(F32))
        for h in range(heads):
            delta[h // 2, h % 2 : h % 2 + 1, cut] = jnp.sum(prod[h * d : (h + 1) * d], axis=0, keepdims=True)

    zero = jnp.zeros((), BF)
    for j in range(0, n, bk):

        def pair(p, carry, j=j):
            at = lambda first: pl.ds(pl.multiple_of(first + p * w, w), w)
            kb, vb = qkv[j : j + bk, at(group)], qkv[j : j + bk, at(2 * group)]
            dk = jnp.zeros((bk, w), F32)
            dv = jnp.zeros((bk, w), F32)
            row = lax.broadcasted_iota(jnp.int32, (w, bq), 0)
            lane = lax.broadcasted_iota(jnp.int32, (bq, w), 1)
            for i in range(j // bq, n // bq):
                cs = slice(i * bq, (i + 1) * bq)
                key = lax.broadcasted_iota(jnp.int32, (bk, bq), 0) + j
                ok = key >= st[:, cs]
                if j + bk > i * bq:
                    ok = ok & (key <= lax.broadcasted_iota(jnp.int32, (bk, bq), 1) + i * bq)
                for h in range(2):
                    rows_h = (row >= h * d) & (row < (h + 1) * d)
                    lanes_h = (lane >= h * d) & (lane < (h + 1) * d)
                    s = _dot(kb, jnp.where(rows_h, qt[at(0), cs], zero), 1, 0) * scale
                    s = jnp.where(ok, s, NEG)
                    e = jnp.exp(s - lse[p, h : h + 1, cs])
                    dp = _dot(vb, jnp.where(rows_h, dot[at(0), cs], zero), 1, 0)
                    ds = (e * (dp - delta[p, h : h + 1, cs])).astype(BF)
                    dv = dv + _dot(e.astype(BF), jnp.where(lanes_h, go[cs, at(0)], zero), 1, 0)
                    dk = dk + _dot(ds, jnp.where(lanes_h, qkv[cs, at(0)], zero), 1, 0)
                    head = pl.ds(pl.multiple_of(p * w + h * d, d), d)
                    dqt[head, cs] += _dot(kt[head, j : j + bk], ds, 1, 0)
            gm[j : j + bk, at(group)] = (dk * scale).astype(BF)
            gm[j : j + bk, at(2 * group)] = dv.astype(BF)
            return carry

        lax.fori_loop(0, heads // 2, pair, 0)
        if pre:
            if j == 0:
                l3(1, 0)
                s5(0)
                s1(2)
            elif j == bk:
                l3(1, 1)
                l4(1, 0)
                l2(2)
            elif j == 2 * bk:
                s6(0)
            else:
                l3(2, 0)
                l3(2, 1)
                l4(1, 1)
        elif j == 0:
            s1(0)
        elif j == bk:
            s2(0)
        elif j == 2 * bk:
            s3(0)
    for i in range(4):
        cut = slice(i * n_rows, (i + 1) * n_rows)
        gm[cut, :group] = (jnp.transpose(dqt[:, cut]) * scale).astype(BF)

    def input_grad():
        for i in range(4):
            cut = slice(i * group, (i + 1) * group)
            zin[cut, :] = _dot(n1t[cut, :], gm[...], 1, 0).astype(BF)
        s0(3)

    if pre:
        input_grad()

    step = n_rows // chunks

    def term(b, c):
        cut = pl.ds(pl.multiple_of(b * n_rows + c * step, step), step)
        return _dot(gm[cut, :], wf[...], 1, 1)

    quad = {}

    def quad_send(slot, src, dst, dev):
        c = rcopy(src, dst, d_s.at[slot], d_r.at[slot], dev)
        c.start()
        quad[slot] = c
        sends.append(c)

    for which, b in ((1, across), (0, twin)):
        for c in range(chunks):
            cut = pl.ds(c * step, step)
            cst[which, cut, :] = term(b, c).astype(BF)
            quad_send(which * chunks + c, cst.at[which, cut], crc.at[which, cut], core_to)
    for c in range(chunks):
        cut = pl.ds(c * step, step)
        value = term(beside, c)
        quad[chunks + c].wait_recv()
        nst[cut, :] = (value + crc[1, cut, :].astype(F32)).astype(BF)
        quad_send(2 * chunks + c, nst.at[cut], nrc.at[cut], near_to)

    if not pre:
        s1(1)
        s1(2)
        s4(0)
    if pre:
        l4(2, 0)
        l4(2, 1)
        s1(3)
        s2(3)
    else:
        input_grad()
        s5(0)

    tg_remote, tg_local = [], []
    gain_sum = jnp.zeros((1, width), F32)
    shift_sum = jnp.zeros((1, width), F32)
    for c in range(chunks):
        cut = pl.ds(c * step, step)
        value = term(member, c)
        quad[c].wait_recv()
        quad[2 * chunks + c].wait_recv()
        dy = value + crc[0, cut, :].astype(F32) + nrc[cut, :].astype(F32)
        rows_in = x[cut, :].astype(F32)
        center = rows_in - jnp.mean(rows_in, axis=-1, keepdims=True)
        rstd = lax.rsqrt(jnp.mean(center * center, axis=-1, keepdims=True) + EPS)
        hat = center * rstd
        gain_sum = gain_sum + jnp.sum(dy * hat, axis=0, keepdims=True)
        shift_sum = shift_sum + jnp.sum(dy, axis=0, keepdims=True)
        dh = dy * gain[...]
        inner = dh - jnp.mean(dh, axis=-1, keepdims=True) - hat * jnp.mean(dh * hat, axis=-1, keepdims=True)
        tgs[cut, :] = (gres[cut, :] + rstd * inner).astype(BF)
        r = rcopy(tgs.at[cut], tg.at[cut], tg_s.at[c], tg_r.at[c], swap_to)
        stay = pltpu.make_async_copy(tgs.at[cut], tg.at[cut], tg_l.at[c])
        tg_remote.append(r)
        tg_local.append(stay)

        @pl.when(jnp.logical_not(stays))
        def _(r=r):
            r.start()

        @pl.when(stays)
        def _(stay=stay):
            stay.start()

    if pre:
        s3(3)

    small = v_in.shape[2]
    for k in range(nd):
        vmine[k] = v_in[k]
        vmine[k, 0:1, :] = gain_sum[:, k * small : (k + 1) * small]
        vmine[k, 1:2, :] = shift_sum[:, k * small : (k + 1) * small]
    vec = []
    for k in range(1, nd):
        c = rcopy(vmine.at[offset(k)], vrc.at[k], v_s.at[k], v_r.at[k], (seq, offset(k)))
        c.start()
        vec.append(c)
        sends.append(c)

    if not pre:
        s2(1)
        s2(2)
        s6(0)
        s1(3)
    total = vmine[me]
    for k, c in enumerate(vec):
        c.wait_recv()
        total = total + vrc[k + 1]
    vz[seq] = total
    z_copies = []
    for i, dev in enumerate((near_to, far_to, third_to)):
        c = rcopy(vz.at[seq], vz.at[seq], vz_s.at[i], vz_r.at[i], dev)
        c.start()
        z_copies.append(c)
        sends.append(c)
    if not pre:
        s3(1)
        s3(2)
        s2(3)
        s4(1)
        s4(2)
        s3(3)
        s5(1)
        s5(2)
    s6(1)
    s6(2)
    s4(3)
    if pre:
        s7(0)
    s5(3)
    for c in z_copies:
        c.wait_recv()
    total = vz[0]
    for i in range(1, ns):
        total = total + vz[i]
    vout[...] = total
    for a in (1, 2) if pre else (0, 1, 2):
        s7(a)

    @pl.when(jnp.logical_not(stays))
    def _():
        if not pre:
            out_remote.wait()
        for c in tg_remote:
            c.wait()

    @pl.when(stays)
    def _():
        if not pre:
            out_local.wait()
        for c in tg_local:
            c.wait()

    for c in sends:
        c.wait_send()
    if pre:
        line_end(1)
        line_end(2)


def back(ga, qkv, att, lse, starts, n1t, wf, x, gres, gain, v_in, res, dwr, dwe, dwo, ns, nd, heads, d):
    n_rows, width = x.shape
    n, group, ncol, chunks = n_rows * ns, width // 4, nd // 2, 4
    any_, vmem = pl.BlockSpec(memory_space=pl.ANY), pl.BlockSpec(memory_space=pltpu.VMEM)
    dma = lambda *shape: pltpu.SemaphoreType.DMA(shape)
    one = pltpu.SemaphoreType.DMA
    sds = jax.ShapeDtypeStruct
    pre = nd == 8
    sizes = [(t.shape[0] // ncol, t.shape[1]) for t in (dwr, dwe, dwo)] + [(width // ncol, 3 * group)]
    plane = list(sizes)
    if pre:
        sizes[0], plane[0] = (width, 4 * dwr.shape[1]), (32, 128)
        sizes[1], plane[1] = dwe.shape, (32, 128)
    vm = lambda dtype, *shape: pltpu.VMEM(shape, dtype)

    def line(shift):
        if pre:
            return [(16, 128), *sizes[1:3]]
        return [(r, c >> shift) for r, c in sizes[:3]]

    slots = max(11, nd)
    rr, cc = width // nd, 3 * group
    return pl.pallas_call(
        functools.partial(back_kernel, ns=ns, nd=nd, heads=heads, d=d, bq=n_rows // 2, bk=n_rows, chunks=chunks),
        in_specs=[vmem] * 11 + [any_] + [vmem if pre else any_] * 2 + [any_],
        out_specs=[any_, any_, vmem, vmem, vmem, vmem if pre else any_, vmem],
        out_shape=[
            sds(res.shape, BF), sds(x.shape, BF), sds((rr, 3 * width), BF), sds((rr, width), BF),
            sds((rr, 2 * dwe.shape[1]), BF), sds(sizes[0][::-1] if pre else sizes[0], BF), sds(v_in.shape[1:], F32),
        ],
        scratch_shapes=[
            vm(BF, n, group), vm(BF, group, n), vm(BF, group, n), vm(BF, group, n), vm(F32, group, n),
            vm(F32, heads // 2, 2, n), vm(BF, n, 3 * group), vm(BF, width, 3 * group),
            vm(BF, 2 * rr, cc), vm(BF, 2 * rr, cc), vm(BF, 2 * rr, cc), vm(BF, 2 * rr, cc), vm(BF, 2, rr, cc),
            vm(BF, 2, n_rows, width), vm(BF, 2, n_rows, width), vm(BF, n_rows, width), vm(BF, n_rows, width),
            vm(BF, n_rows, width), vm(F32, *v_in.shape), vm(F32, *v_in.shape), vm(F32, ns, *v_in.shape[1:]),
            [vm(BF, r, c) for r, c in plane],
            [vm(BF, 2, r // 2, c) for r, c in plane],
            [vm(BF, 4, r // 2, c) if nd == 8 else vm(BF, ncol - 1, r, c) for r, c in plane],
            [vm(BF, 2, r // 2, c) for r, c in plane],
            [vm(BF, r, c) for r, c in line(1)], [vm(BF, r, c) for r, c in line(1)],
            [vm(F32, r, c // 2) if not pre else vm(F32, 8, 128) for r, c in sizes[:3]],
            [vm(BF, r, c // 4) if not pre else vm(BF, 16, 128) for r, c in sizes[:3]],
            [vm(BF, r, c) for r, c in line(2)],
            [vm(BF, r, c) for r, c in sizes[:3]], [vm(BF, r // 2, c) for r, c in sizes[:3]],
            vm(F32, *sizes[2]) if pre else vm(F32, 8, 128),
            dma(4), dma(4), one, dma(4, slots), dma(4, slots), dma(4, 4),
            dma(3 * chunks), dma(3 * chunks), one, one, one, dma(chunks), dma(chunks), dma(chunks),
            dma(nd), dma(nd), dma(3), dma(3), dma(2, 6), dma(2, 6),
        ],
        compiler_params=pltpu.CompilerParams(
            collective_id=1, has_side_effects=True, vmem_limit_bytes=60 << 20
        ),
        cost_estimate=pl.CostEstimate(
            flops=20 * n * n * d * heads, bytes_accessed=60_000_000, transcendentals=n * n * heads
        ),
    )(ga, qkv, att, lse, starts, n1t, wf, x, gres, gain, v_in, res, dwr, dwe, dwo)


def layer_normalize(values, gain, shift):
    center = values - jnp.mean(values, axis=-1, keepdims=True)
    spread = jnp.mean(center * center, axis=-1, keepdims=True)
    return center * lax.rsqrt(spread + EPS) * gain + shift


def smooth_gate(values):
    return jax.nn.gelu(values, approximate=True)


def rows(array, start, size):
    return lax.dynamic_slice_in_dim(array, start, size, 0)


def cols(array, start, size):
    return lax.dynamic_slice_in_dim(array, start, size, 1)


def put(array, piece, row, col):
    return lax.dynamic_update_slice(array, piece, (row, col))


def bf_round(x):
    return lax.reduce_precision(x, 8, 7)


class Links:
    def __init__(self, ns, nd):
        self.ns, self.nd = ns, nd

    def go(self, array, target):
        pairs = []
        for s in range(self.ns):
            for d in range(self.nd):
                ts, td = target(s, d)
                pairs.append((s * self.nd + d, ts * self.nd + td))
        return lax.ppermute(array, ("seq", "dp"), pairs)

    def dp(self, array, k):
        return self.go(array, lambda s, d: (s, d ^ k))

    def core(self, array):
        return self.dp(array, 1)

    def near(self, array):
        return self.go(array, lambda s, d: (s ^ 1, d))

    def far(self, array):
        return self.go(array, lambda s, d: (s ^ 2, d))

    def both(self, array):
        return self.go(array, lambda s, d: (s ^ 1, d ^ 1))

    def swap(self, array):
        return self.go(array, lambda s, d: (2 * (d % 2) + s % 2, d - d % 2 + s // 2))


def on_device(
    tokens, lengths, cotangent, mixer_input, mixer_output, expand_weight, reduce_weight,
    first_gain, first_shift, second_gain, second_shift, output_bias, expand_bias, reduce_bias,
):
    ns, nd = lax.axis_size("seq"), lax.axis_size("dp")
    links = Links(ns, nd)
    seq, me = lax.axis_index("seq"), lax.axis_index("dp")
    half, near_bit, core = seq // 2, seq % 2, me % 2
    column = me // 2
    member = 2 * core + near_bit
    n_rows, width = tokens.shape[1:]
    slots = n_rows * ns
    head_dim = width // HEADS
    hidden = reduce_weight.shape[0] * nd
    group = width // 4
    my_heads = HEADS // 4

    lengths_row = jnp.where(half == core, lengths[0], links.core(lengths)[0])
    entry = jnp.arange(lengths_row.shape[0])
    ends = jnp.sum(jnp.where(entry[None, :] <= entry[:, None], lengths_row[None, :], 0), axis=1)
    place = jnp.arange(slots, dtype=jnp.int32)
    passed = place[:, None] >= ends[None, :]
    starts = jnp.max(jnp.where(passed, ends[None, :], 0), axis=1)
    starts = jnp.where(place < ends[-1], starts, place).reshape(1, slots)
    live = (member * n_rows + jnp.arange(n_rows, dtype=jnp.int32) < ends[-1]).astype(F32)

    small, small_rows = width // nd, mixer_input.shape[0]
    wide = hidden // nd
    vectors = [first_gain, first_shift, second_gain, second_shift, output_bias, reduce_bias]
    vectors = [v[None] for v in vectors] + [expand_bias.reshape(-1, small)]
    vectors = jnp.concatenate([*vectors, jnp.zeros((16 - 6 - wide // small, small), BF)])
    by_core = expand_weight
    if wide % 128:
        by_core = expand_weight.reshape(small_rows, nd // 2, 2, wide).transpose(2, 0, 1, 3)
        by_core = by_core.reshape(2, small_rows, hidden // 2)
    (
        x_low, both_grad, normed_t, input_full, output_full, expand_half, reduce_half, vectors,
        qkv, attended, logsum, attention,
    ) = front(
        tokens[0], cotangent[0], mixer_input, mixer_output, by_core, reduce_weight, vectors,
        starts, ns, nd, my_heads, head_dim,
    )
    vectors = vectors.astype(F32)
    gain_one, _, gain_two, shift_two, output_add, reduce_add = (vectors[:, i].reshape(-1) for i in range(6))
    n_wide = wide // small
    expand_add = vectors[:, 6 : 6 + n_wide].reshape(nd // 2, 2, wide)
    expand_add = lax.dynamic_index_in_dim(expand_add, core, 1, keepdims=False).reshape(-1)

    twin_live = ((member ^ 2) * n_rows + jnp.arange(n_rows, dtype=jnp.int32) < ends[-1]).astype(F32)
    if nd == 8:
        vec = jnp.stack([gain_two, shift_two, output_add, reduce_add])
        vec = jnp.concatenate([vec, jnp.zeros_like(vec)])
        row = lax.broadcasted_iota(jnp.int32, both_grad.shape, 0)
        at = jnp.where(row < n_rows, member * n_rows + row, (member ^ 2) * n_rows + row - n_rows)
        both_grad = jnp.where(at < ends[-1], both_grad, jnp.zeros((), BF))
        result, grad_resid, grad_attention, expand_term, output_term, reduce_term, row_sums, wide_sums = middle(
            attention, output_full, x_low, both_grad, expand_half, reduce_half, vec, expand_add[None], nd,
        )
        gain_two_sum, shift_two_sum, output_bias_sum, reduce_bias_sum = (row_sums[i] for i in range(4))
        expand_bias_sum = wide_sums[0]
        layer_output, result = result, jnp.zeros((16, 128), BF)
    else:
        grad_low, twin_grad = both_grad[:n_rows], both_grad[n_rows:]
        twin_attention = links.core(attention)
        inputs = x_low.astype(F32)
        resid = inputs + mm(attention, output_full) + output_add
        normed_two = layer_normalize(resid, gain_two, shift_two).astype(BF)
        normed_two = jnp.concatenate([normed_two, links.core(normed_two)])
        expanded = mm(normed_two, expand_half) + expand_add
        active = smooth_gate(expanded).astype(BF)
        reduced = mm(active, reduce_half)
        twin_part = links.core(reduced[n_rows:].astype(BF)).astype(F32)
        result = (resid + reduced[:n_rows] + twin_part + reduce_add).astype(BF)
        grad_result = grad_low.astype(F32) * live[:, None]
        result_low = jnp.concatenate([grad_result.astype(BF), (twin_grad.astype(F32) * twin_live[:, None]).astype(BF)])
        reduce_term = mm_left(active, result_low).astype(BF)
        reduce_bias_sum = jnp.sum(grad_result, axis=0)
        grad_active = mm_right(result_low, reduce_half)
        _, gate_back = jax.vjp(smooth_gate, expanded)
        grad_expanded = gate_back(grad_active)[0]
        expand_bias_sum = jnp.sum(grad_expanded, axis=0)
        expanded_low = grad_expanded.astype(BF)
        expand_term = mm_left(normed_two, expanded_low).astype(BF)
        grad_normed = mm_right(expanded_low, expand_half)
        grad_normed_two = grad_normed[:n_rows] + links.core(grad_normed[n_rows:].astype(BF)).astype(F32)
        _, second_back = jax.vjp(layer_normalize, resid, gain_two, shift_two)
        resid_part, gain_two_sum, shift_two_sum = second_back(grad_normed_two)
        grad_resid = grad_result + resid_part
        output_bias_sum = jnp.sum(grad_resid, axis=0)
        resid_low = grad_resid.astype(BF)
        grad_attention = mm_right(resid_low, output_full).astype(BF)
        both_low = jnp.concatenate([resid_low, links.core(resid_low)])
        both_low = cols(both_low, core * (width // 2), width // 2)
        output_term = mm_left(jnp.concatenate([attention, twin_attention]), both_low).astype(BF)

    sums = jnp.stack([gain_two_sum, shift_two_sum, output_bias_sum, reduce_bias_sum])
    sums = sums.reshape(4, nd, small).transpose(1, 0, 2)
    wide_sum = expand_bias_sum.reshape(nd // 2, 1, n_wide, small)
    parity = jnp.arange(2).reshape(1, 2, 1, 1)
    wide_sum = jnp.where(parity == core, wide_sum, 0.0).reshape(nd, n_wide, small)
    pad = -(6 + n_wide) % 8
    sums = jnp.concatenate([jnp.zeros((nd, 2, small)), sums, wide_sum, jnp.zeros((nd, pad, small))], axis=1)

    swapped, tokens_gradient, input_sum, output_sum, expand_sum, reduce_sum, sums = back(
        grad_attention, qkv, attended, logsum, starts, normed_t, input_full, x_low, grad_resid,
        gain_one.reshape(1, width), sums, result, reduce_term, expand_term, output_term,
        ns, nd, my_heads, head_dim,
    )
    if nd != 8:
        layer_output = swapped
    return (
        layer_output[None],
        tokens_gradient.astype(F32)[None],
        input_sum.astype(F32),
        output_sum.astype(F32),
        expand_sum.astype(F32),
        reduce_sum.astype(F32),
        sums[0],
        sums[1],
        sums[2],
        sums[3],
        sums[4],
        sums[6 : 6 + n_wide].reshape(-1),
        sums[5],
    )


def solution(mesh):
    row, vec = P("dp", None), P("dp")
    act = P("dp", "seq", None)
    return jax.shard_map(
        on_device,
        mesh=mesh,
        in_specs=(act, row, act, row, row, row, row, vec, vec, vec, vec, vec, vec, vec),
        out_specs=(act, act, row, row, row, row, vec, vec, vec, vec, vec, vec, vec),
        check_vma=False,
    )
```
